32 devices in a mesh: fsdp: 4 (over y, x), seq: 8 (over z, core).
Axes of the slice: x: 2, y: 2, z: 4, core: 2. Of those that a mesh axis runs over, the one named last changes fastest.
Arguments:
- tokens: bfloat16 [4, 3072, 2048], P('fsdp', 'seq'), may hold values from -40 to 40
- starts: int32 [4, 3], P('fsdp'), may hold values from 0 to 3072, as said below
- w_query: bfloat16 [2048, 2048], P(('fsdp', 'seq')), may hold values from -0.1875 to 0.1875
- w_key: bfloat16 [2048, 256], P(('fsdp', 'seq')), may hold values from -0.1875 to 0.1875
- w_value: bfloat16 [2048, 256], P(('fsdp', 'seq')), may hold values from -0.125 to 0.125
- w_out: bfloat16 [2048, 2048], P(None, ('fsdp', 'seq')), may hold values from -1 to 1
- w_gate: bfloat16 [2048, 5632], P(('fsdp', 'seq')), may hold values from -0.125 to 0.125
- w_up: bfloat16 [2048, 5632], P(('fsdp', 'seq')), may hold values from -0.125 to 0.125
- w_down: bfloat16 [5632, 2048], P(None, ('fsdp', 'seq')), may hold values from -0.078125 to 0.078125
- norm_attn: bfloat16 [2048], P(('fsdp', 'seq')), may hold values from 0.5 to 1.5
- norm_mlp: bfloat16 [2048], P(('fsdp', 'seq')), may hold values from 0.5 to 1.5
- cotangent: bfloat16 [4, 3072, 2048], P('fsdp', 'seq'), may hold values from -6 to 6
Outputs:
- out: bfloat16 [4, 3072, 2048], P('fsdp', 'seq')
- grad_tokens: bfloat16 [4, 3072, 2048], P('fsdp', 'seq')
- grad_query: float32 [2048, 2048], P(('fsdp', 'seq'))
- grad_key: float32 [2048, 256], P(('fsdp', 'seq'))
- grad_value: float32 [2048, 256], P(('fsdp', 'seq'))
- grad_out: float32 [2048, 2048], P(None, ('fsdp', 'seq'))
- grad_gate: float32 [2048, 5632], P(('fsdp', 'seq'))
- grad_up: float32 [2048, 5632], P(('fsdp', 'seq'))
- grad_down: float32 [5632, 2048], P(None, ('fsdp', 'seq'))
- grad_norm_attn: float32 [2048], P(('fsdp', 'seq'))
- grad_norm_mlp: float32 [2048], P(('fsdp', 'seq'))
The draws below stay inside these ranges and needn't reach their ends.
Inputs may be any that keep to these rules, and one draw needn't show every extreme that they name: `starts`: each row lists the first positions of its sequence's documents in rising order, beginning with 0; unused slots hold 3072. Every document has 1024 to 2048 tokens, and each sequence has one of exactly 2048 tokens.
All inputs are finite; a program needn't handle non-finite values.
Results may differ from the reference program's by a relative error of at most 0.02.
Values may be sent and summed in bfloat16 or wider, within the bound.
A program may use at most 448 MiB of HBM per device.

```python
import jax
import jax.numpy as jnp
from jax import lax

D = 2048
HEADS = 32
KV = 4
HD = 64
FF = 5632
BLOCK = 512
MAXDOC = 4096
MINDOC = 1024
SEQS = 4
SEQLEN = 3072
LONGEST = 2048
SLOTS = 3
N_SEQ = 8


def draw_tokens(key, part):
    key_noise, key_rows, key_columns = jax.random.split(key, 3)
    row_scale = 10.0 ** jax.random.uniform(key_rows, (SEQS, SEQLEN, 1), jnp.float32)
    column_scale = 10.0 ** jax.random.uniform(key_columns, (1, 1, D), jnp.float32)
    noise_part = jnp.clip(jax.random.normal(key_noise, (SEQS, SEQLEN, D), jnp.float32), -6.0, 6.0)
    return (noise_part * row_scale * column_scale / 15.0).astype(jnp.bfloat16)


def draw_starts(key, part):
    longest = LONGEST
    seq_rows = []
    for member in range(SEQS):
        member_key = jax.random.fold_in(jax.random.fold_in(key, 7919), member)
        key_lengths, key_insert = jax.random.split(member_key)
        uniform_draws = jax.random.randint(key_lengths, (SLOTS,), 0, 1 << 20, dtype=jnp.int32)
        remaining = jnp.int32(SEQLEN - longest)
        pieces = []
        for slot_index in range(SLOTS - 1):
            ceiling = jnp.minimum(longest, remaining - MINDOC)
            span = jnp.maximum(ceiling - MINDOC + 1, 1)
            cut = MINDOC + uniform_draws[slot_index] % span
            taken = jnp.where(remaining >= 2 * MINDOC, cut, remaining)
            pieces.append(taken)
            remaining = remaining - taken
        pieces.append(jnp.int32(0))
        filled = jnp.stack(pieces)
        used_count = jnp.sum((filled > 0).astype(jnp.int32))
        insert_at = jax.random.randint(key_insert, (), 0, 1 << 20, dtype=jnp.int32) % (used_count + 1)
        slots_at = jnp.arange(SLOTS, dtype=jnp.int32)
        shifted = jnp.concatenate([jnp.zeros((1,), jnp.int32), filled[:-1]])
        lengths = jnp.where(slots_at < insert_at, filled, jnp.where(slots_at == insert_at, longest, shifted))
        doc_ends = jnp.cumsum(lengths)
        seq_rows.append(jnp.where(lengths > 0, doc_ends - lengths, SEQLEN))
    return jnp.stack(seq_rows).astype(jnp.int32)


def with_spikes(drawn, key, source, target, blocks, factor):
    owner, partner = [(jnp.arange(drawn.shape[axis_at]) // (drawn.shape[axis_at] // blocks)).reshape([-1 if axis == axis_at else 1 for axis in range(drawn.ndim)]) for axis_at in (source, target)]
    chosen = jax.random.permutation(key, blocks)[partner]
    strong = (owner == chosen) | (owner == (partner + blocks // 2) % blocks)
    return jnp.where(strong, factor * drawn, drawn)


def shard_levels(rng, shape, cuts, low, high):
    level = 1.0
    for position, shards_of in cuts:
        draws = jax.random.uniform(jax.random.fold_in(jax.random.fold_in(rng, 6), position), (shards_of,), jnp.float32, low / len(cuts), high / len(cuts))
        level = level * jnp.repeat(jnp.exp(draws), shape[position] // shards_of).reshape((-1,) + (1,) * (len(shape) - 1 - position))
    return level


def centred(stream_key, dims, scale, most, cuts=(), kind=jnp.bfloat16):
    entries = scale * jax.random.normal(stream_key, dims, jnp.float32)
    if cuts:
        entries = entries * shard_levels(stream_key, dims, cuts, -0.22, 0.18)
    return jnp.clip(entries, -most, most).astype(kind)


def heavy_noise(rng, dims, deviation, limit, shards, heavy, held_as=jnp.bfloat16):
    array = deviation * jax.random.normal(rng, dims, jnp.float32)
    if shards:
        array = array * shard_levels(rng, dims, shards, -0.22, 0.18)
    return jnp.clip(with_spikes(array, jax.random.fold_in(rng, 3), *heavy), -limit, limit).astype(held_as)


def setup_inputs(seed: int = 0) -> dict:
    keys = jax.random.split(jax.random.key(seed), 13)
    return {
        "tokens": draw_tokens(jax.random.fold_in(keys[12], 71), 0),
        "starts": draw_starts(jax.random.fold_in(keys[12], 71), 0),
        "w_query": centred(keys[2], (D, HEADS * HD), (D // 2) ** -0.5, 0.1875, ((0, 32),)),
        "w_key": centred(keys[3], (D, KV * HD), (D // 2) ** -0.5, 0.1875, ((0, 32),)),
        "w_value": centred(keys[4], (D, KV * HD), D ** -0.5, 0.125, ((0, 32),)),
        "w_out": centred(keys[5], (HEADS * HD, D), (HEADS * HD // 64) ** -0.5, 1.0, ((1, 32),)),
        "w_gate": centred(keys[6], (D, FF), D ** -0.5, 0.125, ((0, 32),)),
        "w_up": centred(keys[7], (D, FF), D ** -0.5, 0.125, ((0, 32),)),
        "w_down": centred(keys[8], (FF, D), FF ** -0.5, 0.078125, ((1, 32),)),
        "norm_attn": jnp.clip(1.0 + 0.1 * jax.random.normal(keys[9], (D,), jnp.float32), 0.5, 1.5).astype(jnp.bfloat16),
        "norm_mlp": jnp.clip(1.0 + 0.1 * jax.random.normal(keys[10], (D,), jnp.float32), 0.5, 1.5).astype(jnp.bfloat16),
        "cotangent": heavy_noise(keys[11], (SEQS, SEQLEN, D), 1.0, 6.0, ((0, 4), (1, 8)), (1, 2, 8, 2.0)),
    }


@jax.custom_vjp
def low(v):
    return lax.optimization_barrier(v.astype(jnp.bfloat16)).astype(jnp.float32)

@jax.custom_vjp
def low_back(v):
    return v

def low_keep(v):
    return (low(v), None)

def low_pass(kept, grad):
    return (grad,)

def back_keep(v):
    return (v, None)

def back_low(kept, grad):
    return (low(grad),)
low.defvjp(low_keep, low_pass)
low_back.defvjp(back_keep, back_low)
EPSILON = 1e-05
ROPE_BASE = 10000.0
MASKED = -1e+30

def product(left, right):
    return jnp.dot(left, right, precision=lax.Precision.HIGHEST, preferred_element_type=jnp.float32)

def norm_apply(values, gain):
    scale_rows = lax.rsqrt(lax.optimization_barrier(jnp.mean(values * values, axis=-1, keepdims=True)) + EPSILON)
    return values * scale_rows * gain

def rotary_tables(positions):
    half_dim = HD // 2
    frequency = ROPE_BASE ** (-(jnp.arange(half_dim, dtype=jnp.float32) / half_dim))
    angles = positions[:, None] * frequency[None, :]
    return (jnp.cos(angles)[:, None, :], jnp.sin(angles)[:, None, :])

def rotate(values, cos_table, sine_table):
    half_dim = HD // 2
    front_half = values[..., :half_dim]
    back_half = values[..., half_dim:]
    return jnp.concatenate([front_half * cos_table - back_half * sine_table, back_half * cos_table + front_half * sine_table], axis=-1)

def attention(query, key_heads, value_heads, firsts):
    length = query.shape[0]
    window = MAXDOC + BLOCK
    score_scale = HD ** (-0.5)
    key_padded = jnp.pad(key_heads, ((MAXDOC, 0), (0, 0), (0, 0)))
    value_padded = jnp.pad(value_heads, ((MAXDOC, 0), (0, 0), (0, 0)))

    def one_block(block_index):
        query_start = block_index * BLOCK
        query_part = lax.dynamic_slice_in_dim(query, query_start, BLOCK, 0)
        key_part = lax.dynamic_slice_in_dim(key_padded, query_start, window, 0)
        value_part = lax.dynamic_slice_in_dim(value_padded, query_start, window, 0)
        query_at = query_start + jnp.arange(BLOCK, dtype=jnp.int32)
        key_at = query_start - MAXDOC + jnp.arange(window, dtype=jnp.int32)
        first_rows = lax.dynamic_slice_in_dim(firsts, query_start, BLOCK, 0)
        scores = low_back(jnp.einsum('qhd,khd->hqk', query_part, key_part, precision=lax.Precision.HIGHEST) * score_scale)
        allowed = (key_at[None, :] <= query_at[:, None]) & (key_at[None, :] >= first_rows[:, None])
        scores = jnp.where(allowed[None], scores, MASKED)
        weights = low(jax.nn.softmax(scores, axis=-1))
        return jnp.einsum('hqk,khd->qhd', weights, value_part, precision=lax.Precision.HIGHEST)
    blocks = lax.map(jax.checkpoint(one_block), jnp.arange(length // BLOCK, dtype=jnp.int32))
    return blocks.reshape(length, query.shape[1], query.shape[2])

def block_layer(inputs, weights, firsts, cos_table, sine_table):
    w_query, w_key, w_value, w_out, w_gate, w_up, w_down, norm_attn, norm_mlp = weights
    length = inputs.shape[0]
    repeats = N_SEQ // KV
    per_slot = HEADS // N_SEQ
    normed = low(norm_apply(inputs, norm_attn))
    query_pre = low_back(product(normed, w_query)).reshape(length, HEADS, HD)
    key_pre = low_back(product(normed, w_key)).reshape(length, KV, HD)
    value_pre = low_back(product(normed, w_value)).reshape(length, KV, HD)
    query = low_back(low(rotate(query_pre, cos_table, sine_table)))
    key_rot = low(rotate(key_pre, cos_table, sine_table))
    value_low = low(value_pre)
    key_slots = low_back(jnp.repeat(key_rot, repeats, axis=1))
    value_slots = low_back(jnp.repeat(value_low, repeats, axis=1))
    attended = attention(query, jnp.repeat(key_slots, per_slot, axis=1), jnp.repeat(value_slots, per_slot, axis=1), firsts)
    attended = low_back(low(attended)).reshape(length, HEADS * HD)
    middle = inputs + low_back(product(attended, w_out))
    normed_mlp = low(norm_apply(middle, norm_mlp))
    gate_values = low_back(product(normed_mlp, w_gate))
    up_values = low_back(product(normed_mlp, w_up))
    hidden = low(jax.nn.silu(gate_values) * up_values)
    return middle + low_back(product(hidden, w_down))

def reference(tokens, starts, w_query, w_key, w_value, w_out, w_gate, w_up, w_down, norm_attn, norm_mlp, cotangent):
    params = (w_query.astype(jnp.float32), w_key.astype(jnp.float32), w_value.astype(jnp.float32), w_out.astype(jnp.float32), w_gate.astype(jnp.float32), w_up.astype(jnp.float32), w_down.astype(jnp.float32), norm_attn.astype(jnp.float32), norm_mlp.astype(jnp.float32))
    length = tokens.shape[1]
    places = jnp.arange(length, dtype=jnp.int32)

    def one_sequence(totals, sliced):
        inputs, start_row, cotangent_row = sliced
        inside = start_row[None, :] <= places[:, None]
        firsts = lax.optimization_barrier(jnp.max(jnp.where(inside, start_row[None, :], 0), axis=1))
        cos_table, sine_table = rotary_tables((places - firsts).astype(jnp.float32))

        def forward(layer_in, weights):
            return block_layer(layer_in, weights, firsts, cos_table, sine_table)
        result, pullback = jax.vjp(forward, inputs.astype(jnp.float32), params)
        grad_inputs, grad_params = pullback(cotangent_row.astype(jnp.float32))
        totals = tuple((running_sum + addend for running_sum, addend in zip(totals, grad_params)))
        return (totals, (result.astype(jnp.bfloat16), grad_inputs.astype(jnp.bfloat16)))
    zero_grads = tuple((jnp.zeros_like(weight) for weight in params))
    totals, (outputs, grad_tokens) = lax.scan(one_sequence, zero_grads, (tokens, starts, cotangent))
    return (outputs, grad_tokens, totals[0], totals[1], totals[2], totals[3], totals[4], totals[5], totals[6], totals[7], totals[8])
```

```python
import functools

import jax
import jax.numpy as jnp
from jax import lax
from jax.experimental import pallas as pl
from jax.experimental.pallas import tpu as pltpu
from jax.sharding import PartitionSpec as P

HEADS = 32
KV = 4
HD = 64
EPSILON = 1e-05
ROPE_BASE = 10000.0
MASKED = -1e30
GROUP = 4
AXES = ("fsdp", "seq")
BF = jnp.bfloat16
F32 = jnp.float32


def contract(left, right, left_dim, right_dim):
    return lax.dot_general(
        left, right, (((left_dim,), (right_dim,)), ((), ())), preferred_element_type=F32
    )


def doc_first(start_row, places):
    inside = start_row[None, :] <= places[:, None]
    return jnp.max(jnp.where(inside, start_row[None, :], 0), axis=1)


def rotary_tables(offsets):
    half_dim = HD // 2
    frequency = ROPE_BASE ** (-(jnp.arange(half_dim, dtype=F32) / half_dim))
    angles = frequency[:, None] * offsets.astype(F32)[None, :]
    return (jnp.cos(angles), jnp.sin(angles))


def rotate(values, cos_table, sine_table):
    half_dim = HD // 2
    front_half = values[:, :half_dim]
    back_half = values[:, half_dim:]
    return jnp.concatenate(
        [
            front_half * cos_table - back_half * sine_table,
            back_half * cos_table + front_half * sine_table,
        ],
        axis=1,
    )


def unrotate(grads_in, cos_table, sine_table):
    return rotate(grads_in, cos_table, -sine_table)


def swap_pair(flag, pair):
    return [jnp.where(flag == 1, pair[1], pair[0]), jnp.where(flag == 1, pair[0], pair[1])]


def forward_kernel(
    meta, query_ref, keyval_ref, first_ref, out_ref, lse_ref, q_all, top, total, acc, *, rows, heads, pair
):
    cell = pl.program_id(0)
    lowest, highest, key_base, first_most, query_at = (meta[cell, i] for i in range(5))
    for head in range(heads):
        q_all[:, head * rows : (head + 1) * rows] = query_ref[head]
    top[...] = jnp.full_like(top, MASKED)
    total[...] = jnp.zeros_like(total)
    acc[...] = jnp.zeros_like(acc)
    width = pair * rows

    def visit(block, masked):
        start = pl.multiple_of(block * rows, rows)
        keyval = keyval_ref[0, pl.ds(start, rows), :]
        key = keyval[:, :HD]
        value_t = keyval[:, HD:].T
        if masked:
            key_at = key_base + start + lax.broadcasted_iota(jnp.int32, (rows, rows), 0)
            token_at = query_at + lax.broadcasted_iota(jnp.int32, (rows, rows), 1)
            allowed = (key_at <= token_at) & (key_at >= first_ref[0])
            bias = jnp.where(allowed, 0.0, MASKED)
            bias = jnp.concatenate([bias] * pair, axis=1)
        for piece in range(heads // pair):
            cols = slice(piece * width, (piece + 1) * width)
            score = contract(key, q_all[:, cols], 1, 0)
            if masked:
                score = score + bias
            before = top[:, cols]
            now = jnp.maximum(before, jnp.max(score, axis=0, keepdims=True))
            weight = jnp.exp(score - now)
            decay = jnp.exp(before - now)
            top[:, cols] = now
            total[:, cols] = total[:, cols] * decay + jnp.sum(weight, axis=0, keepdims=True)
            acc[:, cols] = acc[:, cols] * decay + contract(value_t, weight.astype(BF), 1, 0)

    def step(block, carry):
        plain = jnp.logical_and(key_base + block * rows >= first_most, block < highest)

        @pl.when(plain)
        def _():
            visit(block, False)

        @pl.when(jnp.logical_not(plain))
        def _():
            visit(block, True)

        return carry

    lax.fori_loop(lowest, highest + 1, step, 0)
    sums = total[...]
    scaled = acc[...] * (1.0 / sums)
    for head in range(heads):
        out_ref[head] = scaled[:, head * rows : (head + 1) * rows].astype(BF)
    lse_ref[0] = top[...] + jnp.log(sums)


def backward_kernel(
    meta,
    query_ref,
    keyval_ref,
    first_ref,
    out_ref,
    lse_ref,
    grad_ref,
    dquery_ref,
    dkeyval_ref,
    q_all,
    g_all,
    delta,
    dq_acc,
    dkv_acc,
    *,
    rows,
    heads,
    pair,
):
    cell = pl.program_id(0)
    lowest, highest, key_base, first_most, query_at = (meta[cell, i] for i in range(5))
    for head in range(heads):
        cols = slice(head * rows, (head + 1) * rows)
        q_all[:, cols] = query_ref[head]
        g_all[:, cols] = grad_ref[head]
        delta[:, cols] = jnp.sum(
            grad_ref[head].astype(F32) * out_ref[head].astype(F32), axis=0, keepdims=True
        )
    dq_acc[...] = jnp.zeros_like(dq_acc)

    @pl.when(cell % 2 == 0)
    def _():
        dkv_acc[...] = jnp.zeros_like(dkv_acc)

    width = pair * rows

    def visit(block, masked):
        start = pl.multiple_of(block * rows, rows)
        keyval = keyval_ref[0, pl.ds(start, rows), :]
        key = keyval[:, :HD]
        value = keyval[:, HD:]
        key_t = key.T
        if masked:
            key_at = key_base + start + lax.broadcasted_iota(jnp.int32, (rows, rows), 0)
            token_at = query_at + lax.broadcasted_iota(jnp.int32, (rows, rows), 1)
            allowed = (key_at <= token_at) & (key_at >= first_ref[0])
            bias = jnp.where(allowed, 0.0, MASKED)
            bias = jnp.concatenate([bias] * pair, axis=1)
        dkey = jnp.zeros((rows, HD), F32)
        dvalue = jnp.zeros((rows, HD), F32)
        for piece in range(heads // pair):
            cols = slice(piece * width, (piece + 1) * width)
            score = contract(key, q_all[:, cols], 1, 0)
            if masked:
                score = score + bias
            weight = jnp.exp(score - lse_ref[0, :, cols])
            dweight = contract(value, g_all[:, cols], 1, 0)
            dscore = (weight * (dweight - delta[:, cols])).astype(BF)
            dq_acc[:, cols] = dq_acc[:, cols] + contract(key_t, dscore, 1, 0)
            dkey = dkey + contract(dscore, q_all[:, cols], 1, 1)
            dvalue = dvalue + contract(weight.astype(BF), g_all[:, cols], 1, 1)
        dkv_acc[pl.ds(start, rows), :] = dkv_acc[pl.ds(start, rows), :] + jnp.concatenate(
            [dkey, dvalue], axis=1
        )

    def step(block, carry):
        plain = jnp.logical_and(key_base + block * rows >= first_most, block < highest)

        @pl.when(plain)
        def _():
            visit(block, False)

        @pl.when(jnp.logical_not(plain))
        def _():
            visit(block, True)

        return carry

    lax.fori_loop(lowest, highest + 1, step, 0)
    scaled = dq_acc[...] * HD ** (-0.5)
    for head in range(heads):
        dquery_ref[head] = scaled[:, head * rows : (head + 1) * rows].astype(BF)

    @pl.when(cell % 2 == 1)
    def _():
        dkeyval_ref[0] = dkv_acc[...].astype(BF)


def attention_specs(rows, heads, keys):
    return dict(
        head=pl.BlockSpec((heads, HD, rows), lambda cell, meta: (0, 0, cell)),
        keyval=pl.BlockSpec((1, keys, 2 * HD), lambda cell, meta: (cell // 2, 0, 0)),
        first=pl.BlockSpec((1, 1, rows), lambda cell, meta: (cell, 0, 0)),
        stat=pl.BlockSpec((1, 1, heads * rows), lambda cell, meta: (cell, 0, 0)),
    )


def attend_forward(meta, query, keyval, first):
    heads, _, tokens = query.shape
    rows = tokens // GROUP
    keys = keyval.shape[1]
    specs = attention_specs(rows, heads, keys)
    wide = heads * rows
    return pl.pallas_call(
        functools.partial(forward_kernel, rows=rows, heads=heads, pair=2),
        grid_spec=pltpu.PrefetchScalarGridSpec(
            num_scalar_prefetch=1,
            grid=(GROUP,),
            in_specs=[specs["head"], specs["keyval"], specs["first"]],
            out_specs=[specs["head"], specs["stat"]],
            scratch_shapes=[
                pltpu.VMEM((HD, wide), BF),
                pltpu.VMEM((1, wide), F32),
                pltpu.VMEM((1, wide), F32),
                pltpu.VMEM((HD, wide), F32),
            ],
        ),
        out_shape=(
            jax.ShapeDtypeStruct(query.shape, BF),
            jax.ShapeDtypeStruct((GROUP, 1, wide), F32),
        ),
        compiler_params=pltpu.CompilerParams(
            dimension_semantics=("arbitrary",), vmem_limit_bytes=48 * 1024 * 1024
        ),
        cost_estimate=pl.CostEstimate(
            flops=40_000_000_000, bytes_accessed=10_000_000, transcendentals=0
        ),
        name="attend_forward",
    )(meta, query, keyval, first)


def attend_backward(meta, query, keyval, first, out, lse, grad):
    heads, _, tokens = query.shape
    rows = tokens // GROUP
    keys = keyval.shape[1]
    specs = attention_specs(rows, heads, keys)
    wide = heads * rows
    return pl.pallas_call(
        functools.partial(backward_kernel, rows=rows, heads=heads, pair=2),
        grid_spec=pltpu.PrefetchScalarGridSpec(
            num_scalar_prefetch=1,
            grid=(GROUP,),
            in_specs=[
                specs["head"],
                specs["keyval"],
                specs["first"],
                specs["head"],
                specs["stat"],
                specs["head"],
            ],
            out_specs=[specs["head"], specs["keyval"]],
            scratch_shapes=[
                pltpu.VMEM((HD, wide), BF),
                pltpu.VMEM((HD, wide), BF),
                pltpu.VMEM((1, wide), F32),
                pltpu.VMEM((HD, wide), F32),
                pltpu.VMEM((keys, 2 * HD), F32),
            ],
        ),
        out_shape=(
            jax.ShapeDtypeStruct(query.shape, BF),
            jax.ShapeDtypeStruct(keyval.shape, BF),
        ),
        compiler_params=pltpu.CompilerParams(
            dimension_semantics=("arbitrary",), vmem_limit_bytes=48 * 1024 * 1024
        ),
        cost_estimate=pl.CostEstimate(
            flops=80_000_000_000, bytes_accessed=16_000_000, transcendentals=0
        ),
        name="attend_backward",
    )(meta, query, keyval, first, out, lse, grad)


def shards(
    tokens,
    starts,
    w_query,
    w_key,
    w_value,
    w_out,
    w_gate,
    w_up,
    w_down,
    norm_attn,
    norm_mlp,
    cotangent,
):
    seq_count = lax.axis_size("seq")
    fsdp_count = lax.axis_size("fsdp")
    deep = seq_count // 2
    wide = fsdp_count // 2
    ring = wide * deep
    half_ring = ring // 2
    f_at, s_at = lax.axis_index("fsdp"), lax.axis_index("seq")
    x_at, y_at, c_at, z_at = f_at % 2, f_at // 2, s_at % 2, s_at // 2
    rows = tokens.shape[1]
    width = tokens.shape[2]
    own_rows = w_query.shape[0]

    def perm_of(move):
        found = []
        for f in range(fsdp_count):
            for s in range(seq_count):
                target = move(f // 2, f % 2, s // 2, s % 2)
                if target is not None:
                    ty, tx, tz, tc = target
                    found.append((f * seq_count + s, (ty * 2 + tx) * seq_count + tz * 2 + tc))
        return found

    def ring_place(position):
        position = position % ring
        row, col = position // deep, position % deep
        return row, col if row % 2 == 0 else deep - 1 - col

    def ring_index(y, z):
        return y * deep + (z if y % 2 == 0 else deep - 1 - z)

    def around(step):
        def move(y, x, z, c):
            ty, tz = ring_place(ring_index(y, z) + step)
            return ty, x, tz, c

        return move

    def along(step):
        return lambda y, x, z, c: (y, x, z + step, c) if 0 <= z + step < deep else None

    core_perm = perm_of(lambda y, x, z, c: (y, x, z, 1 - c))
    x_perm = perm_of(lambda y, x, z, c: (y, 1 - x, z, c))
    cross_perm = perm_of(lambda y, x, z, c: (y, 1 - x, z, 1 - c))
    right_perm, left_perm = perm_of(around(1)), perm_of(around(-1))

    def send(value, perm):
        return lax.ppermute(value, AXES, perm)

    position = y_at * deep + jnp.where(y_at % 2 == 0, z_at, deep - 1 - z_at)

    def place_at(offset):
        index = lax.rem(position + offset + 2 * ring, ring)
        row, col = index // deep, index % deep
        return row, jnp.where(row % 2 == 0, col, deep - 1 - col)

    def gather_group(block):
        near = send(block, core_perm)
        far = send(block, x_perm)
        return jnp.concatenate([block, near, far, send(far, core_perm)], axis=0)

    def to_quarters(pieces):
        return jnp.concatenate(
            [p.reshape(own_rows, GROUP, -1).transpose(1, 0, 2) for p in pieces], axis=2
        )

    def exchange_group(quarters):
        def of(dx, dc):
            return lax.dynamic_index_in_dim(
                quarters, (x_at ^ dx) * 2 + (c_at ^ dc), 0, keepdims=False
            )

        got = [
            [of(0, 0), send(of(0, 1), core_perm)],
            [send(of(1, 0), x_perm), send(of(1, 1), cross_perm)],
        ]
        return got

    def absolute(got):
        rows_of = [swap_pair(c_at, pair) for pair in got]
        ordered = [swap_pair(x_at, [rows_of[0][c], rows_of[1][c]]) for c in range(2)]
        return [[ordered[0][x], ordered[1][x]] for x in range(2)]

    def gather_ring(chunk):
        columns = chunk.shape[2]
        whole = jnp.zeros((wide, 2, deep, chunk.shape[1], columns), chunk.dtype)

        def put(whole, piece, offset, x_from):
            row, col = place_at(offset)
            piece = piece[None, :, None]
            return lax.dynamic_update_slice(whole, piece, (row, x_from, col, 0, 0))

        whole = put(whole, chunk, 0, 0)
        right = left = chunk
        for step in range(1, half_ring):
            right = send(right, right_perm)
            left = send(left, left_perm)
            whole = put(whole, right, -step, 0)
            whole = put(whole, left, step, 0)
        whole = put(whole, send(right[:1], right_perm), half_ring, 0)
        whole = put(whole, send(left[1:], left_perm), half_ring, 1)
        return whole.reshape(-1, columns)

    def scatter_ring(partial):
        columns = partial.shape[1]
        parts = partial.reshape(wide, 2, deep, 2 * own_rows, columns)

        def part(offset, x_from=0, x_count=2):
            row, col = place_at(offset)
            return lax.dynamic_slice(
                parts, (row, x_from, col, 0, 0), (1, x_count, 1, 2 * own_rows, columns)
            ).reshape(x_count, 2 * own_rows, columns)

        right = send(part(half_ring, 0, 1), right_perm)
        left = send(part(half_ring, 1, 1), left_perm)
        for step in range(half_ring - 1, 0, -1):
            to_right, to_left = part(step), part(-step)
            if step == half_ring - 1:
                to_right = jnp.concatenate(
                    [(to_right[:1].astype(F32) + right.astype(F32)).astype(BF), to_right[1:]]
                )
                to_left = jnp.concatenate(
                    [to_left[:1], (to_left[1:].astype(F32) + left.astype(F32)).astype(BF)]
                )
            else:
                to_right = (to_right.astype(F32) + right.astype(F32)).astype(BF)
                to_left = (to_left.astype(F32) + left.astype(F32)).astype(BF)
            right = send(to_right, right_perm)
            left = send(to_left, left_perm)
        own = part(0).astype(F32)
        if half_ring > 1:
            return own + right.astype(F32) + left.astype(F32)
        return own + jnp.concatenate([right, left]).astype(F32)

    def gather_weights(pieces):
        got = absolute(exchange_group(to_quarters(pieces)))
        chunk = jnp.stack([jnp.concatenate(got[x], axis=0) for x in range(2)])
        return gather_ring(chunk)

    def scatter_weights(partial):
        chunk = scatter_ring(partial).astype(BF)
        blocks = [[chunk[x, c * own_rows : (c + 1) * own_rows] for c in range(2)] for x in range(2)]
        relative = absolute(blocks)
        got = [
            [relative[0][0], send(relative[0][1], core_perm)],
            [send(relative[1][0], x_perm), send(relative[1][1], cross_perm)],
        ]
        final = absolute(got)
        return jnp.stack([final[0][0], final[0][1], final[1][0], final[1][1]]).astype(F32)

    def columns_of(quarters):
        return quarters.transpose(1, 0, 2).reshape(own_rows, -1)

    def reduce_group(partial):
        parts = partial.reshape(2, 2, rows, width)
        far = parts[1, 0] + send(parts[1, 1].astype(BF), core_perm).astype(F32)
        near = parts[0, 0] + send(parts[0, 1].astype(BF), core_perm).astype(F32)
        return near + send(far.astype(BF), x_perm).astype(F32)

    own_tokens = tokens[0]
    group_tokens = gather_group(own_tokens)
    weights_attn = gather_weights([w_query, w_key, w_value, w_out.T])
    start_rows = [starts[0], send(starts, x_perm)[0]]
    gains = lax.all_gather(jnp.stack([norm_attn, norm_mlp]), AXES, axis=1, tiled=True)
    gain_attn, gain_mlp = gains[0].astype(F32), gains[1].astype(F32)
    group_cotangent = gather_group(cotangent[0])
    w_gate_q = gather_weights([w_gate])
    w_up_q = gather_weights([w_up])
    w_down_q = gather_weights([w_down.T])

    block_at = [rows * (2 * z_at + (c_at ^ dc)) for dc in range(2)]
    within = jnp.arange(rows, dtype=jnp.int32)
    cells = [(dx, dc) for dx in range(2) for dc in range(2)]
    places = [block_at[dc] + within for dx, dc in cells]
    firsts = [doc_first(start_rows[dx], places[i]) for i, (dx, dc) in enumerate(cells)]
    offsets = jnp.concatenate([p - f for p, f in zip(places, firsts)])
    cos_table, sine_table = rotary_tables(offsets)
    first_rows = jnp.stack(firsts)[:, None, :]
    base_block = 2 * (z_at - deep + 1)
    meta = jnp.stack(
        [
            jnp.stack(
                [
                    firsts[i][0] // rows - base_block,
                    block_at[dc] // rows - base_block,
                    base_block * rows,
                    firsts[i][rows - 1],
                    block_at[dc],
                ]
            )
            for i, (dx, dc) in enumerate(cells)
        ]
    ).astype(jnp.int32)

    per_device = HEADS // GROUP
    q_cols = per_device * HD
    qkv_cols = q_cols + 2 * HD
    group_inputs = group_tokens.astype(F32)
    scale_group = lax.rsqrt(jnp.mean(group_inputs * group_inputs, axis=1, keepdims=True) + EPSILON)
    normed = (group_inputs * scale_group * gain_attn).astype(BF)
    w_qkv, w_out_t = weights_attn[:, :qkv_cols], weights_attn[:, qkv_cols:]
    pre = contract(w_qkv, normed, 0, 1)
    query = (
        rotate(pre[:q_cols].reshape(per_device, HD, -1), cos_table, sine_table) * HD ** (-0.5)
    ).astype(BF)
    key = rotate(pre[q_cols : q_cols + HD][None], cos_table, sine_table)[0].astype(BF)
    keyval = jnp.concatenate([key, pre[q_cols + HD :].astype(BF)], axis=0).T
    keyval = keyval.reshape(2, 2, rows, 2 * HD)
    keyval = jnp.stack([jnp.stack(swap_pair(c_at, [keyval[dx, 0], keyval[dx, 1]])) for dx in range(2)])
    keyval = keyval.reshape(2, 2 * rows, 2 * HD)
    earlier = [send(keyval, perm_of(along(step))) for step in range(deep - 1, 0, -1)]
    keyvals = jnp.concatenate(earlier + [keyval], axis=1)

    attended, lse = attend_forward(meta, query, keyvals, first_rows)
    attended_t = attended.reshape(q_cols, -1)
    middle = own_tokens.astype(F32) + reduce_group(contract(attended_t, w_out_t, 0, 1))

    scale_mlp = lax.rsqrt(jnp.mean(middle * middle, axis=1, keepdims=True) + EPSILON)
    normed_mlp = gather_group((middle * scale_mlp * gain_mlp).astype(BF))
    gate = contract(normed_mlp, w_gate_q, 1, 0)
    up = contract(normed_mlp, w_up_q, 1, 0)
    d_hidden = contract(group_cotangent, w_down_q, 1, 0)
    sigmoid = jax.nn.sigmoid(gate)
    silu = gate * sigmoid
    hidden = (silu * up).astype(BF)
    d_gate = (d_hidden * up * sigmoid * (1.0 + gate * (1.0 - sigmoid))).astype(BF)
    d_up = (d_hidden * silu).astype(BF)
    d_normed_mlp = reduce_group(contract(d_gate, w_gate_q, 1, 1) + contract(d_up, w_up_q, 1, 1))
    result = middle + reduce_group(contract(hidden, w_down_q, 1, 1))
    grad_gate = scatter_weights(contract(normed_mlp, d_gate, 0, 0).astype(BF))
    grad_up = scatter_weights(contract(normed_mlp, d_up, 0, 0).astype(BF))
    grad_down = scatter_weights(contract(group_cotangent, hidden, 0, 0).astype(BF))

    def norm_backward(values, scale_rows, gain, grads_in):
        weighted = grads_in * gain
        gain_grad = jnp.sum(grads_in * values * scale_rows, axis=0)
        inner_mean = jnp.mean(weighted * values, axis=1, keepdims=True)
        cube = scale_rows * scale_rows * scale_rows
        return scale_rows * weighted - values * cube * inner_mean, gain_grad

    d_middle, gain_grad_mlp = norm_backward(middle, scale_mlp, gain_mlp, d_normed_mlp)
    d_middle = d_middle + cotangent[0].astype(F32)

    d_branch = gather_group(d_middle.astype(BF))
    d_attended = contract(w_out_t, d_branch, 0, 1).astype(BF).reshape(query.shape)
    grad_out_t = contract(d_branch, attended_t, 0, 1).astype(BF)
    d_query, d_keyvals = attend_backward(meta, query, keyvals, first_rows, attended, lse, d_attended)
    d_chunks = d_keyvals.reshape(2, deep, 2 * rows, 2 * HD)
    d_keyval = d_chunks[:, deep - 1].astype(F32)
    for step in range(1, deep):
        d_keyval = d_keyval + send(d_chunks[:, deep - 1 - step], perm_of(along(-step))).astype(F32)
    d_keyval = d_keyval.reshape(2, 2, rows, 2 * HD)
    d_keyval = jnp.stack([jnp.stack(swap_pair(c_at, [d_keyval[dx, 0], d_keyval[dx, 1]])) for dx in range(2)])
    d_keyval = d_keyval.reshape(GROUP * rows, 2 * HD).T
    d_query_pre = unrotate(d_query.astype(F32), cos_table, sine_table).astype(BF)
    d_key_pre = unrotate(d_keyval[None, :HD], cos_table, sine_table)[0].astype(BF)
    d_pre = jnp.concatenate(
        [d_query_pre.reshape(q_cols, -1), d_key_pre, d_keyval[HD:].astype(BF)], axis=0
    )
    d_normed = reduce_group(contract(d_pre, w_qkv, 0, 1))
    grad_qkv = contract(normed, d_pre, 0, 1).astype(BF)
    grad_attn = scatter_weights(jnp.concatenate([grad_qkv, grad_out_t], axis=1))
    inputs = own_tokens.astype(F32)
    scale_attn = scale_group[:rows]
    d_inputs, gain_grad_attn = norm_backward(inputs, scale_attn, gain_attn, d_normed)
    d_inputs = d_inputs + d_middle

    gain_grads = lax.psum_scatter(
        jnp.stack([gain_grad_attn, gain_grad_mlp]), AXES, scatter_dimension=1, tiled=True
    )
    return (
        result.astype(BF)[None],
        d_inputs.astype(BF)[None],
        columns_of(grad_attn[:, :, :q_cols]),
        columns_of(grad_attn[:, :, q_cols : q_cols + HD]),
        columns_of(grad_attn[:, :, q_cols + HD : qkv_cols]),
        columns_of(grad_attn[:, :, qkv_cols:]).T,
        columns_of(grad_gate),
        columns_of(grad_up),
        columns_of(grad_down).T,
        gain_grads[0],
        gain_grads[1],
    )


def solution(mesh):
    token_spec = P("fsdp", "seq", None)
    row_spec = P(AXES, None)
    column_spec = P(None, AXES)
    gain_spec = P(AXES)
    return jax.shard_map(
        shards,
        mesh=mesh,
        in_specs=(
            token_spec,
            P("fsdp", None),
            row_spec,
            row_spec,
            row_spec,
            column_spec,
            row_spec,
            row_spec,
            column_spec,
            gain_spec,
            gain_spec,
            token_spec,
        ),
        out_specs=(
            token_spec,
            token_spec,
            row_spec,
            row_spec,
            row_spec,
            column_spec,
            row_spec,
            row_spec,
            column_spec,
            gain_spec,
            gain_spec,
        ),
        check_vma=False,
    )
```

```python
import functools

import jax
import jax.numpy as jnp
from jax import lax
from jax.experimental import pallas as pl
from jax.experimental.pallas import tpu as pltpu
from jax.sharding import PartitionSpec as P

HEADS = 32
KV = 4
HD = 64
EPSILON = 1e-05
ROPE_BASE = 10000.0
MASKED = -1e30
GROUP = 4
AXES = ("fsdp", "seq")
BF = jnp.bfloat16
F32 = jnp.float32


def contract(left, right, left_dim, right_dim):
    return lax.dot_general(
        left, right, (((left_dim,), (right_dim,)), ((), ())), preferred_element_type=F32
    )


def doc_first(start_row, places):
    inside = start_row[None, :] <= places[:, None]
    return jnp.max(jnp.where(inside, start_row[None, :], 0), axis=1)


def rotary_tables(offsets):
    half_dim = HD // 2
    frequency = ROPE_BASE ** (-(jnp.arange(half_dim, dtype=F32) / half_dim))
    angles = frequency[:, None] * offsets.astype(F32)[None, :]
    return (jnp.cos(angles), jnp.sin(angles))


def rotate(values, cos_table, sine_table):
    half_dim = HD // 2
    front_half = values[:, :half_dim]
    back_half = values[:, half_dim:]
    return jnp.concatenate(
        [
            front_half * cos_table - back_half * sine_table,
            back_half * cos_table + front_half * sine_table,
        ],
        axis=1,
    )


def unrotate(grads_in, cos_table, sine_table):
    return rotate(grads_in, cos_table, -sine_table)


def swap_pair(flag, pair):
    return [jnp.where(flag == 1, pair[1], pair[0]), jnp.where(flag == 1, pair[0], pair[1])]


def forward_kernel(
    meta, query_ref, keyval_ref, first_ref, out_ref, lse_ref, q_all, top, total, acc, *, rows, heads, pair
):
    cell = pl.program_id(0)
    lowest, highest, key_base, first_most, query_at = (meta[cell, i] for i in range(5))
    for head in range(heads):
        q_all[:, head * rows : (head + 1) * rows] = query_ref[head]
    top[...] = jnp.full_like(top, MASKED)
    total[...] = jnp.zeros_like(total)
    acc[...] = jnp.zeros_like(acc)
    width = pair * rows

    def visit(block, masked):
        start = pl.multiple_of(block * rows, rows)
        keyval = keyval_ref[pl.ds(start, rows), :]
        key = keyval[:, :HD]
        value_t = keyval[:, HD:].T
        if masked:
            key_at = key_base + start + lax.broadcasted_iota(jnp.int32, (rows, rows), 0)
            token_at = query_at + lax.broadcasted_iota(jnp.int32, (rows, rows), 1)
            allowed = (key_at <= token_at) & (key_at >= first_ref[0])
            bias = jnp.where(allowed, 0.0, MASKED)
            bias = jnp.concatenate([bias] * pair, axis=1)
        for piece in range(heads // pair):
            cols = slice(piece * width, (piece + 1) * width)
            score = contract(key, q_all[:, cols], 1, 0)
            if masked:
                score = score + bias
            before = top[:, cols]
            now = jnp.maximum(before, jnp.max(score, axis=0, keepdims=True))
            weight = jnp.exp(score - now)
            decay = jnp.exp(before - now)
            top[:, cols] = now
            total[:, cols] = total[:, cols] * decay + jnp.sum(weight, axis=0, keepdims=True)
            acc[:, cols] = acc[:, cols] * decay + contract(value_t, weight.astype(BF), 1, 0)

    def step(block, carry):
        plain = jnp.logical_and(key_base + block * rows >= first_most, block < highest)

        @pl.when(plain)
        def _():
            visit(block, False)

        @pl.when(jnp.logical_not(plain))
        def _():
            visit(block, True)

        return carry

    lax.fori_loop(lowest, highest + 1, step, 0)
    sums = total[...]
    scaled = acc[...] * (1.0 / sums)
    for head in range(heads):
        out_ref[head] = scaled[:, head * rows : (head + 1) * rows].astype(BF)
    lse_ref[0] = top[...] + jnp.log(sums)


def backward_kernel(
    meta,
    query_ref,
    keyval_ref,
    first_ref,
    out_ref,
    lse_ref,
    grad_ref,
    dquery_ref,
    dkeyval_ref,
    q_all,
    g_all,
    delta,
    dq_acc,
    dkv_acc,
    *,
    rows,
    heads,
    pair,
):
    cell = pl.program_id(0)
    lowest, highest, key_base, first_most, query_at = (meta[cell, i] for i in range(5))
    for head in range(heads):
        cols = slice(head * rows, (head + 1) * rows)
        q_all[:, cols] = query_ref[head]
        g_all[:, cols] = grad_ref[head]
        delta[:, cols] = jnp.sum(
            grad_ref[head].astype(F32) * out_ref[head].astype(F32), axis=0, keepdims=True
        )
    dq_acc[...] = jnp.zeros_like(dq_acc)

    @pl.when(cell == 0)
    def _():
        dkv_acc[...] = jnp.zeros_like(dkv_acc)

    width = pair * rows

    def visit(block, masked):
        start = pl.multiple_of(block * rows, rows)
        keyval = keyval_ref[pl.ds(start, rows), :]
        key = keyval[:, :HD]
        value = keyval[:, HD:]
        key_t = key.T
        if masked:
            key_at = key_base + start + lax.broadcasted_iota(jnp.int32, (rows, rows), 0)
            token_at = query_at + lax.broadcasted_iota(jnp.int32, (rows, rows), 1)
            allowed = (key_at <= token_at) & (key_at >= first_ref[0])
            bias = jnp.where(allowed, 0.0, MASKED)
            bias = jnp.concatenate([bias] * pair, axis=1)
        dkey = jnp.zeros((rows, HD), F32)
        dvalue = jnp.zeros((rows, HD), F32)
        for piece in range(heads // pair):
            cols = slice(piece * width, (piece + 1) * width)
            score = contract(key, q_all[:, cols], 1, 0)
            if masked:
                score = score + bias
            weight = jnp.exp(score - lse_ref[0, :, cols])
            dweight = contract(value, g_all[:, cols], 1, 0)
            dscore = (weight * (dweight - delta[:, cols])).astype(BF)
            dq_acc[:, cols] = dq_acc[:, cols] + contract(key_t, dscore, 1, 0)
            dkey = dkey + contract(dscore, q_all[:, cols], 1, 1)
            dvalue = dvalue + contract(weight.astype(BF), g_all[:, cols], 1, 1)
        dkv_acc[pl.ds(start, rows), :] = dkv_acc[pl.ds(start, rows), :] + jnp.concatenate(
            [dkey, dvalue], axis=1
        )

    def step(block, carry):
        plain = jnp.logical_and(key_base + block * rows >= first_most, block < highest)

        @pl.when(plain)
        def _():
            visit(block, False)

        @pl.when(jnp.logical_not(plain))
        def _():
            visit(block, True)

        return carry

    lax.fori_loop(lowest, highest + 1, step, 0)
    scaled = dq_acc[...] * HD ** (-0.5)
    for head in range(heads):
        dquery_ref[head] = scaled[:, head * rows : (head + 1) * rows].astype(BF)

    @pl.when(cell == 1)
    def _():
        dkeyval_ref[...] = dkv_acc[...].astype(BF)


def attention_specs(rows, heads, keys):
    return dict(
        head=pl.BlockSpec((heads, HD, rows), lambda cell, meta: (0, 0, cell)),
        keyval=pl.BlockSpec((keys, 2 * HD), lambda cell, meta: (0, 0)),
        first=pl.BlockSpec((1, 1, rows), lambda cell, meta: (cell, 0, 0)),
        stat=pl.BlockSpec((1, 1, heads * rows), lambda cell, meta: (cell, 0, 0)),
    )


def attend_forward(meta, query, keyval, first):
    heads, _, tokens = query.shape
    rows = tokens // 2
    keys = keyval.shape[0]
    specs = attention_specs(rows, heads, keys)
    wide = heads * rows
    return pl.pallas_call(
        functools.partial(forward_kernel, rows=rows, heads=heads, pair=2),
        grid_spec=pltpu.PrefetchScalarGridSpec(
            num_scalar_prefetch=1,
            grid=(2,),
            in_specs=[specs["head"], specs["keyval"], specs["first"]],
            out_specs=[specs["head"], specs["stat"]],
            scratch_shapes=[
                pltpu.VMEM((HD, wide), BF),
                pltpu.VMEM((1, wide), F32),
                pltpu.VMEM((1, wide), F32),
                pltpu.VMEM((HD, wide), F32),
            ],
        ),
        out_shape=(
            jax.ShapeDtypeStruct(query.shape, BF),
            jax.ShapeDtypeStruct((2, 1, wide), F32),
        ),
        compiler_params=pltpu.CompilerParams(
            dimension_semantics=("arbitrary",), vmem_limit_bytes=48 * 1024 * 1024
        ),
        cost_estimate=pl.CostEstimate(
            flops=40_000_000_000, bytes_accessed=10_000_000, transcendentals=0
        ),
        name="attend_forward",
    )(meta, query, keyval, first)


def attend_backward(meta, query, keyval, first, out, lse, grad):
    heads, _, tokens = query.shape
    rows = tokens // 2
    keys = keyval.shape[0]
    specs = attention_specs(rows, heads, keys)
    wide = heads * rows
    return pl.pallas_call(
        functools.partial(backward_kernel, rows=rows, heads=heads, pair=2),
        grid_spec=pltpu.PrefetchScalarGridSpec(
            num_scalar_prefetch=1,
            grid=(2,),
            in_specs=[
                specs["head"],
                specs["keyval"],
                specs["first"],
                specs["head"],
                specs["stat"],
                specs["head"],
            ],
            out_specs=[specs["head"], specs["keyval"]],
            scratch_shapes=[
                pltpu.VMEM((HD, wide), BF),
                pltpu.VMEM((HD, wide), BF),
                pltpu.VMEM((1, wide), F32),
                pltpu.VMEM((HD, wide), F32),
                pltpu.VMEM((keys, 2 * HD), F32),
            ],
        ),
        out_shape=(
            jax.ShapeDtypeStruct(query.shape, BF),
            jax.ShapeDtypeStruct(keyval.shape, BF),
        ),
        compiler_params=pltpu.CompilerParams(
            dimension_semantics=("arbitrary",), vmem_limit_bytes=48 * 1024 * 1024
        ),
        cost_estimate=pl.CostEstimate(
            flops=80_000_000_000, bytes_accessed=16_000_000, transcendentals=0
        ),
        name="attend_backward",
    )(meta, query, keyval, first, out, lse, grad)


def shards(
    tokens,
    starts,
    w_query,
    w_key,
    w_value,
    w_out,
    w_gate,
    w_up,
    w_down,
    norm_attn,
    norm_mlp,
    cotangent,
):
    seq_count = lax.axis_size("seq")
    fsdp_count = lax.axis_size("fsdp")
    deep = seq_count // 2
    wide = fsdp_count // 2
    ring = wide * deep
    half_ring = ring // 2
    f_at, s_at = lax.axis_index("fsdp"), lax.axis_index("seq")
    x_at, y_at, c_at, z_at = f_at % 2, f_at // 2, s_at % 2, s_at // 2
    rows = tokens.shape[1]
    width = tokens.shape[2]
    own_rows = w_query.shape[0]

    def perm_of(move):
        found = []
        for f in range(fsdp_count):
            for s in range(seq_count):
                target = move(f // 2, f % 2, s // 2, s % 2)
                if target is not None:
                    ty, tx, tz, tc = target
                    found.append((f * seq_count + s, (ty * 2 + tx) * seq_count + tz * 2 + tc))
        return found

    def ring_place(position):
        position = position % ring
        row, col = position // deep, position % deep
        return row, col if row % 2 == 0 else deep - 1 - col

    def ring_index(y, z):
        return y * deep + (z if y % 2 == 0 else deep - 1 - z)

    def around(step):
        def move(y, x, z, c):
            ty, tz = ring_place(ring_index(y, z) + step)
            return ty, x, tz, c

        return move

    def along(step):
        return lambda y, x, z, c: (y, x, z + step, c) if 0 <= z + step < deep else None

    core_perm = perm_of(lambda y, x, z, c: (y, x, z, 1 - c))
    x_perm = perm_of(lambda y, x, z, c: (y, 1 - x, z, c))
    cross_perm = perm_of(lambda y, x, z, c: (y, 1 - x, z, 1 - c))
    right_perm, left_perm = perm_of(around(1)), perm_of(around(-1))

    def send(value, perm):
        return lax.ppermute(value, AXES, perm)

    position = y_at * deep + jnp.where(y_at % 2 == 0, z_at, deep - 1 - z_at)

    def place_at(offset):
        index = lax.rem(position + offset + 2 * ring, ring)
        row, col = index // deep, index % deep
        return row, jnp.where(row % 2 == 0, col, deep - 1 - col)

    def with_core(block):
        return jnp.concatenate([block, send(block, core_perm)], axis=0)

    def gather_group(block):
        return [with_core(block), with_core(send(block, x_perm))]

    def to_quarters(pieces):
        return jnp.concatenate(
            [p.reshape(own_rows, GROUP, -1).transpose(1, 0, 2) for p in pieces], axis=2
        )

    def exchange_group(quarters):
        def of(dx, dc):
            return lax.dynamic_index_in_dim(
                quarters, (x_at ^ dx) * 2 + (c_at ^ dc), 0, keepdims=False
            )

        got = [
            [of(0, 0), send(of(0, 1), core_perm)],
            [send(of(1, 0), x_perm), send(of(1, 1), cross_perm)],
        ]
        return got

    def absolute(got):
        rows_of = [swap_pair(c_at, pair) for pair in got]
        ordered = [swap_pair(x_at, [rows_of[0][c], rows_of[1][c]]) for c in range(2)]
        return [[ordered[0][x], ordered[1][x]] for x in range(2)]

    class Gather:
        def __init__(self, chunk):
            self.right = self.left = chunk
            self.step, self.got = 0, [(0, 0, chunk)]

        def advance(self, times):
            for _ in range(min(times, half_ring - self.step)):
                self.step += 1
                if self.step < half_ring:
                    self.right = send(self.right, right_perm)
                    self.left = send(self.left, left_perm)
                    self.got += [(-self.step, 0, self.right), (self.step, 0, self.left)]
                else:
                    self.got += [
                        (half_ring, 0, send(self.right[:1], right_perm)),
                        (half_ring, 1, send(self.left[1:], left_perm)),
                    ]

        def wait_for(self, value):
            self.right, self.left = after((self.right, self.left), value)

        def whole(self, cuts):
            results = []
            for low, high in zip(cuts[:-1], cuts[1:]):
                result = jnp.zeros((wide, 2, deep, 2 * own_rows, high - low), BF)
                for offset, x_from, piece in self.got:
                    row, col = place_at(offset)
                    result = lax.dynamic_update_slice(
                        result, piece[None, :, None, :, low:high], (row, x_from, col, 0, 0)
                    )
                results.append(result.reshape(-1, high - low))
            return results

    class Scatter:
        def __init__(self, partial):
            self.parts = partial.reshape(wide, 2, deep, 2 * own_rows, partial.shape[1])
            self.step, self.right, self.left = 0, None, None

        def part(self, offset, x_from=0, x_count=2):
            row, col = place_at(offset)
            return lax.dynamic_slice(
                self.parts,
                (row, x_from, col, 0, 0),
                (1, x_count, 1, 2 * own_rows, self.parts.shape[4]),
            ).reshape(x_count, 2 * own_rows, self.parts.shape[4])

        def advance(self, times):
            for _ in range(min(times, half_ring - self.step)):
                self.step += 1
                offset = half_ring - self.step + 1
                if self.step == 1:
                    to_right, to_left = self.part(offset, 0, 1), self.part(-offset, 1, 1)
                else:
                    to_right, to_left = self.joined(offset, -offset)
                self.right = send(to_right, right_perm)
                self.left = send(to_left, left_perm)

        def joined(self, at_right, at_left):
            to_right, to_left = self.part(at_right), self.part(at_left)
            if self.step == 2:
                to_right = jnp.concatenate([add_low(to_right[:1], self.right), to_right[1:]])
                to_left = jnp.concatenate([to_left[:1], add_low(to_left[1:], self.left)])
                return to_right, to_left
            return add_low(to_right, self.right), add_low(to_left, self.left)

        def wait_for(self, value):
            self.right, self.left = after((self.right, self.left), value)

        def result(self):
            self.advance(half_ring)
            own = self.part(0).astype(F32)
            if half_ring > 1:
                return own + self.right.astype(F32) + self.left.astype(F32)
            return own + jnp.concatenate([self.right, self.left]).astype(F32)

    class Rings:
        def __init__(self, members):
            self.members = members

        def wait_for(self, value):
            for member in self.members:
                member.wait_for(value)

        def advance(self, times):
            for member in self.members:
                member.advance(times)

    def add_low(one, other):
        return (one.astype(F32) + other.astype(F32)).astype(BF)

    per_window = -(-half_ring // 4)

    def group_chunk(pieces):
        got = absolute(exchange_group(to_quarters(pieces)))
        return jnp.stack([jnp.concatenate(got[x], axis=0) for x in range(2)])

    def to_owners(scatter):
        chunk = scatter.result().astype(BF)
        blocks = [[chunk[x, c * own_rows : (c + 1) * own_rows] for c in range(2)] for x in range(2)]
        relative = absolute(blocks)
        got = [
            [relative[0][0], send(relative[0][1], core_perm)],
            [send(relative[1][0], x_perm), send(relative[1][1], cross_perm)],
        ]
        final = absolute(got)
        return jnp.stack([final[0][0], final[0][1], final[1][0], final[1][1]]).astype(F32)

    def columns_of(quarters):
        return quarters.transpose(1, 0, 2).reshape(own_rows, -1)

    def reduce_core(partial):
        return partial[:rows].astype(F32) + send(partial[rows:], core_perm).astype(F32)

    def send_far(partial):
        return send(reduce_core(partial).astype(BF), x_perm).astype(F32)

    index = f_at * seq_count + s_at
    count = fsdp_count * seq_count
    doublings = [
        (bit, [(i, i ^ (1 << bit)) for i in range(count)]) for bit in range(count.bit_length() - 1)
    ]

    def gather_small(value):
        bits = len(doublings)
        x_bit = seq_count.bit_length() - 1
        order = [x_bit] + [bit for bit in range(bits) if bit != x_bit]
        for bit in order:
            _, perm = doublings[bit]
            pair = swap_pair((index >> bit) & 1, [value, send(value, perm)])
            value = jnp.stack(pair, axis=1)
        axes = [1 + order[::-1].index(bit) for bit in range(bits - 1, -1, -1)]
        value = value.transpose([0] + axes + [bits + 1])
        return value.reshape(value.shape[0], -1)

    def sum_small(value):
        for bit, perm in doublings:
            value = value + send(value, perm)
        return value

    def after(value, other):
        return lax.optimization_barrier((value, other))[0]

    q_cols = HEADS // GROUP * HD
    qkv_cols = q_cols + 2 * HD
    hidden_cols = w_gate.shape[1] // GROUP
    gains = gather_small(jnp.stack([norm_attn, norm_mlp])).astype(F32)
    gain_attn, gain_mlp = gains[0], gains[1]
    start_rows = [starts[0], send(starts, x_perm)[0]]
    chunk_attn = group_chunk([w_query, w_key, w_value, w_out.T])
    own_tokens = tokens[0]
    ring_attn = Gather(chunk_attn)
    ring_attn.advance(half_ring)
    group_tokens = gather_group(after(own_tokens, chunk_attn))
    w_down_in, w_gate_in, w_up_in = after((w_down.T, w_gate, w_up), group_tokens[1])
    ring_down = Gather(group_chunk([w_down_in]))
    ring_gate_up = Gather(group_chunk([w_gate_in, w_up_in]))
    rings = Rings([ring_down, ring_gate_up])
    w_qkv, w_out_t = ring_attn.whole([0, qkv_cols, chunk_attn.shape[2]])
    rings.wait_for(w_qkv)
    rings.advance(per_window)
    group_cotangent = gather_group(after(cotangent[0], ring_gate_up.right))

    block_at = [rows * (2 * z_at + (c_at ^ dc)) for dc in range(2)]
    within = jnp.arange(rows, dtype=jnp.int32)
    base_block = 2 * (z_at - deep + 1)
    tables, first_rows, metas = [], [], []
    for dx in range(2):
        places = [block_at[dc] + within for dc in range(2)]
        firsts = [doc_first(start_rows[dx], places[dc]) for dc in range(2)]
        tables.append(rotary_tables(jnp.concatenate([p - f for p, f in zip(places, firsts)])))
        first_rows.append(jnp.stack(firsts)[:, None, :])
        cells = [
            [
                firsts[dc][0] // rows - base_block,
                block_at[dc] // rows - base_block,
                base_block * rows,
                firsts[dc][rows - 1],
                block_at[dc],
            ]
            for dc in range(2)
        ]
        metas.append(jnp.stack([jnp.stack(cell) for cell in cells]).astype(jnp.int32))

    heads = HEADS // GROUP
    normed, scales, queries, keyvals, attended, lses = ([None, None] for _ in range(6))
    for dx in (1, 0):
        group_inputs = group_tokens[dx].astype(F32)
        scales[dx] = lax.rsqrt(jnp.mean(group_inputs * group_inputs, axis=1, keepdims=True) + EPSILON)
        normed[dx] = (group_inputs * scales[dx] * gain_attn).astype(BF)
        pre = contract(w_qkv, normed[dx], 0, 1)
        turned = rotate(pre[:q_cols].reshape(heads, HD, -1), *tables[dx])
        queries[dx] = (turned * HD ** (-0.5)).astype(BF)
        key = rotate(pre[q_cols : q_cols + HD][None], *tables[dx])[0].astype(BF)
        keyval = jnp.concatenate([key, pre[q_cols + HD :].astype(BF)], axis=0).T
        keyval = jnp.concatenate(swap_pair(c_at, [keyval[:rows], keyval[rows:]]))
        earlier = [send(keyval, perm_of(along(step))) for step in range(deep - 1, 0, -1)]
        keyvals[dx] = jnp.concatenate(earlier + [keyval], axis=0)
    attended[1], lses[1] = attend_forward(metas[1], queries[1], keyvals[1], first_rows[1])
    rings.wait_for(attended[1])
    rings.advance(per_window)
    far = send_far(contract(attended[1].reshape(q_cols, -1), w_out_t, 0, 1).astype(BF))
    query_near = after(queries[0], attended[1])
    attended[0], lses[0] = attend_forward(metas[0], query_near, keyvals[0], first_rows[0])
    rings.wait_for(attended[0])
    rings.advance(per_window)
    near = reduce_core(contract(attended[0].reshape(q_cols, -1), w_out_t, 0, 1).astype(BF))
    middle = own_tokens.astype(F32) + near + far
    rings.wait_for(middle)
    rings.advance(half_ring)
    attended_t = [a.reshape(q_cols, -1) for a in attended]

    scale_mlp = lax.rsqrt(jnp.mean(middle * middle, axis=1, keepdims=True) + EPSILON)
    normed_mlp = gather_group((middle * scale_mlp * gain_mlp).astype(BF))
    (w_down_t,) = ring_down.whole([0, hidden_cols])
    (w_gate_up,) = ring_gate_up.whole([0, 2 * hidden_cols])
    hidden, d_gate_up = [None, None], [None, None]
    for dx in range(2):
        d_hidden = contract(group_cotangent[dx], w_down_t, 1, 0)
        gate_up = contract(normed_mlp[dx], w_gate_up, 1, 0)
        gate, up = gate_up[:, :hidden_cols], gate_up[:, hidden_cols:]
        sigmoid = jax.nn.sigmoid(gate)
        silu = gate * sigmoid
        hidden[dx] = (silu * up).astype(BF)
        d_gate = (d_hidden * up * sigmoid * (1.0 + gate * (1.0 - sigmoid))).astype(BF)
        d_up = (d_hidden * silu).astype(BF)
        d_gate_up[dx] = jnp.concatenate([d_gate, d_up], axis=1)
    both_hidden = jnp.concatenate(hidden)
    both_cotangent = jnp.concatenate(group_cotangent)
    ring_down = Scatter(contract(both_cotangent, both_hidden, 0, 0).astype(BF))
    ring_down.advance(per_window)
    far_part = contract(after(d_gate_up[1], ring_down.parts), w_gate_up, 1, 1).astype(BF)
    far = send_far(far_part)
    near = reduce_core(contract(after(d_gate_up[0], far_part), w_gate_up, 1, 1).astype(BF))
    ring_down.wait_for(near)
    ring_down.advance(per_window)
    both_normed = jnp.concatenate(normed_mlp)
    both_d_gate_up = jnp.concatenate([after(d_gate_up[0], near), d_gate_up[1]])
    ring_gate_up = Scatter(contract(both_normed, both_d_gate_up, 0, 0).astype(BF))
    rings = Rings([ring_down, ring_gate_up])
    ring_gate_up.advance(per_window)
    d_normed_mlp = near + far

    def norm_backward(values, scale_rows, gain, grads_in):
        weighted = grads_in * gain
        inner_mean = jnp.mean(weighted * values, axis=1, keepdims=True)
        cube = scale_rows * scale_rows * scale_rows
        return scale_rows * weighted - values * cube * inner_mean

    gain_grad_mlp = jnp.sum(d_normed_mlp * middle * scale_mlp, axis=0)
    d_middle = norm_backward(middle, scale_mlp, gain_mlp, d_normed_mlp) + cotangent[0].astype(F32)
    rings.wait_for(d_middle)
    rings.advance(per_window)

    d_branch = gather_group(d_middle.astype(BF))
    d_keyval, d_query = [None, None], [None, None]
    for dx in range(2):
        d_attended = contract(w_out_t, d_branch[dx], 0, 1).astype(BF).reshape(queries[dx].shape)
        if dx == 1:
            d_attended = after(d_attended, d_query[0])
        d_query[dx], d_keyvals = attend_backward(
            metas[dx], queries[dx], keyvals[dx], first_rows[dx], attended[dx], lses[dx], d_attended
        )
        rings.wait_for(d_query[dx])
        rings.advance(per_window)
        chunks = [d_keyvals[2 * rows * i : 2 * rows * (i + 1)] for i in range(deep)]
        total = chunks[deep - 1].astype(F32)
        for step in range(1, deep):
            total = total + send(chunks[deep - 1 - step], perm_of(along(-step))).astype(F32)
        d_keyval[dx] = jnp.concatenate(swap_pair(c_at, [total[:rows], total[rows:]])).T
    rings.advance(half_ring)
    grad_out_part = contract(d_branch[0], attended_t[0], 0, 1) + contract(
        after(d_branch[1], d_query[1]), attended_t[1], 0, 1
    )
    ring_out = Scatter(grad_out_part.astype(BF))
    ring_out.advance(half_ring)

    result_far = send_far(contract(after(hidden[1], d_query[1]), w_down_t, 1, 1).astype(BF))
    result_near = reduce_core(contract(after(hidden[0], d_query[1]), w_down_t, 1, 1).astype(BF))
    result = middle + result_near + result_far

    d_pre = [None, None]
    for dx in range(2):
        d_query_pre = unrotate(d_query[dx].astype(F32), *tables[dx]).astype(BF)
        d_key_pre = unrotate(d_keyval[dx][None, :HD], *tables[dx])[0].astype(BF)
        d_value_pre = d_keyval[dx][HD:].astype(BF)
        d_pre[dx] = jnp.concatenate([d_query_pre.reshape(q_cols, -1), d_key_pre, d_value_pre])
    near_part = contract(d_pre[0], w_qkv, 0, 1).astype(BF)
    far_part = contract(d_pre[1], w_qkv, 0, 1).astype(BF)
    far = send_far(far_part)
    near = reduce_core(near_part)
    grad_qkv_part = contract(normed[0], d_pre[0], 0, 1) + contract(
        normed[1], after(d_pre[1], far_part), 0, 1
    )
    ring_qkv = Scatter(grad_qkv_part.astype(BF))
    ring_qkv.advance(half_ring)
    gain_grad_attn = sum(
        jnp.sum(part.astype(F32) * group_tokens[dx].astype(F32) * scales[dx], axis=0)
        for dx, part in enumerate((near_part, far_part))
    )
    gain_grads = lax.dynamic_slice_in_dim(
        sum_small(jnp.stack([gain_grad_attn, gain_grad_mlp])), index * own_rows, own_rows, 1
    )
    grad_down = to_owners(ring_down)
    grad_gate_up = to_owners(ring_gate_up)
    grad_out = to_owners(ring_out)
    d_normed = near + far
    d_inputs = norm_backward(own_tokens.astype(F32), scales[0][:rows], gain_attn, d_normed) + d_middle
    grad_qkv = to_owners(ring_qkv)
    return (
        result.astype(BF)[None],
        d_inputs.astype(BF)[None],
        columns_of(grad_qkv[:, :, :q_cols]),
        columns_of(grad_qkv[:, :, q_cols : q_cols + HD]),
        columns_of(grad_qkv[:, :, q_cols + HD :]),
        columns_of(grad_out).T,
        columns_of(grad_gate_up[:, :, :hidden_cols]),
        columns_of(grad_gate_up[:, :, hidden_cols:]),
        columns_of(grad_down).T,
        gain_grads[0],
        gain_grads[1],
    )


def solution(mesh):
    token_spec = P("fsdp", "seq", None)
    row_spec = P(AXES, None)
    column_spec = P(None, AXES)
    gain_spec = P(AXES)
    return jax.shard_map(
        shards,
        mesh=mesh,
        in_specs=(
            token_spec,
            P("fsdp", None),
            row_spec,
            row_spec,
            row_spec,
            column_spec,
            row_spec,
            row_spec,
            column_spec,
            gain_spec,
            gain_spec,
            token_spec,
        ),
        out_specs=(
            token_spec,
            token_spec,
            row_spec,
            row_spec,
            row_spec,
            column_spec,
            row_spec,
            row_spec,
            column_spec,
            gain_spec,
            gain_spec,
        ),
        check_vma=False,
    )
```

```python
import functools

import jax
import jax.numpy as jnp
from jax import lax
from jax.experimental import pallas as pl
from jax.experimental.pallas import tpu as pltpu
from jax.sharding import PartitionSpec as P

HEADS = 32
KV = 4
HD = 64
EPSILON = 1e-05
ROPE_BASE = 10000.0
MASKED = -1e30
GROUP = 4
AXES = ("fsdp", "seq")
BF = jnp.bfloat16
F32 = jnp.float32


def contract(left, right, left_dim, right_dim):
    return lax.dot_general(
        left, right, (((left_dim,), (right_dim,)), ((), ())), preferred_element_type=F32
    )


def doc_first(start_row, places):
    inside = start_row[None, :] <= places[:, None]
    return jnp.max(jnp.where(inside, start_row[None, :], 0), axis=1)


def rotary_tables(offsets):
    half_dim = HD // 2
    frequency = ROPE_BASE ** (-(jnp.arange(half_dim, dtype=F32) / half_dim))
    angles = frequency[:, None] * offsets.astype(F32)[None, :]
    return (jnp.cos(angles), jnp.sin(angles))


def rotate(values, cos_table, sine_table):
    half_dim = HD // 2
    front_half = values[:, :half_dim]
    back_half = values[:, half_dim:]
    return jnp.concatenate(
        [
            front_half * cos_table - back_half * sine_table,
            back_half * cos_table + front_half * sine_table,
        ],
        axis=1,
    )


def unrotate(grads_in, cos_table, sine_table):
    return rotate(grads_in, cos_table, -sine_table)


def swap_pair(flag, pair):
    return [jnp.where(flag == 1, pair[1], pair[0]), jnp.where(flag == 1, pair[0], pair[1])]


def forward_kernel(
    meta, query_ref, keyval_ref, first_ref, out_ref, lse_ref, q_all, top, total, acc, *, rows, heads, pair
):
    cell = pl.program_id(0)
    lowest, highest, key_base, first_most, query_at = (meta[cell, i] for i in range(5))
    for head in range(heads):
        q_all[:, head * rows : (head + 1) * rows] = query_ref[head]
    top[...] = jnp.full_like(top, MASKED)
    total[...] = jnp.zeros_like(total)
    acc[...] = jnp.zeros_like(acc)
    width = pair * rows

    def visit(block, masked):
        start = pl.multiple_of(block * rows, rows)
        keyval = keyval_ref[pl.ds(start, rows), :]
        key = keyval[:, :HD]
        value_t = keyval[:, HD:].T
        if masked:
            key_at = key_base + start + lax.broadcasted_iota(jnp.int32, (rows, rows), 0)
            token_at = query_at + lax.broadcasted_iota(jnp.int32, (rows, rows), 1)
            allowed = (key_at <= token_at) & (key_at >= first_ref[0])
            bias = jnp.where(allowed, 0.0, MASKED)
            bias = jnp.concatenate([bias] * pair, axis=1)
        for piece in range(heads // pair):
            cols = slice(piece * width, (piece + 1) * width)
            score = contract(key, q_all[:, cols], 1, 0)
            if masked:
                score = score + bias
            before = top[:, cols]
            now = jnp.maximum(before, jnp.max(score, axis=0, keepdims=True))
            weight = jnp.exp(score - now)
            decay = jnp.exp(before - now)
            top[:, cols] = now
            total[:, cols] = total[:, cols] * decay + jnp.sum(weight, axis=0, keepdims=True)
            acc[:, cols] = acc[:, cols] * decay + contract(value_t, weight.astype(BF), 1, 0)

    def step(block, carry):
        plain = jnp.logical_and(key_base + block * rows >= first_most, block < highest)

        @pl.when(plain)
        def _():
            visit(block, False)

        @pl.when(jnp.logical_not(plain))
        def _():
            visit(block, True)

        return carry

    lax.fori_loop(lowest, highest + 1, step, 0)
    sums = total[...]
    scaled = acc[...] * (1.0 / sums)
    for head in range(heads):
        out_ref[head] = scaled[:, head * rows : (head + 1) * rows].astype(BF)
    lse_ref[0] = top[...] + jnp.log(sums)


def backward_kernel(
    meta,
    query_ref,
    keyval_ref,
    first_ref,
    out_ref,
    lse_ref,
    grad_ref,
    dquery_ref,
    dkeyval_ref,
    q_all,
    g_all,
    delta,
    dq_acc,
    dkv_acc,
    *,
    rows,
    heads,
    pair,
):
    cell = pl.program_id(0)
    lowest, highest, key_base, first_most, query_at = (meta[cell, i] for i in range(5))
    for head in range(heads):
        cols = slice(head * rows, (head + 1) * rows)
        q_all[:, cols] = query_ref[head]
        g_all[:, cols] = grad_ref[head]
        delta[:, cols] = jnp.sum(
            grad_ref[head].astype(F32) * out_ref[head].astype(F32), axis=0, keepdims=True
        )
    dq_acc[...] = jnp.zeros_like(dq_acc)

    @pl.when(cell == 0)
    def _():
        dkv_acc[...] = jnp.zeros_like(dkv_acc)

    width = pair * rows

    def visit(block, masked):
        start = pl.multiple_of(block * rows, rows)
        keyval = keyval_ref[pl.ds(start, rows), :]
        key = keyval[:, :HD]
        value = keyval[:, HD:]
        key_t = key.T
        if masked:
            key_at = key_base + start + lax.broadcasted_iota(jnp.int32, (rows, rows), 0)
            token_at = query_at + lax.broadcasted_iota(jnp.int32, (rows, rows), 1)
            allowed = (key_at <= token_at) & (key_at >= first_ref[0])
            bias = jnp.where(allowed, 0.0, MASKED)
            bias = jnp.concatenate([bias] * pair, axis=1)
        dkey = jnp.zeros((rows, HD), F32)
        dvalue = jnp.zeros((rows, HD), F32)
        for piece in range(heads // pair):
            cols = slice(piece * width, (piece + 1) * width)
            score = contract(key, q_all[:, cols], 1, 0)
            if masked:
                score = score + bias
            weight = jnp.exp(score - lse_ref[0, :, cols])
            dweight = contract(value, g_all[:, cols], 1, 0)
            dscore = (weight * (dweight - delta[:, cols])).astype(BF)
            dq_acc[:, cols] = dq_acc[:, cols] + contract(key_t, dscore, 1, 0)
            dkey = dkey + contract(dscore, q_all[:, cols], 1, 1)
            dvalue = dvalue + contract(weight.astype(BF), g_all[:, cols], 1, 1)
        dkv_acc[pl.ds(start, rows), :] = dkv_acc[pl.ds(start, rows), :] + jnp.concatenate(
            [dkey, dvalue], axis=1
        )

    def step(block, carry):
        plain = jnp.logical_and(key_base + block * rows >= first_most, block < highest)

        @pl.when(plain)
        def _():
            visit(block, False)

        @pl.when(jnp.logical_not(plain))
        def _():
            visit(block, True)

        return carry

    lax.fori_loop(lowest, highest + 1, step, 0)
    scaled = dq_acc[...] * HD ** (-0.5)
    for head in range(heads):
        dquery_ref[head] = scaled[:, head * rows : (head + 1) * rows].astype(BF)

    @pl.when(cell == 1)
    def _():
        dkeyval_ref[...] = dkv_acc[...].astype(BF)


def attention_specs(rows, heads, keys):
    return dict(
        head=pl.BlockSpec((heads, HD, rows), lambda cell, meta: (0, 0, cell)),
        keyval=pl.BlockSpec((keys, 2 * HD), lambda cell, meta: (0, 0)),
        first=pl.BlockSpec((1, 1, rows), lambda cell, meta: (cell, 0, 0)),
        stat=pl.BlockSpec((1, 1, heads * rows), lambda cell, meta: (cell, 0, 0)),
    )


def attend_forward(meta, query, keyval, first):
    heads, _, tokens = query.shape
    rows = tokens // 2
    keys = keyval.shape[0]
    specs = attention_specs(rows, heads, keys)
    wide = heads * rows
    return pl.pallas_call(
        functools.partial(forward_kernel, rows=rows, heads=heads, pair=2),
        grid_spec=pltpu.PrefetchScalarGridSpec(
            num_scalar_prefetch=1,
            grid=(2,),
            in_specs=[specs["head"], specs["keyval"], specs["first"]],
            out_specs=[specs["head"], specs["stat"]],
            scratch_shapes=[
                pltpu.VMEM((HD, wide), BF),
                pltpu.VMEM((1, wide), F32),
                pltpu.VMEM((1, wide), F32),
                pltpu.VMEM((HD, wide), F32),
            ],
        ),
        out_shape=(
            jax.ShapeDtypeStruct(query.shape, BF),
            jax.ShapeDtypeStruct((2, 1, wide), F32),
        ),
        compiler_params=pltpu.CompilerParams(
            dimension_semantics=("arbitrary",), vmem_limit_bytes=48 * 1024 * 1024
        ),
        cost_estimate=pl.CostEstimate(
            flops=40_000_000_000, bytes_accessed=10_000_000, transcendentals=0
        ),
        name="attend_forward",
    )(meta, query, keyval, first)


def attend_backward(meta, query, keyval, first, out, lse, grad):
    heads, _, tokens = query.shape
    rows = tokens // 2
    keys = keyval.shape[0]
    specs = attention_specs(rows, heads, keys)
    wide = heads * rows
    return pl.pallas_call(
        functools.partial(backward_kernel, rows=rows, heads=heads, pair=2),
        grid_spec=pltpu.PrefetchScalarGridSpec(
            num_scalar_prefetch=1,
            grid=(2,),
            in_specs=[
                specs["head"],
                specs["keyval"],
                specs["first"],
                specs["head"],
                specs["stat"],
                specs["head"],
            ],
            out_specs=[specs["head"], specs["keyval"]],
            scratch_shapes=[
                pltpu.VMEM((HD, wide), BF),
                pltpu.VMEM((HD, wide), BF),
                pltpu.VMEM((1, wide), F32),
                pltpu.VMEM((HD, wide), F32),
                pltpu.VMEM((keys, 2 * HD), F32),
            ],
        ),
        out_shape=(
            jax.ShapeDtypeStruct(query.shape, BF),
            jax.ShapeDtypeStruct(keyval.shape, BF),
        ),
        compiler_params=pltpu.CompilerParams(
            dimension_semantics=("arbitrary",), vmem_limit_bytes=48 * 1024 * 1024
        ),
        cost_estimate=pl.CostEstimate(
            flops=80_000_000_000, bytes_accessed=16_000_000, transcendentals=0
        ),
        name="attend_backward",
    )(meta, query, keyval, first, out, lse, grad)


def opening_kernel(
    tokens,
    quarters_attn,
    quarters_down,
    quarters_gate_up,
    group,
    whole_attn,
    whole_down,
    chunk_gate_up,
    local_sem,
    near_send,
    near_recv,
    swap_send,
    swap_recv,
    hop_send,
    hop_recv,
    *,
    wide,
    deep,
    own_rows,
):
    ring, half_ring = wide * deep, wide * deep // 2
    f_at, s_at = lax.axis_index("fsdp"), lax.axis_index("seq")
    y_at, x_at, z_at, c_at = f_at // 2, lax.rem(f_at, 2), s_at // 2, lax.rem(s_at, 2)
    here = y_at * deep + jnp.where(lax.rem(y_at, 2) == 0, z_at, deep - 1 - z_at)

    def ring_place(offset):
        index = lax.rem(here + offset + 2 * ring, ring)
        row, col = index // deep, lax.rem(index, deep)
        return row, jnp.where(lax.rem(row, 2) == 0, col, deep - 1 - col)

    def ring_device(offset):
        row, col = ring_place(offset)
        return row * 2 + x_at, col * 2 + c_at

    moves = ((0, 1), (1, 0), (1, 1))

    def other(dx, dc):
        return lax.rem(x_at + dx, 2), lax.rem(c_at + dc, 2)

    def group_device(dx, dc):
        x, c = other(dx, dc)
        return y_at * 2 + x, z_at * 2 + c

    def remote(source, target, send, recv, device):
        return pltpu.make_async_remote_copy(
            src_ref=source,
            dst_ref=target,
            send_sem=send,
            recv_sem=recv,
            device_id=device,
            device_id_type=pl.DeviceIdType.MESH,
        )

    barrier = pltpu.get_barrier_semaphore()
    partners = [group_device(*move) for move in moves] + [ring_device(1), ring_device(-1)]
    for device in partners:
        pl.semaphore_signal(barrier, inc=1, device_id=device, device_id_type=pl.DeviceIdType.MESH)
    pl.semaphore_wait(barrier, len(partners))

    my_rows = pl.ds(pl.multiple_of(c_at * own_rows, own_rows), own_rows)
    targets = (
        whole_attn.at[y_at, x_at, z_at, my_rows],
        whole_down.at[y_at, x_at, z_at, my_rows],
        chunk_gate_up.at[x_at, my_rows],
    )
    quarters = (quarters_attn, quarters_down, quarters_gate_up)
    locals_ = [
        pltpu.make_async_copy(quarters[i].at[x_at * 2 + c_at], targets[i], local_sem.at[i])
        for i in range(3)
    ] + [pltpu.make_async_copy(tokens, group.at[0], local_sem.at[3])]

    def swaps(i):
        copies = []
        for j, (dx, dc) in enumerate(moves):
            x, c = other(dx, dc)
            copies.append(
                remote(
                    quarters[i].at[x * 2 + c],
                    targets[i],
                    swap_send.at[i, j],
                    swap_recv.at[i, j],
                    group_device(dx, dc),
                )
            )
        return copies

    swap = [swaps(i) for i in range(3)]
    to_core = remote(tokens, group.at[1], near_send.at[0], near_recv.at[0], group_device(0, 1))
    to_x = remote(tokens, group.at[2], near_send.at[1], near_recv.at[1], group_device(1, 0))
    far_to_core = remote(
        group.at[2], group.at[3], near_send.at[2], near_recv.at[2], group_device(0, 1)
    )
    wholes = (whole_attn, whole_down)

    def hop(i, direction, step):
        row, col = ring_place(-direction * (step - 1))
        if step < half_ring:
            part = wholes[i].at[row, :, col]
        else:
            part = wholes[i].at[row, 0 if direction == 1 else 1, col]
        side = 0 if direction == 1 else 1
        return remote(
            part,
            part,
            hop_send.at[i, side, step - 1],
            hop_recv.at[i, side, step - 1],
            ring_device(direction),
        )

    hops = [
        [[hop(i, direction, step) for direction in (1, -1)] for step in range(1, half_ring + 1)]
        for i in range(2)
    ]

    for copy in locals_:
        copy.start()
    for copy in swap[0]:
        copy.start()
    for copy in swap[1]:
        copy.start()
    to_core.start()
    to_x.start()
    for copy in swap[2]:
        copy.start()
    for i in range(2):
        locals_[i].wait()
        for copy in swap[i]:
            copy.wait_recv()
    for i in range(2):
        for step in range(half_ring):
            if i == 0 or step > 0:
                for copy in hops[i][step]:
                    copy.start()
            if i == 0 and step == half_ring - 1:
                for copy in hops[1][0]:
                    copy.start()
            for copy in hops[i][step]:
                copy.wait_recv()
            if i == 0 and step == half_ring - 1:
                to_x.wait_recv()
                far_to_core.start()
    for copy in locals_[2:]:
        copy.wait()
    for copy in swap[2] + [to_core, far_to_core]:
        copy.wait_recv()
    for copy in swap[0] + swap[1] + swap[2] + [to_core, to_x, far_to_core]:
        copy.wait_send()
    for i in range(2):
        for pair in hops[i]:
            for copy in pair:
                copy.wait_send()


def opening(tokens, quarters_attn, quarters_down, quarters_gate_up, wide, deep):
    own_rows = quarters_attn.shape[1]
    half_ring = wide * deep // 2

    def whole(quarters):
        return jax.ShapeDtypeStruct((wide, 2, deep, 2 * own_rows, quarters.shape[2]), BF)

    anywhere = pl.BlockSpec(memory_space=pl.ANY)
    return pl.pallas_call(
        functools.partial(opening_kernel, wide=wide, deep=deep, own_rows=own_rows),
        out_shape=(
            jax.ShapeDtypeStruct((GROUP, *tokens.shape), BF),
            whole(quarters_attn),
            whole(quarters_down),
            jax.ShapeDtypeStruct((2, 2 * own_rows, quarters_gate_up.shape[2]), BF),
        ),
        in_specs=[anywhere] * 4,
        out_specs=(anywhere,) * 4,
        scratch_shapes=[
            pltpu.SemaphoreType.DMA((4,)),
            pltpu.SemaphoreType.DMA((3,)),
            pltpu.SemaphoreType.DMA((3,)),
            pltpu.SemaphoreType.DMA((3, 3)),
            pltpu.SemaphoreType.DMA((3, 3)),
            pltpu.SemaphoreType.DMA((2, 2, half_ring)),
            pltpu.SemaphoreType.DMA((2, 2, half_ring)),
        ],
        compiler_params=pltpu.CompilerParams(collective_id=0, has_side_effects=True),
        name="opening",
    )(tokens, quarters_attn, quarters_down, quarters_gate_up)


def shards(
    tokens,
    starts,
    w_query,
    w_key,
    w_value,
    w_out,
    w_gate,
    w_up,
    w_down,
    norm_attn,
    norm_mlp,
    cotangent,
):
    seq_count = lax.axis_size("seq")
    fsdp_count = lax.axis_size("fsdp")
    deep = seq_count // 2
    wide = fsdp_count // 2
    ring = wide * deep
    half_ring = ring // 2
    f_at, s_at = lax.axis_index("fsdp"), lax.axis_index("seq")
    x_at, y_at, c_at, z_at = f_at % 2, f_at // 2, s_at % 2, s_at // 2
    rows = tokens.shape[1]
    width = tokens.shape[2]
    own_rows = w_query.shape[0]

    def perm_of(move):
        found = []
        for f in range(fsdp_count):
            for s in range(seq_count):
                target = move(f // 2, f % 2, s // 2, s % 2)
                if target is not None:
                    ty, tx, tz, tc = target
                    found.append((f * seq_count + s, (ty * 2 + tx) * seq_count + tz * 2 + tc))
        return found

    def ring_place(position):
        position = position % ring
        row, col = position // deep, position % deep
        return row, col if row % 2 == 0 else deep - 1 - col

    def ring_index(y, z):
        return y * deep + (z if y % 2 == 0 else deep - 1 - z)

    def around(step):
        def move(y, x, z, c):
            ty, tz = ring_place(ring_index(y, z) + step)
            return ty, x, tz, c

        return move

    def along(step):
        return lambda y, x, z, c: (y, x, z + step, c) if 0 <= z + step < deep else None

    core_perm = perm_of(lambda y, x, z, c: (y, x, z, 1 - c))
    x_perm = perm_of(lambda y, x, z, c: (y, 1 - x, z, c))
    cross_perm = perm_of(lambda y, x, z, c: (y, 1 - x, z, 1 - c))
    right_perm, left_perm = perm_of(around(1)), perm_of(around(-1))

    def send(value, perm):
        return lax.ppermute(value, AXES, perm)

    position = y_at * deep + jnp.where(y_at % 2 == 0, z_at, deep - 1 - z_at)

    def place_at(offset):
        index = lax.rem(position + offset + 2 * ring, ring)
        row, col = index // deep, index % deep
        return row, jnp.where(row % 2 == 0, col, deep - 1 - col)

    def with_core(block):
        return jnp.concatenate([block, send(block, core_perm)], axis=0)

    def gather_group(block):
        return [with_core(block), with_core(send(block, x_perm))]

    def to_quarters(pieces):
        return jnp.concatenate(
            [p.reshape(own_rows, GROUP, -1).transpose(1, 0, 2) for p in pieces], axis=2
        )

    def absolute(got):
        rows_of = [swap_pair(c_at, pair) for pair in got]
        ordered = [swap_pair(x_at, [rows_of[0][c], rows_of[1][c]]) for c in range(2)]
        return [[ordered[0][x], ordered[1][x]] for x in range(2)]

    class Gather:
        def __init__(self, chunk):
            self.right = self.left = chunk
            self.step, self.got = 0, [(0, 0, chunk)]

        def advance(self, times):
            for _ in range(min(times, half_ring - self.step)):
                self.step += 1
                if self.step < half_ring:
                    self.right = send(self.right, right_perm)
                    self.left = send(self.left, left_perm)
                    self.got += [(-self.step, 0, self.right), (self.step, 0, self.left)]
                else:
                    self.got += [
                        (half_ring, 0, send(self.right[:1], right_perm)),
                        (half_ring, 1, send(self.left[1:], left_perm)),
                    ]

        def wait_for(self, value):
            self.right, self.left = after((self.right, self.left), value)

        def whole(self, cuts):
            results = []
            for low, high in zip(cuts[:-1], cuts[1:]):
                result = jnp.zeros((wide, 2, deep, 2 * own_rows, high - low), BF)
                for offset, x_from, piece in self.got:
                    row, col = place_at(offset)
                    result = lax.dynamic_update_slice(
                        result, piece[None, :, None, :, low:high], (row, x_from, col, 0, 0)
                    )
                results.append(result.reshape(-1, high - low))
            return results

    class Scatter:
        def __init__(self, partial):
            self.parts = partial.reshape(wide, 2, deep, 2 * own_rows, partial.shape[1])
            self.step, self.right, self.left = 0, None, None

        def part(self, offset, x_from=0, x_count=2):
            row, col = place_at(offset)
            return lax.dynamic_slice(
                self.parts,
                (row, x_from, col, 0, 0),
                (1, x_count, 1, 2 * own_rows, self.parts.shape[4]),
            ).reshape(x_count, 2 * own_rows, self.parts.shape[4])

        def advance(self, times):
            for _ in range(min(times, half_ring - self.step)):
                self.step += 1
                offset = half_ring - self.step + 1
                if self.step == 1:
                    to_right, to_left = self.part(offset, 0, 1), self.part(-offset, 1, 1)
                else:
                    to_right, to_left = self.joined(offset, -offset)
                self.right = send(to_right, right_perm)
                self.left = send(to_left, left_perm)

        def joined(self, at_right, at_left):
            to_right, to_left = self.part(at_right), self.part(at_left)
            if self.step == 2:
                to_right = jnp.concatenate([add_low(to_right[:1], self.right), to_right[1:]])
                to_left = jnp.concatenate([to_left[:1], add_low(to_left[1:], self.left)])
                return to_right, to_left
            return add_low(to_right, self.right), add_low(to_left, self.left)

        def wait_for(self, value):
            self.right, self.left = after((self.right, self.left), value)

        def result(self):
            self.advance(half_ring)
            own = self.part(0).astype(F32)
            if half_ring > 1:
                return own + self.right.astype(F32) + self.left.astype(F32)
            return own + jnp.concatenate([self.right, self.left]).astype(F32)

    def stage(moving, values):
        ends = [(member.right, member.left) for member in moving]
        ends, values = lax.optimization_barrier((ends, values))
        for member, (right, left) in zip(moving, ends):
            member.right, member.left = right, left
        return values

    def add_low(one, other):
        return (one.astype(F32) + other.astype(F32)).astype(BF)

    per_window = -(-half_ring // 4)

    def to_owners(scatter):
        chunk = scatter.result().astype(BF)
        blocks = [[chunk[x, c * own_rows : (c + 1) * own_rows] for c in range(2)] for x in range(2)]
        relative = absolute(blocks)
        got = [
            [relative[0][0], send(relative[0][1], core_perm)],
            [send(relative[1][0], x_perm), send(relative[1][1], cross_perm)],
        ]
        final = absolute(got)
        return jnp.stack([final[0][0], final[0][1], final[1][0], final[1][1]]).astype(F32)

    def columns_of(quarters):
        return quarters.transpose(1, 0, 2).reshape(own_rows, -1)

    def reduce_core(partial):
        return partial[:rows].astype(F32) + send(partial[rows:], core_perm).astype(F32)

    def send_far(partial):
        return send(reduce_core(partial).astype(BF), x_perm).astype(F32)

    index = f_at * seq_count + s_at
    count = fsdp_count * seq_count
    doublings = [
        (bit, [(i, i ^ (1 << bit)) for i in range(count)]) for bit in range(count.bit_length() - 1)
    ]

    def sum_small(value):
        for bit, perm in doublings:
            value = value + send(value, perm)
        return value

    def after(value, other):
        return lax.optimization_barrier((value, other))[0]

    q_cols = HEADS // GROUP * HD
    qkv_cols = q_cols + 2 * HD
    hidden_cols = w_gate.shape[1] // GROUP
    start_rows = [starts[0], send(starts, x_perm)[0]]
    gain_columns = jnp.pad(jnp.stack([norm_attn, norm_mlp], axis=1), ((0, 0), (0, 126)))
    own_tokens = tokens[0]
    group_blocks, whole_attn, whole_down, chunk_gate_up = opening(
        own_tokens,
        to_quarters([w_query, w_key, w_value, w_out.T, jnp.tile(gain_columns, (1, GROUP))]),
        to_quarters([w_down.T]),
        to_quarters([w_gate, w_up]),
        wide,
        deep,
    )
    group_tokens = [group_blocks[2 * dx : 2 * dx + 2].reshape(2 * rows, width) for dx in range(2)]
    whole_attn = whole_attn.reshape(width, -1)
    w_down_t = whole_down.reshape(width, -1)
    w_qkv = whole_attn[:, :qkv_cols]
    w_out_t = whole_attn[:, qkv_cols : qkv_cols + q_cols]
    gains = whole_attn[:, qkv_cols + q_cols :].T.astype(F32)
    gain_attn, gain_mlp = gains[0], gains[1]
    ring_gate_up = Gather(chunk_gate_up)
    rings = [ring_gate_up]

    def advance(members, times=per_window):
        for member in members:
            member.advance(times)

    advance(rings)
    group_cotangent = gather_group(cotangent[0])

    block_at = [rows * (2 * z_at + (c_at ^ dc)) for dc in range(2)]
    within = jnp.arange(rows, dtype=jnp.int32)
    base_block = 2 * (z_at - deep + 1)
    tables, first_rows, metas = [], [], []
    for dx in range(2):
        places = [block_at[dc] + within for dc in range(2)]
        firsts = [doc_first(start_rows[dx], places[dc]) for dc in range(2)]
        tables.append(rotary_tables(jnp.concatenate([p - f for p, f in zip(places, firsts)])))
        first_rows.append(jnp.stack(firsts)[:, None, :])
        cells = [
            [
                firsts[dc][0] // rows - base_block,
                block_at[dc] // rows - base_block,
                base_block * rows,
                firsts[dc][rows - 1],
                block_at[dc],
            ]
            for dc in range(2)
        ]
        metas.append(jnp.stack([jnp.stack(cell) for cell in cells]).astype(jnp.int32))

    heads = HEADS // GROUP
    normed, scales, queries, keyvals, attended, lses = ([None, None] for _ in range(6))
    for dx in (1, 0):
        group_inputs = group_tokens[dx].astype(F32)
        scales[dx] = lax.rsqrt(jnp.mean(group_inputs * group_inputs, axis=1, keepdims=True) + EPSILON)
        normed[dx] = (group_inputs * scales[dx] * gain_attn).astype(BF)
        pre = contract(w_qkv, normed[dx], 0, 1)
        turned = rotate(pre[:q_cols].reshape(heads, HD, -1), *tables[dx])
        queries[dx] = (turned * HD ** (-0.5)).astype(BF)
        key = rotate(pre[q_cols : q_cols + HD][None], *tables[dx])[0].astype(BF)
        keyval = jnp.concatenate([key, pre[q_cols + HD :].astype(BF)], axis=0).T
        keyval = jnp.concatenate(swap_pair(c_at, [keyval[:rows], keyval[rows:]]))
        earlier = [send(keyval, perm_of(along(step))) for step in range(deep - 1, 0, -1)]
        keyvals[dx] = jnp.concatenate(earlier + [keyval], axis=0)
    keyvals[1] = stage(rings, keyvals[1])
    advance(rings)
    attended[1], lses[1] = attend_forward(metas[1], queries[1], keyvals[1], first_rows[1])
    attended[1] = stage(rings, attended[1])
    advance(rings)
    far_sum = reduce_core(contract(attended[1].reshape(q_cols, -1), w_out_t, 0, 1).astype(BF)).astype(BF)
    far = send(far_sum, x_perm).astype(F32)
    query_near = after(queries[0], far_sum)
    attended[0], lses[0] = attend_forward(metas[0], query_near, keyvals[0], first_rows[0])
    attended[0], far = stage(rings, (attended[0], far))
    advance(rings, half_ring)
    near = reduce_core(contract(attended[0].reshape(q_cols, -1), w_out_t, 0, 1).astype(BF))
    middle = own_tokens.astype(F32) + near + far
    attended_t = [a.reshape(q_cols, -1) for a in attended]

    scale_mlp = lax.rsqrt(jnp.mean(middle * middle, axis=1, keepdims=True) + EPSILON)
    normed_mlp = gather_group((middle * scale_mlp * gain_mlp).astype(BF))
    (w_gate_up,) = ring_gate_up.whole([0, 2 * hidden_cols])
    hidden, d_gate_up = [None, None], [None, None]
    for dx in range(2):
        d_hidden = contract(group_cotangent[dx], w_down_t, 1, 0)
        gate_up = contract(normed_mlp[dx], w_gate_up, 1, 0)
        gate, up = gate_up[:, :hidden_cols], gate_up[:, hidden_cols:]
        sigmoid = jax.nn.sigmoid(gate)
        silu = gate * sigmoid
        hidden[dx] = (silu * up).astype(BF)
        d_gate = (d_hidden * up * sigmoid * (1.0 + gate * (1.0 - sigmoid))).astype(BF)
        d_up = (d_hidden * silu).astype(BF)
        d_gate_up[dx] = jnp.concatenate([d_gate, d_up], axis=1)
    both_hidden = jnp.concatenate(hidden)
    both_cotangent = jnp.concatenate(group_cotangent)
    both_normed = jnp.concatenate(normed_mlp)
    both_d_gate_up = jnp.concatenate(d_gate_up)
    ring_gate_up = Scatter(contract(both_normed, both_d_gate_up, 0, 0).astype(BF))
    ring_gate_up.advance(per_window)
    far_part = contract(after(d_gate_up[1], ring_gate_up.parts), w_gate_up, 1, 1).astype(BF)
    far = send_far(far_part)
    near_part = contract(after(d_gate_up[0], far_part), w_gate_up, 1, 1).astype(BF)
    near_part = stage([ring_gate_up], near_part)
    ring_gate_up.advance(per_window)
    near = reduce_core(near_part)
    ring_down = Scatter(contract(both_cotangent, after(both_hidden, near_part), 0, 0).astype(BF))
    ring_down.advance(per_window)
    d_normed_mlp = near + far

    def norm_backward(values, scale_rows, gain, grads_in):
        weighted = grads_in * gain
        inner_mean = jnp.mean(weighted * values, axis=1, keepdims=True)
        cube = scale_rows * scale_rows * scale_rows
        return scale_rows * weighted - values * cube * inner_mean

    gain_grad_mlp = jnp.sum(d_normed_mlp * middle * scale_mlp, axis=0)
    d_middle = norm_backward(middle, scale_mlp, gain_mlp, d_normed_mlp) + cotangent[0].astype(F32)
    rings = [ring_gate_up, ring_down]
    d_middle = stage(rings, d_middle)
    for member in rings:
        member.advance(per_window)

    d_branch = gather_group(d_middle.astype(BF))
    d_keyval, d_query, d_attended = [None, None], [None, None], [None, None]
    for dx in range(2):
        part = contract(w_out_t, d_branch[dx], 0, 1).astype(BF)
        d_attended[dx] = part.reshape(queries[dx].shape)

    def keyval_home(d_keyvals):
        chunks = [d_keyvals[2 * rows * i : 2 * rows * (i + 1)] for i in range(deep)]
        total = chunks[deep - 1].astype(F32)
        for step in range(1, deep):
            total = total + send(chunks[deep - 1 - step], perm_of(along(-step))).astype(F32)
        return jnp.concatenate(swap_pair(c_at, [total[:rows], total[rows:]])).T

    d_query[0], d_keyvals = attend_backward(
        metas[0], queries[0], keyvals[0], first_rows[0], attended[0], lses[0], d_attended[0]
    )
    d_query[0], d_keyvals = stage(rings, (d_query[0], d_keyvals))
    for member in rings:
        member.advance(per_window)
    d_keyval[0] = keyval_home(d_keyvals)
    result_part = contract(after(hidden[1], d_query[0]), w_down_t, 1, 1).astype(BF)
    result_far = send_far(result_part)
    d_attended[1] = after(d_attended[1], (d_query[0], result_part))
    d_query[1], d_keyvals = attend_backward(
        metas[1], queries[1], keyvals[1], first_rows[1], attended[1], lses[1], d_attended[1]
    )
    d_query[1], d_keyvals, d_keyval[0], result_far = stage(
        rings, (d_query[1], d_keyvals, d_keyval[0], result_far)
    )
    for member in rings:
        member.advance(half_ring)
    d_keyval[1] = keyval_home(d_keyvals)
    grad_out_part = contract(d_branch[0], attended_t[0], 0, 1) + contract(
        after(d_branch[1], d_query[1]), attended_t[1], 0, 1
    )
    ring_out = Scatter(grad_out_part.astype(BF))
    ring_out.advance(half_ring)
    result_near = reduce_core(contract(after(hidden[0], d_query[1]), w_down_t, 1, 1).astype(BF))
    result = middle + result_near + result_far

    d_pre = [None, None]
    for dx in range(2):
        d_query_pre = unrotate(d_query[dx].astype(F32), *tables[dx]).astype(BF)
        d_key_pre = unrotate(d_keyval[dx][None, :HD], *tables[dx])[0].astype(BF)
        d_value_pre = d_keyval[dx][HD:].astype(BF)
        d_pre[dx] = jnp.concatenate([d_query_pre.reshape(q_cols, -1), d_key_pre, d_value_pre])
    near_part = contract(d_pre[0], w_qkv, 0, 1).astype(BF)
    far_part = contract(d_pre[1], w_qkv, 0, 1).astype(BF)
    far = send_far(far_part)
    grad_qkv_part = contract(normed[0], d_pre[0], 0, 1) + contract(
        normed[1], after(d_pre[1], far_part), 0, 1
    )
    ring_qkv = Scatter(grad_qkv_part.astype(BF))
    ring_qkv.advance(half_ring - per_window)
    near = reduce_core(near_part)
    near, far = stage([ring_qkv], (near, far))
    ring_qkv.advance(half_ring)
    gain_grad_attn = sum(
        jnp.sum(part.astype(F32) * group_tokens[dx].astype(F32) * scales[dx], axis=0)
        for dx, part in enumerate((near_part, far_part))
    )
    gain_grads = lax.dynamic_slice_in_dim(
        sum_small(jnp.stack([gain_grad_attn, gain_grad_mlp])), index * own_rows, own_rows, 1
    )
    grad_down = to_owners(ring_down)
    grad_gate_up = to_owners(ring_gate_up)
    grad_out = to_owners(ring_out)
    d_normed = near + far
    d_inputs = norm_backward(own_tokens.astype(F32), scales[0][:rows], gain_attn, d_normed) + d_middle
    grad_qkv = to_owners(ring_qkv)
    return (
        result.astype(BF)[None],
        d_inputs.astype(BF)[None],
        columns_of(grad_qkv[:, :, :q_cols]),
        columns_of(grad_qkv[:, :, q_cols : q_cols + HD]),
        columns_of(grad_qkv[:, :, q_cols + HD :]),
        columns_of(grad_out).T,
        columns_of(grad_gate_up[:, :, :hidden_cols]),
        columns_of(grad_gate_up[:, :, hidden_cols:]),
        columns_of(grad_down).T,
        gain_grads[0],
        gain_grads[1],
    )


def solution(mesh):
    token_spec = P("fsdp", "seq", None)
    row_spec = P(AXES, None)
    column_spec = P(None, AXES)
    gain_spec = P(AXES)
    return jax.shard_map(
        shards,
        mesh=mesh,
        in_specs=(
            token_spec,
            P("fsdp", None),
            row_spec,
            row_spec,
            row_spec,
            column_spec,
            row_spec,
            row_spec,
            column_spec,
            gain_spec,
            gain_spec,
            token_spec,
        ),
        out_specs=(
            token_spec,
            token_spec,
            row_spec,
            row_spec,
            row_spec,
            column_spec,
            row_spec,
            row_spec,
            column_spec,
            gain_spec,
            gain_spec,
        ),
        check_vma=False,
    )
```

```python
import functools

import jax
import jax.numpy as jnp
from jax import lax
from jax.experimental import pallas as pl
from jax.experimental.pallas import tpu as pltpu
from jax.sharding import PartitionSpec as P

HEADS = 32
KV = 4
HD = 64
EPSILON = 1e-05
ROPE_BASE = 10000.0
MASKED = -1e30
GROUP = 4
AXES = ("fsdp", "seq")
BF = jnp.bfloat16
F32 = jnp.float32


def contract(left, right, left_dim, right_dim):
    return lax.dot_general(
        left, right, (((left_dim,), (right_dim,)), ((), ())), preferred_element_type=F32
    )


def doc_first(start_row, places):
    inside = start_row[None, :] <= places[:, None]
    return jnp.max(jnp.where(inside, start_row[None, :], 0), axis=1)


def rotary_tables(offsets):
    half_dim = HD // 2
    frequency = ROPE_BASE ** (-(jnp.arange(half_dim, dtype=F32) / half_dim))
    angles = frequency[:, None] * offsets.astype(F32)[None, :]
    return (jnp.cos(angles), jnp.sin(angles))


def rotate(values, cos_table, sine_table):
    half_dim = HD // 2
    front_half = values[:, :half_dim]
    back_half = values[:, half_dim:]
    return jnp.concatenate(
        [
            front_half * cos_table - back_half * sine_table,
            back_half * cos_table + front_half * sine_table,
        ],
        axis=1,
    )


def unrotate(grads_in, cos_table, sine_table):
    return rotate(grads_in, cos_table, -sine_table)


def swap_pair(flag, pair):
    return [jnp.where(flag == 1, pair[1], pair[0]), jnp.where(flag == 1, pair[0], pair[1])]


def forward_kernel(
    meta, query_ref, keyval_ref, first_ref, out_ref, lse_ref, q_all, top, total, acc, *, rows, heads, pair
):
    cell = pl.program_id(0)
    lowest, highest, key_base, first_most, query_at = (meta[cell, i] for i in range(5))
    for head in range(heads):
        q_all[:, head * rows : (head + 1) * rows] = query_ref[head]
    top[...] = jnp.full_like(top, MASKED)
    total[...] = jnp.zeros_like(total)
    acc[...] = jnp.zeros_like(acc)
    width = pair * rows

    def visit(block, masked):
        start = pl.multiple_of(block * rows, rows)
        keyval = keyval_ref[pl.ds(start, rows), :]
        key = keyval[:, :HD]
        value_t = keyval[:, HD:].T
        if masked:
            key_at = key_base + start + lax.broadcasted_iota(jnp.int32, (rows, rows), 0)
            token_at = query_at + lax.broadcasted_iota(jnp.int32, (rows, rows), 1)
            allowed = (key_at <= token_at) & (key_at >= first_ref[0])
            bias = jnp.where(allowed, 0.0, MASKED)
            bias = jnp.concatenate([bias] * pair, axis=1)
        for piece in range(heads // pair):
            cols = slice(piece * width, (piece + 1) * width)
            score = contract(key, q_all[:, cols], 1, 0)
            if masked:
                score = score + bias
            before = top[:, cols]
            now = jnp.maximum(before, jnp.max(score, axis=0, keepdims=True))
            weight = jnp.exp(score - now)
            decay = jnp.exp(before - now)
            top[:, cols] = now
            total[:, cols] = total[:, cols] * decay + jnp.sum(weight, axis=0, keepdims=True)
            acc[:, cols] = acc[:, cols] * decay + contract(value_t, weight.astype(BF), 1, 0)

    def step(block, carry):
        plain = jnp.logical_and(key_base + block * rows >= first_most, block < highest)

        @pl.when(plain)
        def _():
            visit(block, False)

        @pl.when(jnp.logical_not(plain))
        def _():
            visit(block, True)

        return carry

    lax.fori_loop(lowest, highest + 1, step, 0)
    sums = total[...]
    scaled = acc[...] * (1.0 / sums)
    for head in range(heads):
        out_ref[head] = scaled[:, head * rows : (head + 1) * rows].astype(BF)
    lse_ref[0] = top[...] + jnp.log(sums)


def backward_kernel(
    meta,
    query_ref,
    keyval_ref,
    first_ref,
    out_ref,
    lse_ref,
    grad_ref,
    dquery_ref,
    dkeyval_ref,
    q_all,
    g_all,
    delta,
    dq_acc,
    dkv_acc,
    *,
    rows,
    heads,
    pair,
):
    cell = pl.program_id(0)
    lowest, highest, key_base, first_most, query_at = (meta[cell, i] for i in range(5))
    for head in range(heads):
        cols = slice(head * rows, (head + 1) * rows)
        q_all[:, cols] = query_ref[head]
        g_all[:, cols] = grad_ref[head]
        delta[:, cols] = jnp.sum(
            grad_ref[head].astype(F32) * out_ref[head].astype(F32), axis=0, keepdims=True
        )
    dq_acc[...] = jnp.zeros_like(dq_acc)

    @pl.when(cell == 0)
    def _():
        dkv_acc[...] = jnp.zeros_like(dkv_acc)

    width = pair * rows

    def visit(block, masked):
        start = pl.multiple_of(block * rows, rows)
        keyval = keyval_ref[pl.ds(start, rows), :]
        key = keyval[:, :HD]
        value = keyval[:, HD:]
        key_t = key.T
        if masked:
            key_at = key_base + start + lax.broadcasted_iota(jnp.int32, (rows, rows), 0)
            token_at = query_at + lax.broadcasted_iota(jnp.int32, (rows, rows), 1)
            allowed = (key_at <= token_at) & (key_at >= first_ref[0])
            bias = jnp.where(allowed, 0.0, MASKED)
            bias = jnp.concatenate([bias] * pair, axis=1)
        dkey = jnp.zeros((rows, HD), F32)
        dvalue = jnp.zeros((rows, HD), F32)
        for piece in range(heads // pair):
            cols = slice(piece * width, (piece + 1) * width)
            score = contract(key, q_all[:, cols], 1, 0)
            if masked:
                score = score + bias
            weight = jnp.exp(score - lse_ref[0, :, cols])
            dweight = contract(value, g_all[:, cols], 1, 0)
            dscore = (weight * (dweight - delta[:, cols])).astype(BF)
            dq_acc[:, cols] = dq_acc[:, cols] + contract(key_t, dscore, 1, 0)
            dkey = dkey + contract(dscore, q_all[:, cols], 1, 1)
            dvalue = dvalue + contract(weight.astype(BF), g_all[:, cols], 1, 1)
        dkv_acc[pl.ds(start, rows), :] = dkv_acc[pl.ds(start, rows), :] + jnp.concatenate(
            [dkey, dvalue], axis=1
        )

    def step(block, carry):
        plain = jnp.logical_and(key_base + block * rows >= first_most, block < highest)

        @pl.when(plain)
        def _():
            visit(block, False)

        @pl.when(jnp.logical_not(plain))
        def _():
            visit(block, True)

        return carry

    lax.fori_loop(lowest, highest + 1, step, 0)
    scaled = dq_acc[...] * HD ** (-0.5)
    for head in range(heads):
        dquery_ref[head] = scaled[:, head * rows : (head + 1) * rows].astype(BF)

    @pl.when(cell == 1)
    def _():
        dkeyval_ref[...] = dkv_acc[...].astype(BF)


def attention_specs(rows, heads, keys):
    return dict(
        head=pl.BlockSpec((heads, HD, rows), lambda cell, meta: (0, 0, cell)),
        keyval=pl.BlockSpec((keys, 2 * HD), lambda cell, meta: (0, 0)),
        first=pl.BlockSpec((1, 1, rows), lambda cell, meta: (cell, 0, 0)),
        stat=pl.BlockSpec((1, 1, heads * rows), lambda cell, meta: (cell, 0, 0)),
    )


def attend_forward(meta, query, keyval, first):
    heads, _, tokens = query.shape
    rows = tokens // 2
    keys = keyval.shape[0]
    specs = attention_specs(rows, heads, keys)
    wide = heads * rows
    return pl.pallas_call(
        functools.partial(forward_kernel, rows=rows, heads=heads, pair=2),
        grid_spec=pltpu.PrefetchScalarGridSpec(
            num_scalar_prefetch=1,
            grid=(2,),
            in_specs=[specs["head"], specs["keyval"], specs["first"]],
            out_specs=[specs["head"], specs["stat"]],
            scratch_shapes=[
                pltpu.VMEM((HD, wide), BF),
                pltpu.VMEM((1, wide), F32),
                pltpu.VMEM((1, wide), F32),
                pltpu.VMEM((HD, wide), F32),
            ],
        ),
        out_shape=(
            jax.ShapeDtypeStruct(query.shape, BF),
            jax.ShapeDtypeStruct((2, 1, wide), F32),
        ),
        compiler_params=pltpu.CompilerParams(
            dimension_semantics=("arbitrary",), vmem_limit_bytes=48 * 1024 * 1024
        ),
        cost_estimate=pl.CostEstimate(
            flops=40_000_000_000, bytes_accessed=10_000_000, transcendentals=0
        ),
        name="attend_forward",
    )(meta, query, keyval, first)


def attend_backward(meta, query, keyval, first, out, lse, grad):
    heads, _, tokens = query.shape
    rows = tokens // 2
    keys = keyval.shape[0]
    specs = attention_specs(rows, heads, keys)
    wide = heads * rows
    return pl.pallas_call(
        functools.partial(backward_kernel, rows=rows, heads=heads, pair=2),
        grid_spec=pltpu.PrefetchScalarGridSpec(
            num_scalar_prefetch=1,
            grid=(2,),
            in_specs=[
                specs["head"],
                specs["keyval"],
                specs["first"],
                specs["head"],
                specs["stat"],
                specs["head"],
            ],
            out_specs=[specs["head"], specs["keyval"]],
            scratch_shapes=[
                pltpu.VMEM((HD, wide), BF),
                pltpu.VMEM((HD, wide), BF),
                pltpu.VMEM((1, wide), F32),
                pltpu.VMEM((HD, wide), F32),
                pltpu.VMEM((keys, 2 * HD), F32),
            ],
        ),
        out_shape=(
            jax.ShapeDtypeStruct(query.shape, BF),
            jax.ShapeDtypeStruct(keyval.shape, BF),
        ),
        compiler_params=pltpu.CompilerParams(
            dimension_semantics=("arbitrary",), vmem_limit_bytes=48 * 1024 * 1024
        ),
        cost_estimate=pl.CostEstimate(
            flops=80_000_000_000, bytes_accessed=16_000_000, transcendentals=0
        ),
        name="attend_backward",
    )(meta, query, keyval, first, out, lse, grad)


def feed_kernel(normed, cotangent, w_gate_up, w_down_t, *rest, columns):
    hidden, d_gate_up = rest[-2:]
    step = 256
    for low in range(0, columns, step):
        high = min(low + step, columns)
        gate = contract(normed[...], w_gate_up[:, low:high], 1, 0)
        up = contract(normed[...], w_gate_up[:, columns + low : columns + high], 1, 0)
        d_hidden = contract(cotangent[...], w_down_t[:, low:high], 1, 0)
        sigmoid = 1.0 / (1.0 + jnp.exp(-gate))
        silu = gate * sigmoid
        hidden[:, low:high] = (silu * up).astype(BF)
        d_gate_up[:, low:high] = (
            d_hidden * up * sigmoid * (1.0 + gate * (1.0 - sigmoid))
        ).astype(BF)
        d_gate_up[:, columns + low : columns + high] = (d_hidden * silu).astype(BF)


def feed_forward(normed, cotangent, w_gate_up, w_down_t, half, before=()):
    tokens, width = normed.shape
    columns = w_down_t.shape[1]
    tile = min(256, tokens)
    shift = half * (tokens // tile)
    token_spec = pl.BlockSpec((tile, width), lambda i: (i, 0))

    def weight_spec(wide):
        return pl.BlockSpec((width, wide), lambda i: (0, 0), pipeline_mode=pl.Buffered(1))

    def out_spec(wide):
        return pl.BlockSpec((tile, wide), lambda i: (i + shift, 0))

    return pl.pallas_call(
        functools.partial(feed_kernel, columns=columns),
        grid=(tokens // tile,),
        in_specs=[
            token_spec,
            token_spec,
            weight_spec(2 * columns),
            weight_spec(columns),
            *[pl.BlockSpec(memory_space=pl.ANY) for _ in before],
        ],
        out_specs=(out_spec(columns), out_spec(2 * columns)),
        out_shape=(
            jax.ShapeDtypeStruct((2 * tokens, columns), BF),
            jax.ShapeDtypeStruct((2 * tokens, 2 * columns), BF),
        ),
        input_output_aliases={4 + i: i for i in range(len(before))},
        compiler_params=pltpu.CompilerParams(
            dimension_semantics=("arbitrary",), vmem_limit_bytes=56 * 1024 * 1024
        ),
        cost_estimate=pl.CostEstimate(
            flops=6 * tokens * width * columns, bytes_accessed=6 * width * columns, transcendentals=0
        ),
        name="feed_forward",
    )(normed, cotangent, w_gate_up, w_down_t, *before)


def opening_kernel(
    tokens,
    quarters_attn,
    quarters_down,
    quarters_gate_up,
    group,
    whole_attn,
    whole_down,
    whole_gate_up,
    local_sem,
    near_send,
    near_recv,
    swap_send,
    swap_recv,
    hop_send,
    hop_recv,
    *,
    wide,
    deep,
    own_rows,
):
    ring, half_ring = wide * deep, wide * deep // 2
    f_at, s_at = lax.axis_index("fsdp"), lax.axis_index("seq")
    y_at, x_at, z_at, c_at = f_at // 2, lax.rem(f_at, 2), s_at // 2, lax.rem(s_at, 2)
    here = y_at * deep + jnp.where(lax.rem(y_at, 2) == 0, z_at, deep - 1 - z_at)

    def ring_place(offset):
        index = lax.rem(here + offset + 2 * ring, ring)
        row, col = index // deep, lax.rem(index, deep)
        return row, jnp.where(lax.rem(row, 2) == 0, col, deep - 1 - col)

    def ring_device(offset):
        row, col = ring_place(offset)
        return row * 2 + x_at, col * 2 + c_at

    moves = ((0, 1), (1, 0), (1, 1))

    def other(dx, dc):
        return lax.rem(x_at + dx, 2), lax.rem(c_at + dc, 2)

    def group_device(dx, dc):
        x, c = other(dx, dc)
        return y_at * 2 + x, z_at * 2 + c

    def remote(source, target, send, recv, device):
        return pltpu.make_async_remote_copy(
            src_ref=source,
            dst_ref=target,
            send_sem=send,
            recv_sem=recv,
            device_id=device,
            device_id_type=pl.DeviceIdType.MESH,
        )

    barrier = pltpu.get_barrier_semaphore()
    partners = [group_device(*move) for move in moves] + [ring_device(1), ring_device(-1)]
    for device in partners:
        pl.semaphore_signal(barrier, inc=1, device_id=device, device_id_type=pl.DeviceIdType.MESH)
    pl.semaphore_wait(barrier, len(partners))

    my_rows = pl.ds(pl.multiple_of(c_at * own_rows, own_rows), own_rows)
    targets = (
        whole_attn.at[y_at, x_at, z_at, my_rows],
        whole_down.at[y_at, x_at, z_at, my_rows],
        whole_gate_up.at[y_at, x_at, z_at, my_rows],
    )
    quarters = (quarters_attn, quarters_down, quarters_gate_up)
    locals_ = [
        pltpu.make_async_copy(quarters[i].at[x_at * 2 + c_at], targets[i], local_sem.at[i])
        for i in range(3)
    ] + [pltpu.make_async_copy(tokens, group.at[0], local_sem.at[3])]

    def swaps(i):
        copies = []
        for j, (dx, dc) in enumerate(moves):
            x, c = other(dx, dc)
            copies.append(
                remote(
                    quarters[i].at[x * 2 + c],
                    targets[i],
                    swap_send.at[i, j],
                    swap_recv.at[i, j],
                    group_device(dx, dc),
                )
            )
        return copies

    swap = [swaps(i) for i in range(3)]
    to_core = remote(tokens, group.at[1], near_send.at[0], near_recv.at[0], group_device(0, 1))
    to_x = remote(tokens, group.at[2], near_send.at[1], near_recv.at[1], group_device(1, 0))
    far_to_core = remote(
        group.at[2], group.at[3], near_send.at[2], near_recv.at[2], group_device(0, 1)
    )
    wholes = (whole_attn, whole_down)

    def hop(i, direction, step):
        row, col = ring_place(-direction * (step - 1))
        if step < half_ring:
            part = wholes[i].at[row, :, col]
        else:
            part = wholes[i].at[row, 0 if direction == 1 else 1, col]
        side = 0 if direction == 1 else 1
        return remote(
            part,
            part,
            hop_send.at[i, side, step - 1],
            hop_recv.at[i, side, step - 1],
            ring_device(direction),
        )

    hops = [
        [[hop(i, direction, step) for direction in (1, -1)] for step in range(1, half_ring + 1)]
        for i in range(2)
    ]

    for copy in locals_:
        copy.start()
    for copy in swap[0]:
        copy.start()
    for copy in swap[1]:
        copy.start()
    to_core.start()
    to_x.start()
    for copy in swap[2]:
        copy.start()
    for i in range(2):
        locals_[i].wait()
        for copy in swap[i]:
            copy.wait_recv()
    for i in range(2):
        for step in range(half_ring):
            if i == 0 or step > 0:
                for copy in hops[i][step]:
                    copy.start()
            if i == 0 and step == half_ring - 1:
                for copy in hops[1][0]:
                    copy.start()
            for copy in hops[i][step]:
                copy.wait_recv()
            if i == 0 and step == half_ring - 1:
                to_x.wait_recv()
                far_to_core.start()
    for copy in locals_[2:]:
        copy.wait()
    for copy in swap[2] + [to_core, far_to_core]:
        copy.wait_recv()
    for copy in swap[0] + swap[1] + swap[2] + [to_core, to_x, far_to_core]:
        copy.wait_send()
    for i in range(2):
        for pair in hops[i]:
            for copy in pair:
                copy.wait_send()


def opening(tokens, quarters_attn, quarters_down, quarters_gate_up, wide, deep):
    own_rows = quarters_attn.shape[1]
    half_ring = wide * deep // 2

    def whole(quarters):
        return jax.ShapeDtypeStruct((wide, 2, deep, 2 * own_rows, quarters.shape[2]), BF)

    anywhere = pl.BlockSpec(memory_space=pl.ANY)
    return pl.pallas_call(
        functools.partial(opening_kernel, wide=wide, deep=deep, own_rows=own_rows),
        out_shape=(
            jax.ShapeDtypeStruct((GROUP, *tokens.shape), BF),
            whole(quarters_attn),
            whole(quarters_down),
            whole(quarters_gate_up),
        ),
        in_specs=[anywhere] * 4,
        out_specs=(anywhere,) * 4,
        scratch_shapes=[
            pltpu.SemaphoreType.DMA((4,)),
            pltpu.SemaphoreType.DMA((3,)),
            pltpu.SemaphoreType.DMA((3,)),
            pltpu.SemaphoreType.DMA((3, 3)),
            pltpu.SemaphoreType.DMA((3, 3)),
            pltpu.SemaphoreType.DMA((2, 2, half_ring)),
            pltpu.SemaphoreType.DMA((2, 2, half_ring)),
        ],
        compiler_params=pltpu.CompilerParams(collective_id=0, has_side_effects=True),
        name="opening",
    )(tokens, quarters_attn, quarters_down, quarters_gate_up)


def closing_kernel(
    partial,
    near_part,
    far_part,
    chunk_gate_up,
    chunk_down,
    d_normed,
    owned_attn,
    owned_gate_up,
    owned_down,
    land,
    chunk_attn,
    core_land,
    x_stage,
    x_land,
    local_sem,
    near_send,
    near_recv,
    swap_send,
    swap_recv,
    hop_send,
    hop_recv,
    *,
    wide,
    deep,
    own_rows,
):
    ring, half_ring = wide * deep, wide * deep // 2
    f_at, s_at = lax.axis_index("fsdp"), lax.axis_index("seq")
    y_at, x_at, z_at, c_at = f_at // 2, lax.rem(f_at, 2), s_at // 2, lax.rem(s_at, 2)
    here = y_at * deep + jnp.where(lax.rem(y_at, 2) == 0, z_at, deep - 1 - z_at)

    def ring_place(offset):
        index = lax.rem(here + offset + 2 * ring, ring)
        row, col = index // deep, lax.rem(index, deep)
        return row, jnp.where(lax.rem(row, 2) == 0, col, deep - 1 - col)

    def ring_device(offset):
        row, col = ring_place(offset)
        return row * 2 + x_at, col * 2 + c_at

    moves = ((0, 1), (1, 0), (1, 1))

    def other(dx, dc):
        return lax.rem(x_at + dx, 2), lax.rem(c_at + dc, 2)

    def group_device(dx, dc):
        x, c = other(dx, dc)
        return y_at * 2 + x, z_at * 2 + c

    def remote(source, target, send, recv, device):
        return pltpu.make_async_remote_copy(
            src_ref=source,
            dst_ref=target,
            send_sem=send,
            recv_sem=recv,
            device_id=device,
            device_id_type=pl.DeviceIdType.MESH,
        )

    barrier = pltpu.get_barrier_semaphore()
    partners = [group_device(*move) for move in moves] + [ring_device(1), ring_device(-1)]
    for device in partners:
        pl.semaphore_signal(barrier, inc=1, device_id=device, device_id_type=pl.DeviceIdType.MESH)
    pl.semaphore_wait(barrier, len(partners))

    rows = x_land.shape[0]
    far_core = remote(
        far_part.at[rows:], core_land.at[0], near_send.at[0], near_recv.at[0], group_device(0, 1)
    )
    near_core = remote(
        near_part.at[rows:], core_land.at[1], near_send.at[1], near_recv.at[1], group_device(0, 1)
    )
    far_x = remote(x_stage, x_land, near_send.at[2], near_recv.at[2], group_device(1, 0))

    def hop(side, step):
        direction = 1 - 2 * side
        if step == 1:
            row, col = ring_place(direction * half_ring)
            source, target = partial.at[row, side, col], land.at[side, 0, side]
        else:
            source, target = land.at[side, step - 2], land.at[side, step - 1]
        return remote(
            source,
            target,
            hop_send.at[side, step - 1],
            hop_recv.at[side, step - 1],
            ring_device(direction),
        )

    chunks = (chunk_attn, chunk_gate_up, chunk_down)
    owned = (owned_attn, owned_gate_up, owned_down)

    def piece(i, x, c):
        return chunks[i].at[x, pl.ds(pl.multiple_of(c * own_rows, own_rows), own_rows)]

    def swaps(i):
        copies = []
        for j, (dx, dc) in enumerate(moves):
            copies.append(
                remote(
                    piece(i, *other(dx, dc)),
                    owned[i].at[x_at * 2 + c_at],
                    swap_send.at[i, j],
                    swap_recv.at[i, j],
                    group_device(dx, dc),
                )
            )
        return copies

    swap = [swaps(i) for i in range(3)]
    keep = [
        pltpu.make_async_copy(piece(i, x_at, c_at), owned[i].at[x_at * 2 + c_at], local_sem.at[i])
        for i in range(3)
    ]

    far_core.start()
    near_core.start()
    for side in range(2):
        hop(side, 1).start()
    far_core.wait_recv()
    x_stage[...] = (far_part[:rows].astype(F32) + core_land[0].astype(F32)).astype(BF)
    far_x.start()
    for i in (1, 2):
        for copy in swap[i]:
            copy.start()
        keep[i].start()
    for step in range(2, half_ring + 1):
        for side in range(2):
            hop(side, step - 1).wait_recv()
            row, col = ring_place((1 - 2 * side) * (half_ring - step + 1))
            if step == 2:
                mine = partial[row, side, col].astype(F32) + land[side, 0, side].astype(F32)
                land[side, 0, side] = mine.astype(BF)
                land[side, 0, 1 - side] = partial[row, 1 - side, col]
            else:
                for half in range(2):
                    mine = partial[row, half, col].astype(F32)
                    mine = mine + land[side, step - 2, half].astype(F32)
                    land[side, step - 2, half] = mine.astype(BF)
            hop(side, step).start()
    near_core.wait_recv()
    for side in range(2):
        hop(side, half_ring).wait_recv()
    for half in range(2):
        total = partial[y_at, half, z_at].astype(F32) + land[0, half_ring - 1, half].astype(F32)
        total = total + land[1, half_ring - 1, half].astype(F32)
        chunk_attn[half] = total.astype(BF)
    for copy in swap[0]:
        copy.start()
    keep[0].start()
    far_x.wait_recv()
    d_normed[...] = (
        near_part[:rows].astype(F32) + core_land[1].astype(F32) + x_land[...].astype(F32)
    )
    for i in (1, 2, 0):
        keep[i].wait()
        for copy in swap[i]:
            copy.wait_recv()
    for copy in swap[0] + swap[1] + swap[2] + [far_core, near_core, far_x]:
        copy.wait_send()
    for side in range(2):
        for step in range(1, half_ring + 1):
            hop(side, step).wait_send()


def closing(partial, near_part, far_part, chunk_gate_up, chunk_down, wide, deep):
    own_rows = partial.shape[3] // 2
    half_ring = wide * deep // 2
    rows, width = near_part.shape[0] // 2, near_part.shape[1]
    columns = partial.shape[4]
    anywhere = pl.BlockSpec(memory_space=pl.ANY)
    vmem = pl.BlockSpec(memory_space=pltpu.VMEM)

    def quarters(wanted):
        return jax.ShapeDtypeStruct((GROUP, own_rows, wanted), BF)

    return pl.pallas_call(
        functools.partial(closing_kernel, wide=wide, deep=deep, own_rows=own_rows),
        out_shape=(
            jax.ShapeDtypeStruct((rows, width), F32),
            quarters(columns),
            quarters(chunk_gate_up.shape[2]),
            quarters(chunk_down.shape[2]),
        ),
        in_specs=[vmem, vmem, vmem, anywhere, anywhere],
        out_specs=(vmem, anywhere, anywhere, anywhere),
        scratch_shapes=[
            pltpu.VMEM((2, half_ring, 2, 2 * own_rows, columns), BF),
            pltpu.VMEM((2, 2 * own_rows, columns), BF),
            pltpu.VMEM((2, rows, width), BF),
            pltpu.VMEM((rows, width), BF),
            pltpu.VMEM((rows, width), BF),
            pltpu.SemaphoreType.DMA((3,)),
            pltpu.SemaphoreType.DMA((3,)),
            pltpu.SemaphoreType.DMA((3,)),
            pltpu.SemaphoreType.DMA((3, 3)),
            pltpu.SemaphoreType.DMA((3, 3)),
            pltpu.SemaphoreType.DMA((2, half_ring)),
            pltpu.SemaphoreType.DMA((2, half_ring)),
        ],
        compiler_params=pltpu.CompilerParams(
            collective_id=1, has_side_effects=True, vmem_limit_bytes=56 * 1024 * 1024
        ),
        name="closing",
    )(partial, near_part, far_part, chunk_gate_up, chunk_down)


def shards(
    tokens,
    starts,
    w_query,
    w_key,
    w_value,
    w_out,
    w_gate,
    w_up,
    w_down,
    norm_attn,
    norm_mlp,
    cotangent,
):
    seq_count = lax.axis_size("seq")
    fsdp_count = lax.axis_size("fsdp")
    deep = seq_count // 2
    wide = fsdp_count // 2
    ring = wide * deep
    half_ring = ring // 2
    f_at, s_at = lax.axis_index("fsdp"), lax.axis_index("seq")
    x_at, y_at, c_at, z_at = f_at % 2, f_at // 2, s_at % 2, s_at // 2
    rows = tokens.shape[1]
    width = tokens.shape[2]
    own_rows = w_query.shape[0]

    def perm_of(move):
        found = []
        for f in range(fsdp_count):
            for s in range(seq_count):
                target = move(f // 2, f % 2, s // 2, s % 2)
                if target is not None:
                    ty, tx, tz, tc = target
                    found.append((f * seq_count + s, (ty * 2 + tx) * seq_count + tz * 2 + tc))
        return found

    def ring_place(position):
        position = position % ring
        row, col = position // deep, position % deep
        return row, col if row % 2 == 0 else deep - 1 - col

    def ring_index(y, z):
        return y * deep + (z if y % 2 == 0 else deep - 1 - z)

    def around(step):
        def move(y, x, z, c):
            ty, tz = ring_place(ring_index(y, z) + step)
            return ty, x, tz, c

        return move

    def along(step):
        return lambda y, x, z, c: (y, x, z + step, c) if 0 <= z + step < deep else None

    core_perm = perm_of(lambda y, x, z, c: (y, x, z, 1 - c))
    x_perm = perm_of(lambda y, x, z, c: (y, 1 - x, z, c))
    cross_perm = perm_of(lambda y, x, z, c: (y, 1 - x, z, 1 - c))
    right_perm, left_perm = perm_of(around(1)), perm_of(around(-1))

    def send(value, perm):
        return lax.ppermute(value, AXES, perm)

    position = y_at * deep + jnp.where(y_at % 2 == 0, z_at, deep - 1 - z_at)

    def place_at(offset):
        index = lax.rem(position + offset + 2 * ring, ring)
        row, col = index // deep, index % deep
        return row, jnp.where(row % 2 == 0, col, deep - 1 - col)

    def with_core(block):
        return jnp.concatenate([block, send(block, core_perm)], axis=0)

    def gather_group(block):
        return [with_core(block), with_core(send(block, x_perm))]

    def to_quarters(pieces):
        return jnp.concatenate(
            [p.reshape(own_rows, GROUP, -1).transpose(1, 0, 2) for p in pieces], axis=2
        )

    def absolute(got):
        rows_of = [swap_pair(c_at, pair) for pair in got]
        ordered = [swap_pair(x_at, [rows_of[0][c], rows_of[1][c]]) for c in range(2)]
        return [[ordered[0][x], ordered[1][x]] for x in range(2)]

    class Gather:
        def __init__(self, room):
            self.room = room
            row, col = place_at(0)
            size = (1, 2, 1, *room.shape[3:])
            chunk = lax.dynamic_slice(room, (row, 0, col, 0, 0), size).reshape(2, *room.shape[3:])
            self.right = self.left = chunk
            self.step, self.got = 0, []

        def advance(self, times):
            for _ in range(min(times, half_ring - self.step)):
                self.step += 1
                if self.step < half_ring:
                    self.right = send(self.right, right_perm)
                    self.left = send(self.left, left_perm)
                    self.got += [(-self.step, 0, self.right), (self.step, 0, self.left)]
                else:
                    self.got += [
                        (half_ring, 0, send(self.right[:1], right_perm)),
                        (half_ring, 1, send(self.left[1:], left_perm)),
                    ]

        def wait_for(self, value):
            self.right, self.left = after((self.right, self.left), value)

        def whole(self):
            result = self.room
            for offset, x_from, piece in self.got:
                row, col = place_at(offset)
                result = lax.dynamic_update_slice(
                    result, piece[None, :, None], (row, x_from, col, 0, 0)
                )
            return result.reshape(-1, result.shape[4])

    class Scatter:
        def __init__(self, partial):
            self.parts = partial.reshape(wide, 2, deep, 2 * own_rows, partial.shape[1])
            self.step, self.right, self.left = 0, None, None

        def part(self, offset, x_from=0, x_count=2):
            row, col = place_at(offset)
            return lax.dynamic_slice(
                self.parts,
                (row, x_from, col, 0, 0),
                (1, x_count, 1, 2 * own_rows, self.parts.shape[4]),
            ).reshape(x_count, 2 * own_rows, self.parts.shape[4])

        def advance(self, times):
            for _ in range(min(times, half_ring - self.step)):
                self.step += 1
                offset = half_ring - self.step + 1
                if self.step == 1:
                    to_right, to_left = self.part(offset, 0, 1), self.part(-offset, 1, 1)
                else:
                    to_right, to_left = self.joined(offset, -offset)
                self.right = send(to_right, right_perm)
                self.left = send(to_left, left_perm)

        def joined(self, at_right, at_left):
            to_right, to_left = self.part(at_right), self.part(at_left)
            if self.step == 2:
                to_right = jnp.concatenate([add_low(to_right[:1], self.right), to_right[1:]])
                to_left = jnp.concatenate([to_left[:1], add_low(to_left[1:], self.left)])
                return to_right, to_left
            return add_low(to_right, self.right), add_low(to_left, self.left)

        def wait_for(self, value):
            self.right, self.left = after((self.right, self.left), value)

        def result(self):
            self.advance(half_ring)
            own = self.part(0).astype(F32)
            if half_ring > 1:
                return own + self.right.astype(F32) + self.left.astype(F32)
            return own + jnp.concatenate([self.right, self.left]).astype(F32)

    def stage(moving, values):
        ends = [(member.right, member.left) for member in moving]
        ends, values = lax.optimization_barrier((ends, values))
        for member, (right, left) in zip(moving, ends):
            member.right, member.left = right, left
        return values

    def add_low(one, other):
        return (one.astype(F32) + other.astype(F32)).astype(BF)

    per_window = -(-half_ring // 4)

    def columns_of(quarters):
        return quarters.transpose(1, 0, 2).reshape(own_rows, -1)

    def reduce_core(partial):
        return partial[:rows].astype(F32) + send(partial[rows:], core_perm).astype(F32)

    def send_far(partial):
        return send(reduce_core(partial).astype(BF), x_perm).astype(F32)

    index = f_at * seq_count + s_at
    count = fsdp_count * seq_count
    doublings = [
        (bit, [(i, i ^ (1 << bit)) for i in range(count)]) for bit in range(count.bit_length() - 1)
    ]

    def sum_small(value):
        for bit, perm in doublings:
            value = value + send(value, perm)
        return value

    def after(value, other):
        return lax.optimization_barrier((value, other))[0]

    q_cols = HEADS // GROUP * HD
    qkv_cols = q_cols + 2 * HD
    hidden_cols = w_gate.shape[1] // GROUP
    start_rows = [starts[0], send(starts, x_perm)[0]]
    block_at = [rows * (2 * z_at + (c_at ^ dc)) for dc in range(2)]
    within = jnp.arange(rows, dtype=jnp.int32)
    base_block = 2 * (z_at - deep + 1)
    tables, first_rows, metas = [], [], []
    for dx in range(2):
        places = [block_at[dc] + within for dc in range(2)]
        firsts = [doc_first(start_rows[dx], places[dc]) for dc in range(2)]
        tables.append(rotary_tables(jnp.concatenate([p - f for p, f in zip(places, firsts)])))
        first_rows.append(jnp.stack(firsts)[:, None, :])
        cells = [
            [
                firsts[dc][0] // rows - base_block,
                block_at[dc] // rows - base_block,
                base_block * rows,
                firsts[dc][rows - 1],
                block_at[dc],
            ]
            for dc in range(2)
        ]
        metas.append(jnp.stack([jnp.stack(cell) for cell in cells]).astype(jnp.int32))

    gain_columns = jnp.pad(jnp.stack([norm_attn, norm_mlp], axis=1), ((0, 0), (0, 126)))
    own_tokens, tables, first_rows, metas = after((tokens[0], tables, first_rows, metas), start_rows[1])
    own_tokens = after(own_tokens, (tables, first_rows, metas))
    group_blocks, whole_attn, whole_down, whole_gate_up = opening(
        own_tokens,
        to_quarters([w_query, w_key, w_value, w_out.T, jnp.tile(gain_columns, (1, GROUP))]),
        to_quarters([w_down.T]),
        to_quarters([w_gate, w_up]),
        wide,
        deep,
    )
    group_tokens = [group_blocks[2 * dx : 2 * dx + 2].reshape(2 * rows, width) for dx in range(2)]
    whole_attn = whole_attn.reshape(width, -1)
    w_down_t = whole_down.reshape(width, -1)
    w_qkv = whole_attn[:, :qkv_cols]
    w_out_t = whole_attn[:, qkv_cols : qkv_cols + q_cols]
    gains = whole_attn[:, qkv_cols + q_cols :].T.astype(F32)
    gain_attn, gain_mlp = gains[0], gains[1]
    ring_gate_up = Gather(whole_gate_up)
    rings = [ring_gate_up]

    def advance(members, times=per_window):
        for member in members:
            member.advance(times)

    advance(rings)
    group_cotangent = gather_group(after(cotangent[0], group_blocks))

    heads = HEADS // GROUP
    normed, scales, queries, keyvals, attended, lses = ([None, None] for _ in range(6))
    for dx in (1, 0):
        group_inputs = group_tokens[dx].astype(F32)
        scales[dx] = lax.rsqrt(jnp.mean(group_inputs * group_inputs, axis=1, keepdims=True) + EPSILON)
        normed[dx] = (group_inputs * scales[dx] * gain_attn).astype(BF)
        pre = contract(w_qkv, normed[dx], 0, 1)
        turned = rotate(pre[:q_cols].reshape(heads, HD, -1), *tables[dx])
        queries[dx] = (turned * HD ** (-0.5)).astype(BF)
        key = rotate(pre[q_cols : q_cols + HD][None], *tables[dx])[0].astype(BF)
        keyval = jnp.concatenate([key, pre[q_cols + HD :].astype(BF)], axis=0).T
        keyval = jnp.concatenate(swap_pair(c_at, [keyval[:rows], keyval[rows:]]))
        earlier = [send(keyval, perm_of(along(step))) for step in range(deep - 1, 0, -1)]
        keyvals[dx] = jnp.concatenate(earlier + [keyval], axis=0)
    keyvals[1] = stage(rings, keyvals[1])
    advance(rings)
    attended[1], lses[1] = attend_forward(metas[1], queries[1], keyvals[1], first_rows[1])
    attended[1] = stage(rings, attended[1])
    advance(rings)
    far_sum = reduce_core(contract(attended[1].reshape(q_cols, -1), w_out_t, 0, 1).astype(BF)).astype(BF)
    far = send(far_sum, x_perm).astype(F32)
    query_near = after(queries[0], far_sum)
    attended[0], lses[0] = attend_forward(metas[0], query_near, keyvals[0], first_rows[0])
    attended[0], far = stage(rings, (attended[0], far))
    advance(rings, half_ring)
    near = reduce_core(contract(attended[0].reshape(q_cols, -1), w_out_t, 0, 1).astype(BF))
    middle = own_tokens.astype(F32) + near + far
    attended_t = [a.reshape(q_cols, -1) for a in attended]

    scale_mlp = lax.rsqrt(jnp.mean(middle * middle, axis=1, keepdims=True) + EPSILON)
    normed_own = (middle * scale_mlp * gain_mlp).astype(BF)
    normed_far = send(normed_own, x_perm)
    normed_mlp = [with_core(normed_own), None]
    w_gate_up = ring_gate_up.whole()
    both = feed_forward(normed_mlp[0], group_cotangent[0], w_gate_up, w_down_t, 0)
    normed_far, both = stage([], (normed_far, both))
    normed_mlp[1] = with_core(normed_far)
    both = feed_forward(normed_mlp[1], group_cotangent[1], w_gate_up, w_down_t, 1, both)
    both_hidden, both_d_gate_up = both
    hidden = [both_hidden[: 2 * rows], both_hidden[2 * rows :]]
    d_gate_up = [both_d_gate_up[: 2 * rows], both_d_gate_up[2 * rows :]]
    both_cotangent = jnp.concatenate(group_cotangent)
    both_normed = jnp.concatenate(normed_mlp)
    far_part = contract(d_gate_up[1], w_gate_up, 1, 1).astype(BF)
    far_sum = reduce_core(far_part).astype(BF)
    far = send(far_sum, x_perm)
    near_part = contract(after(d_gate_up[0], far_part), w_gate_up, 1, 1).astype(BF)
    near = reduce_core(near_part)
    both_hidden = after(both_hidden, (near_part, far_sum))
    ring_down = Scatter(contract(both_cotangent, both_hidden, 0, 0).astype(BF))
    ring_down.advance(per_window)
    both_d_gate_up = after(both_d_gate_up, ring_down.parts)
    ring_gate_up = Scatter(contract(both_normed, both_d_gate_up, 0, 0).astype(BF))
    far, ring_gate_up.parts = stage([ring_down], (far, ring_gate_up.parts))
    far = far.astype(F32)
    ring_gate_up.advance(per_window)
    d_normed_mlp = near + far

    def norm_backward(values, scale_rows, gain, grads_in):
        weighted = grads_in * gain
        inner_mean = jnp.mean(weighted * values, axis=1, keepdims=True)
        cube = scale_rows * scale_rows * scale_rows
        return scale_rows * weighted - values * cube * inner_mean

    gain_grad_mlp = jnp.sum(d_normed_mlp * middle * scale_mlp, axis=0)
    d_middle = norm_backward(middle, scale_mlp, gain_mlp, d_normed_mlp) + cotangent[0].astype(F32)
    rings = [ring_gate_up, ring_down]

    branch_own = d_middle.astype(BF)
    branch_far = send(branch_own, x_perm)
    d_branch = [with_core(branch_own), None]
    d_keyval, d_query = [None, None], [None, None]

    def d_attended(dx):
        return contract(w_out_t, d_branch[dx], 0, 1).astype(BF).reshape(queries[dx].shape)

    def keyval_home(d_keyvals):
        chunks = [d_keyvals[2 * rows * i : 2 * rows * (i + 1)] for i in range(deep)]
        total = chunks[deep - 1].astype(F32)
        for step in range(1, deep):
            total = total + send(chunks[deep - 1 - step], perm_of(along(-step))).astype(F32)
        return jnp.concatenate(swap_pair(c_at, [total[:rows], total[rows:]])).T

    d_near = stage([ring_gate_up], d_attended(0))
    advance(rings)
    d_query[0], d_keyvals = attend_backward(
        metas[0], queries[0], keyvals[0], first_rows[0], attended[0], lses[0], d_near
    )
    d_query[0], d_keyvals, branch_far = stage(rings, (d_query[0], d_keyvals, branch_far))
    advance(rings)
    d_keyval[0] = keyval_home(d_keyvals)
    d_branch[1] = with_core(branch_far)
    result_part = contract(after(hidden[1], d_query[0]), w_down_t, 1, 1).astype(BF)
    result_sum = reduce_core(result_part).astype(BF)
    result_far = send(result_sum, x_perm).astype(F32)
    d_far = after(d_attended(1), (d_query[0], result_sum))
    d_query[1], d_keyvals = attend_backward(
        metas[1], queries[1], keyvals[1], first_rows[1], attended[1], lses[1], d_far
    )
    d_query[1], d_keyvals, d_keyval[0], result_far = stage(
        rings, (d_query[1], d_keyvals, d_keyval[0], result_far)
    )
    for member in rings:
        member.advance(half_ring)
    d_keyval[1] = keyval_home(d_keyvals)
    grad_out_part = contract(d_branch[0], attended_t[0], 0, 1) + contract(
        after(d_branch[1], d_query[1]), attended_t[1], 0, 1
    )
    result_near = reduce_core(contract(after(hidden[0], d_query[1]), w_down_t, 1, 1).astype(BF))
    result = middle + result_near + result_far

    d_pre = [None, None]
    for dx in range(2):
        d_query_pre = unrotate(d_query[dx].astype(F32), *tables[dx]).astype(BF)
        d_key_pre = unrotate(d_keyval[dx][None, :HD], *tables[dx])[0].astype(BF)
        d_value_pre = d_keyval[dx][HD:].astype(BF)
        d_pre[dx] = jnp.concatenate([d_query_pre.reshape(q_cols, -1), d_key_pre, d_value_pre])
    near_part = contract(d_pre[0], w_qkv, 0, 1).astype(BF)
    far_part = contract(d_pre[1], w_qkv, 0, 1).astype(BF)
    grad_qkv_part = contract(normed[0], d_pre[0], 0, 1) + contract(normed[1], d_pre[1], 0, 1)
    gain_grad_attn = sum(
        jnp.sum(part.astype(F32) * group_tokens[dx].astype(F32) * scales[dx], axis=0)
        for dx, part in enumerate((near_part, far_part))
    )
    gain_partial = jnp.pad(jnp.stack([gain_grad_attn, gain_grad_mlp], axis=1), ((0, 0), (0, 126)))
    partial = jnp.concatenate([grad_qkv_part, gain_partial, grad_out_part], axis=1).astype(BF)
    d_normed, grad_attn, grad_gate_up, grad_down = closing(
        partial.reshape(wide, 2, deep, 2 * own_rows, -1),
        near_part,
        far_part,
        ring_gate_up.result().astype(BF),
        ring_down.result().astype(BF),
        wide,
        deep,
    )
    grad_attn, grad_gate_up, grad_down = (
        grads.astype(F32) for grads in (grad_attn, grad_gate_up, grad_down)
    )
    gain_grads = jnp.sum(grad_attn[:, :, qkv_cols : qkv_cols + 2], axis=0).T
    d_inputs = norm_backward(own_tokens.astype(F32), scales[0][:rows], gain_attn, d_normed) + d_middle
    return (
        result.astype(BF)[None],
        d_inputs.astype(BF)[None],
        columns_of(grad_attn[:, :, :q_cols]),
        columns_of(grad_attn[:, :, q_cols : q_cols + HD]),
        columns_of(grad_attn[:, :, q_cols + HD : qkv_cols]),
        columns_of(grad_attn[:, :, qkv_cols + 128 :]).T,
        columns_of(grad_gate_up[:, :, :hidden_cols]),
        columns_of(grad_gate_up[:, :, hidden_cols:]),
        columns_of(grad_down).T,
        gain_grads[0],
        gain_grads[1],
    )


def solution(mesh):
    token_spec = P("fsdp", "seq", None)
    row_spec = P(AXES, None)
    column_spec = P(None, AXES)
    gain_spec = P(AXES)
    return jax.shard_map(
        shards,
        mesh=mesh,
        in_specs=(
            token_spec,
            P("fsdp", None),
            row_spec,
            row_spec,
            row_spec,
            column_spec,
            row_spec,
            row_spec,
            column_spec,
            gain_spec,
            gain_spec,
            token_spec,
        ),
        out_specs=(
            token_spec,
            token_spec,
            row_spec,
            row_spec,
            row_spec,
            column_spec,
            row_spec,
            row_spec,
            column_spec,
            gain_spec,
            gain_spec,
        ),
        check_vma=False,
    )
```

```python
import functools

import jax
import jax.numpy as jnp
from jax import lax
from jax.experimental import pallas as pl
from jax.experimental.pallas import tpu as pltpu
from jax.sharding import PartitionSpec as P

HEADS = 32
KV = 4
HD = 64
EPSILON = 1e-05
ROPE_BASE = 10000.0
MASKED = -1e30
GROUP = 4
AXES = ("fsdp", "seq")
BF = jnp.bfloat16
F32 = jnp.float32


def contract(left, right, left_dim, right_dim):
    return lax.dot_general(
        left, right, (((left_dim,), (right_dim,)), ((), ())), preferred_element_type=F32
    )


def doc_first(start_row, places):
    inside = start_row[None, :] <= places[:, None]
    return jnp.max(jnp.where(inside, start_row[None, :], 0), axis=1)


def rotary_tables(offsets):
    half_dim = HD // 2
    frequency = ROPE_BASE ** (-(jnp.arange(half_dim, dtype=F32) / half_dim))
    angles = frequency[:, None] * offsets.astype(F32)[None, :]
    return (jnp.cos(angles), jnp.sin(angles))


def rotate(values, cos_table, sine_table):
    half_dim = HD // 2
    front_half = values[:, :half_dim]
    back_half = values[:, half_dim:]
    return jnp.concatenate(
        [
            front_half * cos_table - back_half * sine_table,
            back_half * cos_table + front_half * sine_table,
        ],
        axis=1,
    )


def unrotate(grads_in, cos_table, sine_table):
    return rotate(grads_in, cos_table, -sine_table)


def swap_pair(flag, pair):
    return [jnp.where(flag == 1, pair[1], pair[0]), jnp.where(flag == 1, pair[0], pair[1])]


def forward_kernel(
    meta, query_ref, keyval_ref, first_ref, out_ref, lse_ref, q_all, top, total, acc, *, rows, heads, pair
):
    cell = pl.program_id(0)
    lowest, highest, key_base, first_most, query_at = (meta[cell, i] for i in range(5))
    for head in range(heads):
        q_all[:, head * rows : (head + 1) * rows] = query_ref[head]
    top[...] = jnp.full_like(top, MASKED)
    total[...] = jnp.zeros_like(total)
    acc[...] = jnp.zeros_like(acc)
    width = pair * rows

    def visit(block, masked):
        start = pl.multiple_of(block * rows, rows)
        keyval = keyval_ref[pl.ds(start, rows), :]
        key = keyval[:, :HD]
        value_t = keyval[:, HD:].T
        if masked:
            key_at = key_base + start + lax.broadcasted_iota(jnp.int32, (rows, rows), 0)
            token_at = query_at + lax.broadcasted_iota(jnp.int32, (rows, rows), 1)
            allowed = (key_at <= token_at) & (key_at >= first_ref[0])
            bias = jnp.where(allowed, 0.0, MASKED)
            bias = jnp.concatenate([bias] * pair, axis=1)
        for piece in range(heads // pair):
            cols = slice(piece * width, (piece + 1) * width)
            score = contract(key, q_all[:, cols], 1, 0)
            if masked:
                score = score + bias
            before = top[:, cols]
            now = jnp.maximum(before, jnp.max(score, axis=0, keepdims=True))
            weight = jnp.exp(score - now)
            decay = jnp.exp(before - now)
            top[:, cols] = now
            total[:, cols] = total[:, cols] * decay + jnp.sum(weight, axis=0, keepdims=True)
            acc[:, cols] = acc[:, cols] * decay + contract(value_t, weight.astype(BF), 1, 0)

    def step(block, carry):
        plain = jnp.logical_and(key_base + block * rows >= first_most, block < highest)

        @pl.when(plain)
        def _():
            visit(block, False)

        @pl.when(jnp.logical_not(plain))
        def _():
            visit(block, True)

        return carry

    lax.fori_loop(lowest, highest + 1, step, 0)
    sums = total[...]
    scaled = acc[...] * (1.0 / sums)
    for head in range(heads):
        out_ref[head] = scaled[:, head * rows : (head + 1) * rows].astype(BF)
    lse_ref[0] = top[...] + jnp.log(sums)


def backward_kernel(
    meta,
    query_ref,
    keyval_ref,
    first_ref,
    out_ref,
    lse_ref,
    grad_ref,
    dquery_ref,
    dkeyval_ref,
    q_all,
    g_all,
    delta,
    dq_acc,
    dkv_acc,
    *,
    rows,
    heads,
    pair,
):
    cell = pl.program_id(0)
    lowest, highest, key_base, first_most, query_at = (meta[cell, i] for i in range(5))
    for head in range(heads):
        cols = slice(head * rows, (head + 1) * rows)
        q_all[:, cols] = query_ref[head]
        g_all[:, cols] = grad_ref[head]
        delta[:, cols] = jnp.sum(
            grad_ref[head].astype(F32) * out_ref[head].astype(F32), axis=0, keepdims=True
        )
    dq_acc[...] = jnp.zeros_like(dq_acc)

    @pl.when(cell == 0)
    def _():
        dkv_acc[...] = jnp.zeros_like(dkv_acc)

    width = pair * rows

    def visit(block, masked):
        start = pl.multiple_of(block * rows, rows)
        keyval = keyval_ref[pl.ds(start, rows), :]
        key = keyval[:, :HD]
        value = keyval[:, HD:]
        key_t = key.T
        if masked:
            key_at = key_base + start + lax.broadcasted_iota(jnp.int32, (rows, rows), 0)
            token_at = query_at + lax.broadcasted_iota(jnp.int32, (rows, rows), 1)
            allowed = (key_at <= token_at) & (key_at >= first_ref[0])
            bias = jnp.where(allowed, 0.0, MASKED)
            bias = jnp.concatenate([bias] * pair, axis=1)
        dkey = jnp.zeros((rows, HD), F32)
        dvalue = jnp.zeros((rows, HD), F32)
        for piece in range(heads // pair):
            cols = slice(piece * width, (piece + 1) * width)
            score = contract(key, q_all[:, cols], 1, 0)
            if masked:
                score = score + bias
            weight = jnp.exp(score - lse_ref[0, :, cols])
            dweight = contract(value, g_all[:, cols], 1, 0)
            dscore = (weight * (dweight - delta[:, cols])).astype(BF)
            dq_acc[:, cols] = dq_acc[:, cols] + contract(key_t, dscore, 1, 0)
            dkey = dkey + contract(dscore, q_all[:, cols], 1, 1)
            dvalue = dvalue + contract(weight.astype(BF), g_all[:, cols], 1, 1)
        dkv_acc[pl.ds(start, rows), :] = dkv_acc[pl.ds(start, rows), :] + jnp.concatenate(
            [dkey, dvalue], axis=1
        )

    def step(block, carry):
        plain = jnp.logical_and(key_base + block * rows >= first_most, block < highest)

        @pl.when(plain)
        def _():
            visit(block, False)

        @pl.when(jnp.logical_not(plain))
        def _():
            visit(block, True)

        return carry

    lax.fori_loop(lowest, highest + 1, step, 0)
    scaled = dq_acc[...] * HD ** (-0.5)
    for head in range(heads):
        dquery_ref[head] = scaled[:, head * rows : (head + 1) * rows].astype(BF)

    @pl.when(cell == 1)
    def _():
        dkeyval_ref[...] = dkv_acc[...].astype(BF)


def attention_specs(rows, heads, keys):
    return dict(
        head=pl.BlockSpec((heads, HD, rows), lambda cell, meta: (0, 0, cell)),
        keyval=pl.BlockSpec((keys, 2 * HD), lambda cell, meta: (0, 0)),
        first=pl.BlockSpec((1, 1, rows), lambda cell, meta: (cell, 0, 0)),
        stat=pl.BlockSpec((1, 1, heads * rows), lambda cell, meta: (cell, 0, 0)),
    )


def attend_forward(meta, query, keyval, first):
    heads, _, tokens = query.shape
    rows = tokens // 2
    keys = keyval.shape[0]
    specs = attention_specs(rows, heads, keys)
    wide = heads * rows
    return pl.pallas_call(
        functools.partial(forward_kernel, rows=rows, heads=heads, pair=4),
        grid_spec=pltpu.PrefetchScalarGridSpec(
            num_scalar_prefetch=1,
            grid=(2,),
            in_specs=[specs["head"], specs["keyval"], specs["first"]],
            out_specs=[specs["head"], specs["stat"]],
            scratch_shapes=[
                pltpu.VMEM((HD, wide), BF),
                pltpu.VMEM((1, wide), F32),
                pltpu.VMEM((1, wide), F32),
                pltpu.VMEM((HD, wide), F32),
            ],
        ),
        out_shape=(
            jax.ShapeDtypeStruct(query.shape, BF),
            jax.ShapeDtypeStruct((2, 1, wide), F32),
        ),
        compiler_params=pltpu.CompilerParams(
            dimension_semantics=("arbitrary",), vmem_limit_bytes=48 * 1024 * 1024
        ),
        cost_estimate=pl.CostEstimate(
            flops=40_000_000_000, bytes_accessed=10_000_000, transcendentals=0
        ),
        name="attend_forward",
    )(meta, query, keyval, first)


def attend_backward(meta, query, keyval, first, out, lse, grad):
    heads, _, tokens = query.shape
    rows = tokens // 2
    keys = keyval.shape[0]
    specs = attention_specs(rows, heads, keys)
    wide = heads * rows
    return pl.pallas_call(
        functools.partial(backward_kernel, rows=rows, heads=heads, pair=4),
        grid_spec=pltpu.PrefetchScalarGridSpec(
            num_scalar_prefetch=1,
            grid=(2,),
            in_specs=[
                specs["head"],
                specs["keyval"],
                specs["first"],
                specs["head"],
                specs["stat"],
                specs["head"],
            ],
            out_specs=[specs["head"], specs["keyval"]],
            scratch_shapes=[
                pltpu.VMEM((HD, wide), BF),
                pltpu.VMEM((HD, wide), BF),
                pltpu.VMEM((1, wide), F32),
                pltpu.VMEM((HD, wide), F32),
                pltpu.VMEM((keys, 2 * HD), F32),
            ],
        ),
        out_shape=(
            jax.ShapeDtypeStruct(query.shape, BF),
            jax.ShapeDtypeStruct(keyval.shape, BF),
        ),
        compiler_params=pltpu.CompilerParams(
            dimension_semantics=("arbitrary",), vmem_limit_bytes=48 * 1024 * 1024
        ),
        cost_estimate=pl.CostEstimate(
            flops=80_000_000_000, bytes_accessed=16_000_000, transcendentals=0
        ),
        name="attend_backward",
    )(meta, query, keyval, first, out, lse, grad)


def feed_kernel(normed, cotangent, w_gate_up, w_down_t, *rest, columns):
    hidden, d_gate_up = rest[-2:]
    step = 256
    for low in range(0, columns, step):
        high = min(low + step, columns)
        gate = contract(normed[...], w_gate_up[:, low:high], 1, 0)
        up = contract(normed[...], w_gate_up[:, columns + low : columns + high], 1, 0)
        d_hidden = contract(cotangent[...], w_down_t[:, low:high], 1, 0)
        sigmoid = 1.0 / (1.0 + jnp.exp(-gate))
        silu = gate * sigmoid
        hidden[:, low:high] = (silu * up).astype(BF)
        d_gate_up[:, low:high] = (
            d_hidden * up * sigmoid * (1.0 + gate * (1.0 - sigmoid))
        ).astype(BF)
        d_gate_up[:, columns + low : columns + high] = (d_hidden * silu).astype(BF)


def feed_forward(normed, cotangent, w_gate_up, w_down_t, halves, before=()):
    tokens, width = cotangent.shape[0] // 2, cotangent.shape[1]
    columns = w_down_t.shape[1]
    tile = min(256, tokens)
    shifts = [half * (tokens // tile) for half in halves]

    def token_spec(shift):
        return pl.BlockSpec((tile, width), lambda i: (i + shift, 0))

    def weight_spec(wide):
        return pl.BlockSpec((width, wide), lambda i: (0, 0), pipeline_mode=pl.Buffered(1))

    def out_spec(wide):
        return pl.BlockSpec((tile, wide), lambda i: (i + shifts[2], 0))

    return pl.pallas_call(
        functools.partial(feed_kernel, columns=columns),
        grid=(tokens // tile,),
        in_specs=[
            token_spec(shifts[0]),
            token_spec(shifts[1]),
            weight_spec(2 * columns),
            weight_spec(columns),
            *[pl.BlockSpec(memory_space=pl.ANY) for _ in before],
        ],
        out_specs=(out_spec(columns), out_spec(2 * columns)),
        out_shape=(
            jax.ShapeDtypeStruct((2 * tokens, columns), BF),
            jax.ShapeDtypeStruct((2 * tokens, 2 * columns), BF),
        ),
        input_output_aliases={4 + i: i for i in range(len(before))},
        compiler_params=pltpu.CompilerParams(
            dimension_semantics=("arbitrary",), vmem_limit_bytes=56 * 1024 * 1024
        ),
        cost_estimate=pl.CostEstimate(
            flops=6 * tokens * width * columns, bytes_accessed=6 * width * columns, transcendentals=0
        ),
        name="feed_forward",
    )(normed, cotangent, w_gate_up, w_down_t, *before)


def opening_kernel(
    tokens,
    quarters_attn,
    quarters_down,
    quarters_gate_up,
    group,
    whole_attn,
    whole_down,
    whole_gate_up,
    local_sem,
    near_send,
    near_recv,
    swap_send,
    swap_recv,
    hop_send,
    hop_recv,
    *,
    wide,
    deep,
    own_rows,
):
    ring, half_ring = wide * deep, wide * deep // 2
    f_at, s_at = lax.axis_index("fsdp"), lax.axis_index("seq")
    y_at, x_at, z_at, c_at = f_at // 2, lax.rem(f_at, 2), s_at // 2, lax.rem(s_at, 2)
    here = y_at * deep + jnp.where(lax.rem(y_at, 2) == 0, z_at, deep - 1 - z_at)

    def ring_place(offset):
        index = lax.rem(here + offset + 2 * ring, ring)
        row, col = index // deep, lax.rem(index, deep)
        return row, jnp.where(lax.rem(row, 2) == 0, col, deep - 1 - col)

    def ring_device(offset):
        row, col = ring_place(offset)
        return row * 2 + x_at, col * 2 + c_at

    moves = ((0, 1), (1, 0), (1, 1))

    def other(dx, dc):
        return lax.rem(x_at + dx, 2), lax.rem(c_at + dc, 2)

    def group_device(dx, dc):
        x, c = other(dx, dc)
        return y_at * 2 + x, z_at * 2 + c

    def remote(source, target, send, recv, device):
        return pltpu.make_async_remote_copy(
            src_ref=source,
            dst_ref=target,
            send_sem=send,
            recv_sem=recv,
            device_id=device,
            device_id_type=pl.DeviceIdType.MESH,
        )

    barrier = pltpu.get_barrier_semaphore()
    partners = [group_device(*move) for move in moves] + [ring_device(1), ring_device(-1)]
    for device in partners:
        pl.semaphore_signal(barrier, inc=1, device_id=device, device_id_type=pl.DeviceIdType.MESH)
    pl.semaphore_wait(barrier, len(partners))

    my_rows = pl.ds(pl.multiple_of(c_at * own_rows, own_rows), own_rows)
    targets = (
        whole_attn.at[y_at, x_at, z_at, my_rows],
        whole_down.at[y_at, x_at, z_at, my_rows],
        whole_gate_up.at[y_at, x_at, z_at, my_rows],
    )
    quarters = (quarters_attn, quarters_down, quarters_gate_up)
    locals_ = [
        pltpu.make_async_copy(quarters[i].at[x_at * 2 + c_at], targets[i], local_sem.at[i])
        for i in range(3)
    ] + [pltpu.make_async_copy(tokens, group.at[0], local_sem.at[3])]

    def swaps(i):
        copies = []
        for j, (dx, dc) in enumerate(moves):
            x, c = other(dx, dc)
            copies.append(
                remote(
                    quarters[i].at[x * 2 + c],
                    targets[i],
                    swap_send.at[i, j],
                    swap_recv.at[i, j],
                    group_device(dx, dc),
                )
            )
        return copies

    swap = [swaps(i) for i in range(3)]
    to_core = remote(tokens, group.at[1], near_send.at[0], near_recv.at[0], group_device(0, 1))
    to_x = remote(tokens, group.at[2], near_send.at[1], near_recv.at[1], group_device(1, 0))
    far_to_core = remote(
        group.at[2], group.at[3], near_send.at[2], near_recv.at[2], group_device(0, 1)
    )
    wholes = (whole_attn, whole_down)

    def hop(i, direction, step):
        row, col = ring_place(-direction * (step - 1))
        if step < half_ring:
            part = wholes[i].at[row, :, col]
        else:
            part = wholes[i].at[row, 0 if direction == 1 else 1, col]
        side = 0 if direction == 1 else 1
        return remote(
            part,
            part,
            hop_send.at[i, side, step - 1],
            hop_recv.at[i, side, step - 1],
            ring_device(direction),
        )

    hops = [
        [[hop(i, direction, step) for direction in (1, -1)] for step in range(1, half_ring + 1)]
        for i in range(2)
    ]

    for copy in locals_:
        copy.start()
    for copy in swap[0]:
        copy.start()
    for copy in swap[1]:
        copy.start()
    to_core.start()
    to_x.start()
    for copy in swap[2]:
        copy.start()
    for i in range(2):
        locals_[i].wait()
        for copy in swap[i]:
            copy.wait_recv()
    for i in range(2):
        for step in range(half_ring):
            if i == 0 or step > 0:
                for copy in hops[i][step]:
                    copy.start()
            if i == 0 and step == half_ring - 1:
                for copy in hops[1][0]:
                    copy.start()
            for copy in hops[i][step]:
                copy.wait_recv()
            if i == 0 and step == half_ring - 1:
                to_x.wait_recv()
                far_to_core.start()
    for copy in locals_[2:]:
        copy.wait()
    for copy in swap[2] + [to_core, far_to_core]:
        copy.wait_recv()
    for copy in swap[0] + swap[1] + swap[2] + [to_core, to_x, far_to_core]:
        copy.wait_send()
    for i in range(2):
        for pair in hops[i]:
            for copy in pair:
                copy.wait_send()


def opening(tokens, quarters_attn, quarters_down, quarters_gate_up, wide, deep):
    own_rows = quarters_attn.shape[1]
    half_ring = wide * deep // 2

    def whole(quarters):
        return jax.ShapeDtypeStruct((wide, 2, deep, 2 * own_rows, quarters.shape[2]), BF)

    anywhere = pl.BlockSpec(memory_space=pl.ANY)
    return pl.pallas_call(
        functools.partial(opening_kernel, wide=wide, deep=deep, own_rows=own_rows),
        out_shape=(
            jax.ShapeDtypeStruct((GROUP, *tokens.shape), BF),
            whole(quarters_attn),
            whole(quarters_down),
            whole(quarters_gate_up),
        ),
        in_specs=[anywhere] * 4,
        out_specs=(anywhere,) * 4,
        scratch_shapes=[
            pltpu.SemaphoreType.DMA((4,)),
            pltpu.SemaphoreType.DMA((3,)),
            pltpu.SemaphoreType.DMA((3,)),
            pltpu.SemaphoreType.DMA((3, 3)),
            pltpu.SemaphoreType.DMA((3, 3)),
            pltpu.SemaphoreType.DMA((2, 2, half_ring)),
            pltpu.SemaphoreType.DMA((2, 2, half_ring)),
        ],
        compiler_params=pltpu.CompilerParams(collective_id=0, has_side_effects=True),
        name="opening",
    )(tokens, quarters_attn, quarters_down, quarters_gate_up)


def closing_kernel(
    partial,
    near_part,
    far_part,
    chunk_gate_up,
    chunk_down,
    d_normed,
    owned_attn,
    owned_gate_up,
    owned_down,
    land,
    chunk_attn,
    core_land,
    x_stage,
    x_land,
    local_sem,
    near_send,
    near_recv,
    swap_send,
    swap_recv,
    hop_send,
    hop_recv,
    *,
    wide,
    deep,
    own_rows,
):
    ring, half_ring = wide * deep, wide * deep // 2
    f_at, s_at = lax.axis_index("fsdp"), lax.axis_index("seq")
    y_at, x_at, z_at, c_at = f_at // 2, lax.rem(f_at, 2), s_at // 2, lax.rem(s_at, 2)
    here = y_at * deep + jnp.where(lax.rem(y_at, 2) == 0, z_at, deep - 1 - z_at)

    def ring_place(offset):
        index = lax.rem(here + offset + 2 * ring, ring)
        row, col = index // deep, lax.rem(index, deep)
        return row, jnp.where(lax.rem(row, 2) == 0, col, deep - 1 - col)

    def ring_device(offset):
        row, col = ring_place(offset)
        return row * 2 + x_at, col * 2 + c_at

    moves = ((0, 1), (1, 0), (1, 1))

    def other(dx, dc):
        return lax.rem(x_at + dx, 2), lax.rem(c_at + dc, 2)

    def group_device(dx, dc):
        x, c = other(dx, dc)
        return y_at * 2 + x, z_at * 2 + c

    def remote(source, target, send, recv, device):
        return pltpu.make_async_remote_copy(
            src_ref=source,
            dst_ref=target,
            send_sem=send,
            recv_sem=recv,
            device_id=device,
            device_id_type=pl.DeviceIdType.MESH,
        )

    barrier = pltpu.get_barrier_semaphore()
    partners = [group_device(*move) for move in moves] + [ring_device(1), ring_device(-1)]
    for device in partners:
        pl.semaphore_signal(barrier, inc=1, device_id=device, device_id_type=pl.DeviceIdType.MESH)
    pl.semaphore_wait(barrier, len(partners))

    rows = x_land.shape[0]
    far_core = remote(
        far_part.at[rows:], core_land.at[0], near_send.at[0], near_recv.at[0], group_device(0, 1)
    )
    near_core = remote(
        near_part.at[rows:], core_land.at[1], near_send.at[1], near_recv.at[1], group_device(0, 1)
    )
    far_x = remote(x_stage, x_land, near_send.at[2], near_recv.at[2], group_device(1, 0))

    def hop(side, step):
        direction = 1 - 2 * side
        if step == 1:
            row, col = ring_place(direction * half_ring)
            source, target = partial.at[row, side, col], land.at[side, 0, side]
        else:
            source, target = land.at[side, step - 2], land.at[side, step - 1]
        return remote(
            source,
            target,
            hop_send.at[side, step - 1],
            hop_recv.at[side, step - 1],
            ring_device(direction),
        )

    chunks = (chunk_attn, chunk_gate_up, chunk_down)
    owned = (owned_attn, owned_gate_up, owned_down)

    def piece(i, x, c):
        return chunks[i].at[x, pl.ds(pl.multiple_of(c * own_rows, own_rows), own_rows)]

    def swaps(i):
        copies = []
        for j, (dx, dc) in enumerate(moves):
            copies.append(
                remote(
                    piece(i, *other(dx, dc)),
                    owned[i].at[x_at * 2 + c_at],
                    swap_send.at[i, j],
                    swap_recv.at[i, j],
                    group_device(dx, dc),
                )
            )
        return copies

    swap = [swaps(i) for i in range(3)]
    keep = [
        pltpu.make_async_copy(piece(i, x_at, c_at), owned[i].at[x_at * 2 + c_at], local_sem.at[i])
        for i in range(3)
    ]

    far_core.start()
    near_core.start()
    for side in range(2):
        hop(side, 1).start()
    far_core.wait_recv()
    x_stage[...] = (far_part[:rows].astype(F32) + core_land[0].astype(F32)).astype(BF)
    far_x.start()
    for i in (1, 2):
        for copy in swap[i]:
            copy.start()
        keep[i].start()
    for step in range(2, half_ring + 1):
        for side in range(2):
            hop(side, step - 1).wait_recv()
            row, col = ring_place((1 - 2 * side) * (half_ring - step + 1))
            if step == 2:
                mine = partial[row, side, col].astype(F32) + land[side, 0, side].astype(F32)
                land[side, 0, side] = mine.astype(BF)
                land[side, 0, 1 - side] = partial[row, 1 - side, col]
            else:
                for half in range(2):
                    mine = partial[row, half, col].astype(F32)
                    mine = mine + land[side, step - 2, half].astype(F32)
                    land[side, step - 2, half] = mine.astype(BF)
            hop(side, step).start()
    near_core.wait_recv()
    for side in range(2):
        hop(side, half_ring).wait_recv()
    for half in range(2):
        total = partial[y_at, half, z_at].astype(F32) + land[0, half_ring - 1, half].astype(F32)
        total = total + land[1, half_ring - 1, half].astype(F32)
        chunk_attn[half] = total.astype(BF)
    for copy in swap[0]:
        copy.start()
    keep[0].start()
    far_x.wait_recv()
    d_normed[...] = (
        near_part[:rows].astype(F32) + core_land[1].astype(F32) + x_land[...].astype(F32)
    )
    for i in (1, 2, 0):
        keep[i].wait()
        for copy in swap[i]:
            copy.wait_recv()
    for copy in swap[0] + swap[1] + swap[2] + [far_core, near_core, far_x]:
        copy.wait_send()
    for side in range(2):
        for step in range(1, half_ring + 1):
            hop(side, step).wait_send()


def closing(partial, near_part, far_part, chunk_gate_up, chunk_down, wide, deep):
    own_rows = partial.shape[3] // 2
    half_ring = wide * deep // 2
    rows, width = near_part.shape[0] // 2, near_part.shape[1]
    columns = partial.shape[4]
    anywhere = pl.BlockSpec(memory_space=pl.ANY)
    vmem = pl.BlockSpec(memory_space=pltpu.VMEM)

    def quarters(wanted):
        return jax.ShapeDtypeStruct((GROUP, own_rows, wanted), BF)

    return pl.pallas_call(
        functools.partial(closing_kernel, wide=wide, deep=deep, own_rows=own_rows),
        out_shape=(
            jax.ShapeDtypeStruct((rows, width), F32),
            quarters(columns),
            quarters(chunk_gate_up.shape[2]),
            quarters(chunk_down.shape[2]),
        ),
        in_specs=[vmem, vmem, vmem, anywhere, anywhere],
        out_specs=(vmem, anywhere, anywhere, anywhere),
        scratch_shapes=[
            pltpu.VMEM((2, half_ring, 2, 2 * own_rows, columns), BF),
            pltpu.VMEM((2, 2 * own_rows, columns), BF),
            pltpu.VMEM((2, rows, width), BF),
            pltpu.VMEM((rows, width), BF),
            pltpu.VMEM((rows, width), BF),
            pltpu.SemaphoreType.DMA((3,)),
            pltpu.SemaphoreType.DMA((3,)),
            pltpu.SemaphoreType.DMA((3,)),
            pltpu.SemaphoreType.DMA((3, 3)),
            pltpu.SemaphoreType.DMA((3, 3)),
            pltpu.SemaphoreType.DMA((2, half_ring)),
            pltpu.SemaphoreType.DMA((2, half_ring)),
        ],
        compiler_params=pltpu.CompilerParams(
            collective_id=1, has_side_effects=True, vmem_limit_bytes=56 * 1024 * 1024
        ),
        name="closing",
    )(partial, near_part, far_part, chunk_gate_up, chunk_down)


def shards(
    tokens,
    starts,
    w_query,
    w_key,
    w_value,
    w_out,
    w_gate,
    w_up,
    w_down,
    norm_attn,
    norm_mlp,
    cotangent,
):
    seq_count = lax.axis_size("seq")
    fsdp_count = lax.axis_size("fsdp")
    deep = seq_count // 2
    wide = fsdp_count // 2
    ring = wide * deep
    half_ring = ring // 2
    f_at, s_at = lax.axis_index("fsdp"), lax.axis_index("seq")
    x_at, y_at, c_at, z_at = f_at % 2, f_at // 2, s_at % 2, s_at // 2
    rows = tokens.shape[1]
    width = tokens.shape[2]
    own_rows = w_query.shape[0]

    def perm_of(move):
        found = []
        for f in range(fsdp_count):
            for s in range(seq_count):
                target = move(f // 2, f % 2, s // 2, s % 2)
                if target is not None:
                    ty, tx, tz, tc = target
                    found.append((f * seq_count + s, (ty * 2 + tx) * seq_count + tz * 2 + tc))
        return found

    def ring_place(position):
        position = position % ring
        row, col = position // deep, position % deep
        return row, col if row % 2 == 0 else deep - 1 - col

    def ring_index(y, z):
        return y * deep + (z if y % 2 == 0 else deep - 1 - z)

    def around(step):
        def move(y, x, z, c):
            ty, tz = ring_place(ring_index(y, z) + step)
            return ty, x, tz, c

        return move

    def along(step):
        return lambda y, x, z, c: (y, x, z + step, c) if 0 <= z + step < deep else None

    core_perm = perm_of(lambda y, x, z, c: (y, x, z, 1 - c))
    x_perm = perm_of(lambda y, x, z, c: (y, 1 - x, z, c))
    cross_perm = perm_of(lambda y, x, z, c: (y, 1 - x, z, 1 - c))
    right_perm, left_perm = perm_of(around(1)), perm_of(around(-1))

    def send(value, perm):
        return lax.ppermute(value, AXES, perm)

    position = y_at * deep + jnp.where(y_at % 2 == 0, z_at, deep - 1 - z_at)

    def place_at(offset):
        index = lax.rem(position + offset + 2 * ring, ring)
        row, col = index // deep, index % deep
        return row, jnp.where(row % 2 == 0, col, deep - 1 - col)

    def with_core(block):
        return jnp.concatenate([block, send(block, core_perm)], axis=0)

    def gather_group(block):
        return [with_core(block), with_core(send(block, x_perm))]

    def to_quarters(pieces):
        return jnp.concatenate(
            [p.reshape(own_rows, GROUP, -1).transpose(1, 0, 2) for p in pieces], axis=2
        )

    def absolute(got):
        rows_of = [swap_pair(c_at, pair) for pair in got]
        ordered = [swap_pair(x_at, [rows_of[0][c], rows_of[1][c]]) for c in range(2)]
        return [[ordered[0][x], ordered[1][x]] for x in range(2)]

    class Gather:
        def __init__(self, room):
            self.room = room
            row, col = place_at(0)
            size = (1, 2, 1, *room.shape[3:])
            chunk = lax.dynamic_slice(room, (row, 0, col, 0, 0), size).reshape(2, *room.shape[3:])
            self.right = self.left = chunk
            self.step, self.got = 0, []

        def advance(self, times):
            for _ in range(min(times, half_ring - self.step)):
                self.step += 1
                if self.step < half_ring:
                    self.right = send(self.right, right_perm)
                    self.left = send(self.left, left_perm)
                    self.got += [(-self.step, 0, self.right), (self.step, 0, self.left)]
                else:
                    self.got += [
                        (half_ring, 0, send(self.right[:1], right_perm)),
                        (half_ring, 1, send(self.left[1:], left_perm)),
                    ]

        def wait_for(self, value):
            self.right, self.left = after((self.right, self.left), value)

        def whole(self):
            result = self.room
            for offset, x_from, piece in self.got:
                row, col = place_at(offset)
                result = lax.dynamic_update_slice(
                    result, piece[None, :, None], (row, x_from, col, 0, 0)
                )
            return result.reshape(-1, result.shape[4])

    class Scatter:
        def __init__(self, partial):
            self.parts = partial.reshape(wide, 2, deep, 2 * own_rows, partial.shape[1])
            self.step, self.right, self.left = 0, None, None

        def part(self, offset, x_from=0, x_count=2):
            row, col = place_at(offset)
            return lax.dynamic_slice(
                self.parts,
                (row, x_from, col, 0, 0),
                (1, x_count, 1, 2 * own_rows, self.parts.shape[4]),
            ).reshape(x_count, 2 * own_rows, self.parts.shape[4])

        def advance(self, times):
            for _ in range(min(times, half_ring - self.step)):
                self.step += 1
                offset = half_ring - self.step + 1
                if self.step == 1:
                    to_right, to_left = self.part(offset, 0, 1), self.part(-offset, 1, 1)
                else:
                    to_right, to_left = self.joined(offset, -offset)
                self.right = send(to_right, right_perm)
                self.left = send(to_left, left_perm)

        def joined(self, at_right, at_left):
            to_right, to_left = self.part(at_right), self.part(at_left)
            if self.step == 2:
                to_right = jnp.concatenate([add_low(to_right[:1], self.right), to_right[1:]])
                to_left = jnp.concatenate([to_left[:1], add_low(to_left[1:], self.left)])
                return to_right, to_left
            return add_low(to_right, self.right), add_low(to_left, self.left)

        def wait_for(self, value):
            self.right, self.left = after((self.right, self.left), value)

        def result(self):
            self.advance(half_ring)
            own = self.part(0).astype(F32)
            if half_ring > 1:
                return own + self.right.astype(F32) + self.left.astype(F32)
            return own + jnp.concatenate([self.right, self.left]).astype(F32)

    def stage(moving, values):
        ends = [(member.right, member.left) for member in moving]
        ends, values = lax.optimization_barrier((ends, values))
        for member, (right, left) in zip(moving, ends):
            member.right, member.left = right, left
        return values

    def add_low(one, other):
        return (one.astype(F32) + other.astype(F32)).astype(BF)

    per_window = -(-half_ring // 4)

    def columns_of(quarters):
        return quarters.transpose(1, 0, 2).reshape(own_rows, -1)

    def reduce_core(partial):
        return partial[:rows].astype(F32) + send(partial[rows:], core_perm).astype(F32)

    def send_far(partial):
        return send(reduce_core(partial).astype(BF), x_perm).astype(F32)

    index = f_at * seq_count + s_at
    count = fsdp_count * seq_count
    doublings = [
        (bit, [(i, i ^ (1 << bit)) for i in range(count)]) for bit in range(count.bit_length() - 1)
    ]

    def sum_small(value):
        for bit, perm in doublings:
            value = value + send(value, perm)
        return value

    def after(value, other):
        return lax.optimization_barrier((value, other))[0]

    q_cols = HEADS // GROUP * HD
    qkv_cols = q_cols + 2 * HD
    hidden_cols = w_gate.shape[1] // GROUP
    start_rows = [starts[0], send(starts, x_perm)[0]]
    block_at = [rows * (2 * z_at + (c_at ^ dc)) for dc in range(2)]
    within = jnp.arange(rows, dtype=jnp.int32)
    base_block = 2 * (z_at - deep + 1)
    tables, first_rows, metas = [], [], []
    for dx in range(2):
        places = [block_at[dc] + within for dc in range(2)]
        firsts = [doc_first(start_rows[dx], places[dc]) for dc in range(2)]
        tables.append(rotary_tables(jnp.concatenate([p - f for p, f in zip(places, firsts)])))
        first_rows.append(jnp.stack(firsts)[:, None, :])
        cells = [
            [
                firsts[dc][0] // rows - base_block,
                block_at[dc] // rows - base_block,
                base_block * rows,
                firsts[dc][rows - 1],
                block_at[dc],
            ]
            for dc in range(2)
        ]
        metas.append(jnp.stack([jnp.stack(cell) for cell in cells]).astype(jnp.int32))

    gain_columns = jnp.pad(jnp.stack([norm_attn, norm_mlp], axis=1), ((0, 0), (0, 126)))
    own_tokens, tables, first_rows, metas = after((tokens[0], tables, first_rows, metas), start_rows[1])
    own_tokens = after(own_tokens, (tables, first_rows, metas))
    group_blocks, whole_attn, whole_down, whole_gate_up = opening(
        own_tokens,
        to_quarters([w_query, w_key, w_value, w_out.T, jnp.tile(gain_columns, (1, GROUP))]),
        to_quarters([w_down.T]),
        to_quarters([w_gate, w_up]),
        wide,
        deep,
    )
    group_tokens = [group_blocks[2 * dx : 2 * dx + 2].reshape(2 * rows, width) for dx in range(2)]
    whole_attn = whole_attn.reshape(width, -1)
    w_down_t = whole_down.reshape(width, -1)
    w_qkv = whole_attn[:, :qkv_cols]
    w_out_t = whole_attn[:, qkv_cols : qkv_cols + q_cols]
    gains = whole_attn[:, qkv_cols + q_cols :].T.astype(F32)
    gain_attn, gain_mlp = gains[0], gains[1]
    ring_gate_up = Gather(whole_gate_up)
    rings = [ring_gate_up]

    def advance(members, times=per_window):
        for member in members:
            member.advance(times)

    advance(rings)
    own_cotangent = after(cotangent[0], group_blocks)
    far_cotangent = send(own_cotangent, x_perm)
    both_cotangent = jnp.concatenate(
        [own_cotangent, send(own_cotangent, core_perm), far_cotangent, send(far_cotangent, core_perm)]
    )

    heads = HEADS // GROUP
    normed, scales, queries, keyvals, attended, lses = ([None, None] for _ in range(6))
    for dx in (1, 0):
        group_inputs = group_tokens[dx].astype(F32)
        scales[dx] = lax.rsqrt(jnp.mean(group_inputs * group_inputs, axis=1, keepdims=True) + EPSILON)
        normed[dx] = (group_inputs * scales[dx] * gain_attn).astype(BF)
        pre = contract(w_qkv, normed[dx], 0, 1)
        turned = rotate(pre[:q_cols].reshape(heads, HD, -1), *tables[dx])
        queries[dx] = (turned * HD ** (-0.5)).astype(BF)
        key = rotate(pre[q_cols : q_cols + HD][None], *tables[dx])[0].astype(BF)
        keyval = jnp.concatenate([key, pre[q_cols + HD :].astype(BF)], axis=0).T
        keyval = jnp.concatenate(swap_pair(c_at, [keyval[:rows], keyval[rows:]]))
        earlier = [send(keyval, perm_of(along(step))) for step in range(deep - 1, 0, -1)]
        keyvals[dx] = jnp.concatenate(earlier + [keyval], axis=0)
    keyvals[1] = stage(rings, keyvals[1])
    advance(rings)
    attended[1], lses[1] = attend_forward(metas[1], queries[1], keyvals[1], first_rows[1])
    attended[1] = stage(rings, attended[1])
    advance(rings)
    far_sum = reduce_core(contract(attended[1].reshape(q_cols, -1), w_out_t, 0, 1).astype(BF)).astype(BF)
    far = send(far_sum, x_perm).astype(F32)
    query_near = after(queries[0], far_sum)
    attended[0], lses[0] = attend_forward(metas[0], query_near, keyvals[0], first_rows[0])
    attended[0], far = stage(rings, (attended[0], far))
    advance(rings, half_ring)
    near = reduce_core(contract(attended[0].reshape(q_cols, -1), w_out_t, 0, 1).astype(BF))
    middle = own_tokens.astype(F32) + near + far
    attended_t = [a.reshape(q_cols, -1) for a in attended]

    scale_mlp = lax.rsqrt(jnp.mean(middle * middle, axis=1, keepdims=True) + EPSILON)
    normed_own = (middle * scale_mlp * gain_mlp).astype(BF)
    normed_far = send(normed_own, x_perm)
    normed_near = [normed_own, send(normed_own, core_perm)]
    w_gate_up = ring_gate_up.whole()
    normed_near, both_cotangent = stage([], (normed_near, both_cotangent))
    both = feed_forward(
        jnp.concatenate(normed_near), both_cotangent, w_gate_up, w_down_t, (0, 0, 0)
    )
    normed_far, both = stage([], (normed_far, both))
    both_normed = jnp.concatenate([*normed_near, normed_far, send(normed_far, core_perm)])
    both = feed_forward(both_normed, both_cotangent, w_gate_up, w_down_t, (1, 1, 1), both)
    both_hidden, both_d_gate_up = both
    hidden = [both_hidden[: 2 * rows], both_hidden[2 * rows :]]
    d_gate_up = [both_d_gate_up[: 2 * rows], both_d_gate_up[2 * rows :]]
    far_part = contract(d_gate_up[1], w_gate_up, 1, 1).astype(BF)
    far_sum = reduce_core(far_part).astype(BF)
    far = send(far_sum, x_perm)
    near_part = contract(after(d_gate_up[0], far_part), w_gate_up, 1, 1).astype(BF)
    near = reduce_core(near_part)
    both_hidden = after(both_hidden, (near_part, far_sum))
    ring_down = Scatter(contract(both_cotangent, both_hidden, 0, 0).astype(BF))
    ring_down.advance(per_window)
    both_d_gate_up = after(both_d_gate_up, ring_down.parts)
    ring_gate_up = Scatter(contract(both_normed, both_d_gate_up, 0, 0).astype(BF))
    far, ring_gate_up.parts = stage([ring_down], (far, ring_gate_up.parts))
    far = far.astype(F32)
    ring_gate_up.advance(per_window)
    d_normed_mlp = near + far

    def norm_backward(values, scale_rows, gain, grads_in):
        weighted = grads_in * gain
        inner_mean = jnp.mean(weighted * values, axis=1, keepdims=True)
        cube = scale_rows * scale_rows * scale_rows
        return scale_rows * weighted - values * cube * inner_mean

    gain_grad_mlp = jnp.sum(d_normed_mlp * middle * scale_mlp, axis=0)
    d_middle = norm_backward(middle, scale_mlp, gain_mlp, d_normed_mlp) + cotangent[0].astype(F32)
    rings = [ring_gate_up, ring_down]

    branch_own = d_middle.astype(BF)
    branch_far = send(branch_own, x_perm)
    d_branch = [with_core(branch_own), None]
    d_keyval, d_query = [None, None], [None, None]

    def d_attended(dx):
        return contract(w_out_t, d_branch[dx], 0, 1).astype(BF).reshape(queries[dx].shape)

    def keyval_home(d_keyvals):
        chunks = [d_keyvals[2 * rows * i : 2 * rows * (i + 1)] for i in range(deep)]
        total = chunks[deep - 1].astype(F32)
        came = [send(chunks[deep - 1 - step], perm_of(along(-step))) for step in range(1, deep)]
        for part in came:
            total = total + part.astype(F32)
        return jnp.concatenate(swap_pair(c_at, [total[:rows], total[rows:]])).T

    d_near = stage([ring_gate_up], d_attended(0))
    advance(rings)
    d_query[0], d_keyvals = attend_backward(
        metas[0], queries[0], keyvals[0], first_rows[0], attended[0], lses[0], d_near
    )
    d_query[0], d_keyvals, branch_far = stage(rings, (d_query[0], d_keyvals, branch_far))
    advance(rings)
    d_keyval[0] = keyval_home(d_keyvals)
    d_branch[1] = with_core(branch_far)
    result_part = contract(after(hidden[1], d_query[0]), w_down_t, 1, 1).astype(BF)
    result_sum = reduce_core(result_part).astype(BF)
    result_far = send(result_sum, x_perm).astype(F32)
    d_far = after(d_attended(1), (d_query[0], result_sum))
    d_query[1], d_keyvals = attend_backward(
        metas[1], queries[1], keyvals[1], first_rows[1], attended[1], lses[1], d_far
    )
    d_query[1], d_keyvals, d_keyval[0], result_far = stage(
        rings, (d_query[1], d_keyvals, d_keyval[0], result_far)
    )
    for member in rings:
        member.advance(half_ring)
    d_keyval[1] = keyval_home(d_keyvals)
    grad_out_part = contract(d_branch[0], attended_t[0], 0, 1) + contract(
        after(d_branch[1], d_query[1]), attended_t[1], 0, 1
    )
    result_near = reduce_core(contract(after(hidden[0], d_query[1]), w_down_t, 1, 1).astype(BF))
    result = middle + result_near + result_far

    d_pre = [None, None]
    for dx in range(2):
        d_query_pre = unrotate(d_query[dx].astype(F32), *tables[dx]).astype(BF)
        d_key_pre = unrotate(d_keyval[dx][None, :HD], *tables[dx])[0].astype(BF)
        d_value_pre = d_keyval[dx][HD:].astype(BF)
        d_pre[dx] = jnp.concatenate([d_query_pre.reshape(q_cols, -1), d_key_pre, d_value_pre])
    near_part = contract(d_pre[0], w_qkv, 0, 1).astype(BF)
    far_part = contract(d_pre[1], w_qkv, 0, 1).astype(BF)
    grad_qkv_part = contract(normed[0], d_pre[0], 0, 1) + contract(normed[1], d_pre[1], 0, 1)
    gain_grad_attn = sum(
        jnp.sum(part.astype(F32) * group_tokens[dx].astype(F32) * scales[dx], axis=0)
        for dx, part in enumerate((near_part, far_part))
    )
    gain_partial = jnp.pad(jnp.stack([gain_grad_attn, gain_grad_mlp], axis=1), ((0, 0), (0, 126)))
    partial = jnp.concatenate([grad_qkv_part, gain_partial, grad_out_part], axis=1).astype(BF)
    d_normed, grad_attn, grad_gate_up, grad_down = closing(
        partial.reshape(wide, 2, deep, 2 * own_rows, -1),
        near_part,
        far_part,
        ring_gate_up.result().astype(BF),
        ring_down.result().astype(BF),
        wide,
        deep,
    )
    grad_attn, grad_gate_up, grad_down = (
        grads.astype(F32) for grads in (grad_attn, grad_gate_up, grad_down)
    )
    gain_grads = jnp.sum(grad_attn[:, :, qkv_cols : qkv_cols + 2], axis=0).T
    d_inputs = norm_backward(own_tokens.astype(F32), scales[0][:rows], gain_attn, d_normed) + d_middle
    return (
        result.astype(BF)[None],
        d_inputs.astype(BF)[None],
        columns_of(grad_attn[:, :, :q_cols]),
        columns_of(grad_attn[:, :, q_cols : q_cols + HD]),
        columns_of(grad_attn[:, :, q_cols + HD : qkv_cols]),
        columns_of(grad_attn[:, :, qkv_cols + 128 :]).T,
        columns_of(grad_gate_up[:, :, :hidden_cols]),
        columns_of(grad_gate_up[:, :, hidden_cols:]),
        columns_of(grad_down).T,
        gain_grads[0],
        gain_grads[1],
    )


def solution(mesh):
    token_spec = P("fsdp", "seq", None)
    row_spec = P(AXES, None)
    column_spec = P(None, AXES)
    gain_spec = P(AXES)
    return jax.shard_map(
        shards,
        mesh=mesh,
        in_specs=(
            token_spec,
            P("fsdp", None),
            row_spec,
            row_spec,
            row_spec,
            column_spec,
            row_spec,
            row_spec,
            column_spec,
            gain_spec,
            gain_spec,
            token_spec,
        ),
        out_specs=(
            token_spec,
            token_spec,
            row_spec,
            row_spec,
            row_spec,
            column_spec,
            row_spec,
            row_spec,
            column_spec,
            gain_spec,
            gain_spec,
        ),
        check_vma=False,
    )
```

```python
import functools

import jax
import jax.numpy as jnp
from jax import lax
from jax.experimental import pallas as pl
from jax.experimental.pallas import tpu as pltpu
from jax.sharding import PartitionSpec as P

HEADS = 32
KV = 4
HD = 64
EPSILON = 1e-05
ROPE_BASE = 10000.0
MASKED = -1e30
GROUP = 4
AXES = ("fsdp", "seq")
BF = jnp.bfloat16
F32 = jnp.float32


def contract(left, right, left_dim, right_dim):
    return lax.dot_general(
        left, right, (((left_dim,), (right_dim,)), ((), ())), preferred_element_type=F32
    )


def rotary_tables(offsets):
    half_dim = HD // 2
    frequency = ROPE_BASE ** (-(jnp.arange(half_dim, dtype=F32) / half_dim))
    angles = frequency[:, None] * offsets.astype(F32)[None, :]
    return (jnp.cos(angles), jnp.sin(angles))


def rotate(values, cos_table, sine_table):
    half_dim = HD // 2
    front_half = values[:, :half_dim]
    back_half = values[:, half_dim:]
    return jnp.concatenate(
        [
            front_half * cos_table - back_half * sine_table,
            back_half * cos_table + front_half * sine_table,
        ],
        axis=1,
    )


def unrotate(grads_in, cos_table, sine_table):
    return rotate(grads_in, cos_table, -sine_table)


def swap_pair(flag, pair):
    return [jnp.where(flag == 1, pair[1], pair[0]), jnp.where(flag == 1, pair[0], pair[1])]


def forward_kernel(
    meta, query_ref, keyval_ref, first_ref, out_ref, lse_ref, q_all, top, total, acc, *, rows, heads, pair
):
    cell = pl.program_id(0)
    lowest, highest, key_base, first_most, query_at = (meta[cell, i] for i in range(5))
    for head in range(heads):
        q_all[:, head * rows : (head + 1) * rows] = query_ref[head]
    top[...] = jnp.full_like(top, MASKED)
    total[...] = jnp.zeros_like(total)
    acc[...] = jnp.zeros_like(acc)
    width = pair * rows

    def visit(block, masked):
        start = pl.multiple_of(block * rows, rows)
        keyval = keyval_ref[pl.ds(start, rows), :]
        key = keyval[:, :HD]
        value_t = keyval[:, HD:].T
        if masked:
            key_at = key_base + start + lax.broadcasted_iota(jnp.int32, (rows, rows), 0)
            token_at = query_at + lax.broadcasted_iota(jnp.int32, (rows, rows), 1)
            allowed = (key_at <= token_at) & (key_at >= first_ref[0])
            bias = jnp.where(allowed, 0.0, MASKED)
            bias = jnp.concatenate([bias] * pair, axis=1)
        for piece in range(heads // pair):
            cols = slice(piece * width, (piece + 1) * width)
            score = contract(key, q_all[:, cols], 1, 0)
            if masked:
                score = score + bias
            before = top[:, cols]
            now = jnp.maximum(before, jnp.max(score, axis=0, keepdims=True))
            weight = jnp.exp(score - now)
            decay = jnp.exp(before - now)
            top[:, cols] = now
            total[:, cols] = total[:, cols] * decay + jnp.sum(weight, axis=0, keepdims=True)
            acc[:, cols] = acc[:, cols] * decay + contract(value_t, weight.astype(BF), 1, 0)

    def step(block, carry):
        plain = jnp.logical_and(key_base + block * rows >= first_most, block < highest)

        @pl.when(plain)
        def _():
            visit(block, False)

        @pl.when(jnp.logical_not(plain))
        def _():
            visit(block, True)

        return carry

    lax.fori_loop(lowest, highest + 1, step, 0)
    sums = total[...]
    scaled = acc[...] * (1.0 / sums)
    for head in range(heads):
        out_ref[head] = scaled[:, head * rows : (head + 1) * rows].astype(BF)
    lse_ref[0] = top[...] + jnp.log(sums)


def backward_kernel(
    meta,
    query_ref,
    keyval_ref,
    first_ref,
    out_ref,
    lse_ref,
    grad_ref,
    dquery_ref,
    dkeyval_ref,
    q_all,
    g_all,
    delta,
    dq_acc,
    dkv_acc,
    *,
    rows,
    heads,
    pair,
):
    cell = pl.program_id(0)
    lowest, highest, key_base, first_most, query_at = (meta[cell, i] for i in range(5))
    for head in range(heads):
        cols = slice(head * rows, (head + 1) * rows)
        q_all[:, cols] = query_ref[head]
        g_all[:, cols] = grad_ref[head]
        delta[:, cols] = jnp.sum(
            grad_ref[head].astype(F32) * out_ref[head].astype(F32), axis=0, keepdims=True
        )
    dq_acc[...] = jnp.zeros_like(dq_acc)

    @pl.when(cell == 0)
    def _():
        dkv_acc[...] = jnp.zeros_like(dkv_acc)

    width = pair * rows

    def visit(block, masked):
        start = pl.multiple_of(block * rows, rows)
        keyval = keyval_ref[pl.ds(start, rows), :]
        key = keyval[:, :HD]
        value = keyval[:, HD:]
        key_t = key.T
        if masked:
            key_at = key_base + start + lax.broadcasted_iota(jnp.int32, (rows, rows), 0)
            token_at = query_at + lax.broadcasted_iota(jnp.int32, (rows, rows), 1)
            allowed = (key_at <= token_at) & (key_at >= first_ref[0])
            bias = jnp.where(allowed, 0.0, MASKED)
            bias = jnp.concatenate([bias] * pair, axis=1)
        dkey = jnp.zeros((rows, HD), F32)
        dvalue = jnp.zeros((rows, HD), F32)
        for piece in range(heads // pair):
            cols = slice(piece * width, (piece + 1) * width)
            score = contract(key, q_all[:, cols], 1, 0)
            if masked:
                score = score + bias
            weight = jnp.exp(score - lse_ref[0, :, cols])
            dweight = contract(value, g_all[:, cols], 1, 0)
            dscore = (weight * (dweight - delta[:, cols])).astype(BF)
            dq_acc[:, cols] = dq_acc[:, cols] + contract(key_t, dscore, 1, 0)
            dkey = dkey + contract(dscore, q_all[:, cols], 1, 1)
            dvalue = dvalue + contract(weight.astype(BF), g_all[:, cols], 1, 1)
        dkv_acc[pl.ds(start, rows), :] = dkv_acc[pl.ds(start, rows), :] + jnp.concatenate(
            [dkey, dvalue], axis=1
        )

    def step(block, carry):
        plain = jnp.logical_and(key_base + block * rows >= first_most, block < highest)

        @pl.when(plain)
        def _():
            visit(block, False)

        @pl.when(jnp.logical_not(plain))
        def _():
            visit(block, True)

        return carry

    lax.fori_loop(lowest, highest + 1, step, 0)
    scaled = dq_acc[...] * HD ** (-0.5)
    for head in range(heads):
        dquery_ref[head] = scaled[:, head * rows : (head + 1) * rows].astype(BF)

    @pl.when(cell == 1)
    def _():
        dkeyval_ref[...] = dkv_acc[...].astype(BF)


def attention_specs(rows, heads, keys):
    return dict(
        head=pl.BlockSpec((heads, HD, rows), lambda cell, meta: (0, 0, cell)),
        keyval=pl.BlockSpec((keys, 2 * HD), lambda cell, meta: (0, 0)),
        first=pl.BlockSpec((1, 1, rows), lambda cell, meta: (cell, 0, 0)),
        stat=pl.BlockSpec((1, 1, heads * rows), lambda cell, meta: (cell, 0, 0)),
    )


def attend_forward(meta, query, keyval, first):
    heads, _, tokens = query.shape
    rows = tokens // 2
    keys = keyval.shape[0]
    specs = attention_specs(rows, heads, keys)
    wide = heads * rows
    return pl.pallas_call(
        functools.partial(forward_kernel, rows=rows, heads=heads, pair=4),
        grid_spec=pltpu.PrefetchScalarGridSpec(
            num_scalar_prefetch=1,
            grid=(2,),
            in_specs=[specs["head"], specs["keyval"], specs["first"]],
            out_specs=[specs["head"], specs["stat"]],
            scratch_shapes=[
                pltpu.VMEM((HD, wide), BF),
                pltpu.VMEM((1, wide), F32),
                pltpu.VMEM((1, wide), F32),
                pltpu.VMEM((HD, wide), F32),
            ],
        ),
        out_shape=(
            jax.ShapeDtypeStruct(query.shape, BF),
            jax.ShapeDtypeStruct((2, 1, wide), F32),
        ),
        compiler_params=pltpu.CompilerParams(
            dimension_semantics=("arbitrary",), vmem_limit_bytes=48 * 1024 * 1024
        ),
        cost_estimate=pl.CostEstimate(
            flops=40_000_000_000, bytes_accessed=10_000_000, transcendentals=0
        ),
        name="attend_forward",
    )(meta, query, keyval, first)


def attend_backward(meta, query, keyval, first, out, lse, grad):
    heads, _, tokens = query.shape
    rows = tokens // 2
    keys = keyval.shape[0]
    specs = attention_specs(rows, heads, keys)
    wide = heads * rows
    return pl.pallas_call(
        functools.partial(backward_kernel, rows=rows, heads=heads, pair=4),
        grid_spec=pltpu.PrefetchScalarGridSpec(
            num_scalar_prefetch=1,
            grid=(2,),
            in_specs=[
                specs["head"],
                specs["keyval"],
                specs["first"],
                specs["head"],
                specs["stat"],
                specs["head"],
            ],
            out_specs=[specs["head"], specs["keyval"]],
            scratch_shapes=[
                pltpu.VMEM((HD, wide), BF),
                pltpu.VMEM((HD, wide), BF),
                pltpu.VMEM((1, wide), F32),
                pltpu.VMEM((HD, wide), F32),
                pltpu.VMEM((keys, 2 * HD), F32),
            ],
        ),
        out_shape=(
            jax.ShapeDtypeStruct(query.shape, BF),
            jax.ShapeDtypeStruct(keyval.shape, BF),
        ),
        compiler_params=pltpu.CompilerParams(
            dimension_semantics=("arbitrary",), vmem_limit_bytes=48 * 1024 * 1024
        ),
        cost_estimate=pl.CostEstimate(
            flops=80_000_000_000, bytes_accessed=16_000_000, transcendentals=0
        ),
        name="attend_backward",
    )(meta, query, keyval, first, out, lse, grad)


def feed_kernel(normed, cotangent, w_gate_up, w_down_t, *rest, columns):
    hidden, d_gate_up = rest[-2:]
    step = 256
    for low in range(0, columns, step):
        high = min(low + step, columns)
        gate = contract(normed[...], w_gate_up[:, low:high], 1, 0)
        up = contract(normed[...], w_gate_up[:, columns + low : columns + high], 1, 0)
        d_hidden = contract(cotangent[...], w_down_t[:, low:high], 1, 0)
        sigmoid = 1.0 / (1.0 + jnp.exp(-gate))
        silu = gate * sigmoid
        hidden[:, low:high] = (silu * up).astype(BF)
        d_gate_up[:, low:high] = (
            d_hidden * up * sigmoid * (1.0 + gate * (1.0 - sigmoid))
        ).astype(BF)
        d_gate_up[:, columns + low : columns + high] = (d_hidden * silu).astype(BF)


def feed_forward(normed, cotangent, w_gate_up, w_down_t, halves, before=()):
    tokens, width = cotangent.shape[0] // 2, cotangent.shape[1]
    columns = w_down_t.shape[1]
    tile = min(256, tokens)
    shifts = [half * (tokens // tile) for half in halves]

    def token_spec(shift):
        return pl.BlockSpec((tile, width), lambda i: (i + shift, 0))

    def weight_spec(wide):
        return pl.BlockSpec((width, wide), lambda i: (0, 0), pipeline_mode=pl.Buffered(1))

    def out_spec(wide):
        return pl.BlockSpec((tile, wide), lambda i: (i + shifts[2], 0))

    return pl.pallas_call(
        functools.partial(feed_kernel, columns=columns),
        grid=(tokens // tile,),
        in_specs=[
            token_spec(shifts[0]),
            token_spec(shifts[1]),
            weight_spec(2 * columns),
            weight_spec(columns),
            *[pl.BlockSpec(memory_space=pl.ANY) for _ in before],
        ],
        out_specs=(out_spec(columns), out_spec(2 * columns)),
        out_shape=(
            jax.ShapeDtypeStruct((2 * tokens, columns), BF),
            jax.ShapeDtypeStruct((2 * tokens, 2 * columns), BF),
        ),
        input_output_aliases={4 + i: i for i in range(len(before))},
        compiler_params=pltpu.CompilerParams(
            dimension_semantics=("arbitrary",), vmem_limit_bytes=56 * 1024 * 1024
        ),
        cost_estimate=pl.CostEstimate(
            flops=6 * tokens * width * columns, bytes_accessed=6 * width * columns, transcendentals=0
        ),
        name="feed_forward",
    )(normed, cotangent, w_gate_up, w_down_t, *before)


def opening_kernel(
    tokens,
    quarters_attn,
    quarters_down,
    quarters_gate_up,
    group,
    whole_attn,
    whole_down,
    whole_gate_up,
    local_sem,
    near_send,
    near_recv,
    swap_send,
    swap_recv,
    hop_send,
    hop_recv,
    *,
    wide,
    deep,
    own_rows,
):
    ring, half_ring = wide * deep, wide * deep // 2
    f_at, s_at = lax.axis_index("fsdp"), lax.axis_index("seq")
    y_at, x_at, z_at, c_at = f_at // 2, lax.rem(f_at, 2), s_at // 2, lax.rem(s_at, 2)
    here = y_at * deep + jnp.where(lax.rem(y_at, 2) == 0, z_at, deep - 1 - z_at)

    def ring_place(offset):
        index = lax.rem(here + offset + 2 * ring, ring)
        row, col = index // deep, lax.rem(index, deep)
        return row, jnp.where(lax.rem(row, 2) == 0, col, deep - 1 - col)

    def ring_device(offset):
        row, col = ring_place(offset)
        return row * 2 + x_at, col * 2 + c_at

    moves = ((0, 1), (1, 0), (1, 1))

    def other(dx, dc):
        return lax.rem(x_at + dx, 2), lax.rem(c_at + dc, 2)

    def group_device(dx, dc):
        x, c = other(dx, dc)
        return y_at * 2 + x, z_at * 2 + c

    def remote(source, target, send, recv, device):
        return pltpu.make_async_remote_copy(
            src_ref=source,
            dst_ref=target,
            send_sem=send,
            recv_sem=recv,
            device_id=device,
            device_id_type=pl.DeviceIdType.MESH,
        )

    barrier = pltpu.get_barrier_semaphore()
    partners = [group_device(*move) for move in moves] + [ring_device(1), ring_device(-1)]
    for device in partners:
        pl.semaphore_signal(barrier, inc=1, device_id=device, device_id_type=pl.DeviceIdType.MESH)
    pl.semaphore_wait(barrier, len(partners))

    my_rows = pl.ds(pl.multiple_of(c_at * own_rows, own_rows), own_rows)
    targets = (
        whole_attn.at[y_at, x_at, z_at, my_rows],
        whole_down.at[y_at, x_at, z_at, my_rows],
        whole_gate_up.at[y_at, x_at, z_at, my_rows],
    )
    quarters = (quarters_attn, quarters_down, quarters_gate_up)
    locals_ = [
        pltpu.make_async_copy(quarters[i].at[x_at * 2 + c_at], targets[i], local_sem.at[i])
        for i in range(3)
    ] + [pltpu.make_async_copy(tokens, group.at[0], local_sem.at[3])]

    def swaps(i):
        copies = []
        for j, (dx, dc) in enumerate(moves):
            x, c = other(dx, dc)
            copies.append(
                remote(
                    quarters[i].at[x * 2 + c],
                    targets[i],
                    swap_send.at[i, j],
                    swap_recv.at[i, j],
                    group_device(dx, dc),
                )
            )
        return copies

    swap = [swaps(i) for i in range(3)]
    to_core = remote(tokens, group.at[1], near_send.at[0], near_recv.at[0], group_device(0, 1))
    to_x = remote(tokens, group.at[2], near_send.at[1], near_recv.at[1], group_device(1, 0))
    far_to_core = remote(
        group.at[2], group.at[3], near_send.at[2], near_recv.at[2], group_device(0, 1)
    )
    wholes = (whole_attn, whole_down)

    def hop(i, direction, step):
        row, col = ring_place(-direction * (step - 1))
        if step < half_ring:
            part = wholes[i].at[row, :, col]
        else:
            part = wholes[i].at[row, 0 if direction == 1 else 1, col]
        side = 0 if direction == 1 else 1
        return remote(
            part,
            part,
            hop_send.at[i, side, step - 1],
            hop_recv.at[i, side, step - 1],
            ring_device(direction),
        )

    hops = [
        [[hop(i, direction, step) for direction in (1, -1)] for step in range(1, half_ring + 1)]
        for i in range(2)
    ]

    for copy in locals_:
        copy.start()
    for copy in swap[0]:
        copy.start()
    for copy in swap[1]:
        copy.start()
    to_core.start()
    to_x.start()
    for copy in swap[2]:
        copy.start()
    for i in range(2):
        locals_[i].wait()
        for copy in swap[i]:
            copy.wait_recv()
    for i in range(2):
        for step in range(half_ring):
            if i == 0 or step > 0:
                for copy in hops[i][step]:
                    copy.start()
            if i == 0 and step == half_ring - 1:
                for copy in hops[1][0]:
                    copy.start()
            for copy in hops[i][step]:
                copy.wait_recv()
            if i == 0 and step == half_ring - 1:
                to_x.wait_recv()
                far_to_core.start()
    for copy in locals_[2:]:
        copy.wait()
    for copy in swap[2] + [to_core, far_to_core]:
        copy.wait_recv()
    for copy in swap[0] + swap[1] + swap[2] + [to_core, to_x, far_to_core]:
        copy.wait_send()
    for i in range(2):
        for pair in hops[i]:
            for copy in pair:
                copy.wait_send()


def opening(tokens, quarters_attn, quarters_down, quarters_gate_up, wide, deep):
    own_rows = quarters_attn.shape[1]
    half_ring = wide * deep // 2

    def whole(quarters):
        return jax.ShapeDtypeStruct((wide, 2, deep, 2 * own_rows, quarters.shape[2]), BF)

    anywhere = pl.BlockSpec(memory_space=pl.ANY)
    return pl.pallas_call(
        functools.partial(opening_kernel, wide=wide, deep=deep, own_rows=own_rows),
        out_shape=(
            jax.ShapeDtypeStruct((GROUP, *tokens.shape), BF),
            whole(quarters_attn),
            whole(quarters_down),
            whole(quarters_gate_up),
        ),
        in_specs=[anywhere] * 4,
        out_specs=(anywhere,) * 4,
        scratch_shapes=[
            pltpu.SemaphoreType.DMA((4,)),
            pltpu.SemaphoreType.DMA((3,)),
            pltpu.SemaphoreType.DMA((3,)),
            pltpu.SemaphoreType.DMA((3, 3)),
            pltpu.SemaphoreType.DMA((3, 3)),
            pltpu.SemaphoreType.DMA((2, 2, half_ring)),
            pltpu.SemaphoreType.DMA((2, 2, half_ring)),
        ],
        compiler_params=pltpu.CompilerParams(collective_id=0, has_side_effects=True),
        name="opening",
    )(tokens, quarters_attn, quarters_down, quarters_gate_up)


def closing_kernel(
    partial,
    near_part,
    far_part,
    chunk_gate_up,
    chunk_down,
    d_normed,
    owned_attn,
    owned_gate_up,
    owned_down,
    land,
    chunk_attn,
    core_land,
    x_stage,
    x_land,
    local_sem,
    near_send,
    near_recv,
    swap_send,
    swap_recv,
    hop_send,
    hop_recv,
    *,
    wide,
    deep,
    own_rows,
):
    ring, half_ring = wide * deep, wide * deep // 2
    f_at, s_at = lax.axis_index("fsdp"), lax.axis_index("seq")
    y_at, x_at, z_at, c_at = f_at // 2, lax.rem(f_at, 2), s_at // 2, lax.rem(s_at, 2)
    here = y_at * deep + jnp.where(lax.rem(y_at, 2) == 0, z_at, deep - 1 - z_at)

    def ring_place(offset):
        index = lax.rem(here + offset + 2 * ring, ring)
        row, col = index // deep, lax.rem(index, deep)
        return row, jnp.where(lax.rem(row, 2) == 0, col, deep - 1 - col)

    def ring_device(offset):
        row, col = ring_place(offset)
        return row * 2 + x_at, col * 2 + c_at

    moves = ((0, 1), (1, 0), (1, 1))

    def other(dx, dc):
        return lax.rem(x_at + dx, 2), lax.rem(c_at + dc, 2)

    def group_device(dx, dc):
        x, c = other(dx, dc)
        return y_at * 2 + x, z_at * 2 + c

    def remote(source, target, send, recv, device):
        return pltpu.make_async_remote_copy(
            src_ref=source,
            dst_ref=target,
            send_sem=send,
            recv_sem=recv,
            device_id=device,
            device_id_type=pl.DeviceIdType.MESH,
        )

    barrier = pltpu.get_barrier_semaphore()
    partners = [group_device(*move) for move in moves] + [ring_device(1), ring_device(-1)]
    for device in partners:
        pl.semaphore_signal(barrier, inc=1, device_id=device, device_id_type=pl.DeviceIdType.MESH)
    pl.semaphore_wait(barrier, len(partners))

    rows = x_land.shape[0]
    far_core = remote(
        far_part.at[rows:], core_land.at[0], near_send.at[0], near_recv.at[0], group_device(0, 1)
    )
    near_core = remote(
        near_part.at[rows:], core_land.at[1], near_send.at[1], near_recv.at[1], group_device(0, 1)
    )
    far_x = remote(x_stage, x_land, near_send.at[2], near_recv.at[2], group_device(1, 0))

    def hop(side, step):
        direction = 1 - 2 * side
        if step == 1:
            row, col = ring_place(direction * half_ring)
            source, target = partial.at[row, side, col], land.at[side, 0, side]
        else:
            source, target = land.at[side, step - 2], land.at[side, step - 1]
        return remote(
            source,
            target,
            hop_send.at[side, step - 1],
            hop_recv.at[side, step - 1],
            ring_device(direction),
        )

    chunks = (chunk_attn, chunk_gate_up, chunk_down)
    owned = (owned_attn, owned_gate_up, owned_down)

    def piece(i, x, c):
        return chunks[i].at[x, pl.ds(pl.multiple_of(c * own_rows, own_rows), own_rows)]

    def swaps(i):
        copies = []
        for j, (dx, dc) in enumerate(moves):
            copies.append(
                remote(
                    piece(i, *other(dx, dc)),
                    owned[i].at[x_at * 2 + c_at],
                    swap_send.at[i, j],
                    swap_recv.at[i, j],
                    group_device(dx, dc),
                )
            )
        return copies

    swap = [swaps(i) for i in range(3)]
    keep = [
        pltpu.make_async_copy(piece(i, x_at, c_at), owned[i].at[x_at * 2 + c_at], local_sem.at[i])
        for i in range(3)
    ]

    far_core.start()
    near_core.start()
    for side in range(2):
        hop(side, 1).start()
    far_core.wait_recv()
    x_stage[...] = (far_part[:rows].astype(F32) + core_land[0].astype(F32)).astype(BF)
    far_x.start()
    for i in (1, 2):
        for copy in swap[i]:
            copy.start()
        keep[i].start()
    for step in range(2, half_ring + 1):
        for side in range(2):
            hop(side, step - 1).wait_recv()
            row, col = ring_place((1 - 2 * side) * (half_ring - step + 1))
            if step == 2:
                mine = partial[row, side, col].astype(F32) + land[side, 0, side].astype(F32)
                land[side, 0, side] = mine.astype(BF)
                land[side, 0, 1 - side] = partial[row, 1 - side, col]
            else:
                for half in range(2):
                    mine = partial[row, half, col].astype(F32)
                    mine = mine + land[side, step - 2, half].astype(F32)
                    land[side, step - 2, half] = mine.astype(BF)
            hop(side, step).start()
    near_core.wait_recv()
    for side in range(2):
        hop(side, half_ring).wait_recv()
    for half in range(2):
        total = partial[y_at, half, z_at].astype(F32) + land[0, half_ring - 1, half].astype(F32)
        total = total + land[1, half_ring - 1, half].astype(F32)
        chunk_attn[half] = total.astype(BF)
    for copy in swap[0]:
        copy.start()
    keep[0].start()
    far_x.wait_recv()
    d_normed[...] = (
        near_part[:rows].astype(F32) + core_land[1].astype(F32) + x_land[...].astype(F32)
    )
    for i in (1, 2, 0):
        keep[i].wait()
        for copy in swap[i]:
            copy.wait_recv()
    for copy in swap[0] + swap[1] + swap[2] + [far_core, near_core, far_x]:
        copy.wait_send()
    for side in range(2):
        for step in range(1, half_ring + 1):
            hop(side, step).wait_send()


def closing(partial, near_part, far_part, chunk_gate_up, chunk_down, wide, deep):
    own_rows = partial.shape[3] // 2
    half_ring = wide * deep // 2
    rows, width = near_part.shape[0] // 2, near_part.shape[1]
    columns = partial.shape[4]
    anywhere = pl.BlockSpec(memory_space=pl.ANY)
    vmem = pl.BlockSpec(memory_space=pltpu.VMEM)

    def quarters(wanted):
        return jax.ShapeDtypeStruct((GROUP, own_rows, wanted), BF)

    return pl.pallas_call(
        functools.partial(closing_kernel, wide=wide, deep=deep, own_rows=own_rows),
        out_shape=(
            jax.ShapeDtypeStruct((rows, width), F32),
            quarters(columns),
            quarters(chunk_gate_up.shape[2]),
            quarters(chunk_down.shape[2]),
        ),
        in_specs=[vmem, vmem, vmem, anywhere, anywhere],
        out_specs=(vmem, anywhere, anywhere, anywhere),
        scratch_shapes=[
            pltpu.VMEM((2, half_ring, 2, 2 * own_rows, columns), BF),
            pltpu.VMEM((2, 2 * own_rows, columns), BF),
            pltpu.VMEM((2, rows, width), BF),
            pltpu.VMEM((rows, width), BF),
            pltpu.VMEM((rows, width), BF),
            pltpu.SemaphoreType.DMA((3,)),
            pltpu.SemaphoreType.DMA((3,)),
            pltpu.SemaphoreType.DMA((3,)),
            pltpu.SemaphoreType.DMA((3, 3)),
            pltpu.SemaphoreType.DMA((3, 3)),
            pltpu.SemaphoreType.DMA((2, half_ring)),
            pltpu.SemaphoreType.DMA((2, half_ring)),
        ],
        compiler_params=pltpu.CompilerParams(
            collective_id=1, has_side_effects=True, vmem_limit_bytes=56 * 1024 * 1024
        ),
        name="closing",
    )(partial, near_part, far_part, chunk_gate_up, chunk_down)


def shards(
    tokens,
    starts,
    w_query,
    w_key,
    w_value,
    w_out,
    w_gate,
    w_up,
    w_down,
    norm_attn,
    norm_mlp,
    cotangent,
):
    seq_count = lax.axis_size("seq")
    fsdp_count = lax.axis_size("fsdp")
    deep = seq_count // 2
    wide = fsdp_count // 2
    ring = wide * deep
    half_ring = ring // 2
    f_at, s_at = lax.axis_index("fsdp"), lax.axis_index("seq")
    x_at, y_at, c_at, z_at = f_at % 2, f_at // 2, s_at % 2, s_at // 2
    rows = tokens.shape[1]
    width = tokens.shape[2]
    own_rows = w_query.shape[0]

    def perm_of(move):
        found = []
        for f in range(fsdp_count):
            for s in range(seq_count):
                target = move(f // 2, f % 2, s // 2, s % 2)
                if target is not None:
                    ty, tx, tz, tc = target
                    found.append((f * seq_count + s, (ty * 2 + tx) * seq_count + tz * 2 + tc))
        return found

    def ring_place(position):
        position = position % ring
        row, col = position // deep, position % deep
        return row, col if row % 2 == 0 else deep - 1 - col

    def ring_index(y, z):
        return y * deep + (z if y % 2 == 0 else deep - 1 - z)

    def around(step):
        def move(y, x, z, c):
            ty, tz = ring_place(ring_index(y, z) + step)
            return ty, x, tz, c

        return move

    def along(step):
        return lambda y, x, z, c: (y, x, z + step, c) if 0 <= z + step < deep else None

    core_perm = perm_of(lambda y, x, z, c: (y, x, z, 1 - c))
    x_perm = perm_of(lambda y, x, z, c: (y, 1 - x, z, c))
    cross_perm = perm_of(lambda y, x, z, c: (y, 1 - x, z, 1 - c))
    right_perm, left_perm = perm_of(around(1)), perm_of(around(-1))

    def send(value, perm):
        return lax.ppermute(value, AXES, perm)

    position = y_at * deep + jnp.where(y_at % 2 == 0, z_at, deep - 1 - z_at)

    def place_at(offset):
        index = lax.rem(position + offset + 2 * ring, ring)
        row, col = index // deep, index % deep
        return row, jnp.where(row % 2 == 0, col, deep - 1 - col)

    def with_core(block):
        return jnp.concatenate([block, send(block, core_perm)], axis=0)

    def gather_group(block):
        return [with_core(block), with_core(send(block, x_perm))]

    def to_quarters(pieces):
        return jnp.concatenate(
            [p.reshape(own_rows, GROUP, -1).transpose(1, 0, 2) for p in pieces], axis=2
        )

    def absolute(got):
        rows_of = [swap_pair(c_at, pair) for pair in got]
        ordered = [swap_pair(x_at, [rows_of[0][c], rows_of[1][c]]) for c in range(2)]
        return [[ordered[0][x], ordered[1][x]] for x in range(2)]

    class Gather:
        def __init__(self, room):
            self.room = room
            row, col = place_at(0)
            size = (1, 2, 1, *room.shape[3:])
            chunk = lax.dynamic_slice(room, (row, 0, col, 0, 0), size).reshape(2, *room.shape[3:])
            self.right = self.left = chunk
            self.step, self.got = 0, []

        def advance(self, times):
            for _ in range(min(times, half_ring - self.step)):
                self.step += 1
                if self.step < half_ring:
                    self.right = send(self.right, right_perm)
                    self.left = send(self.left, left_perm)
                    self.got += [(-self.step, 0, self.right), (self.step, 0, self.left)]
                else:
                    self.got += [
                        (half_ring, 0, send(self.right[:1], right_perm)),
                        (half_ring, 1, send(self.left[1:], left_perm)),
                    ]

        def wait_for(self, value):
            self.right, self.left = after((self.right, self.left), value)

        def whole(self):
            result = self.room
            for offset, x_from, piece in self.got:
                row, col = place_at(offset)
                result = lax.dynamic_update_slice(
                    result, piece[None, :, None], (row, x_from, col, 0, 0)
                )
            return result.reshape(-1, result.shape[4])

    class Scatter:
        def __init__(self, partial):
            self.parts = partial.reshape(wide, 2, deep, 2 * own_rows, partial.shape[1])
            self.step, self.right, self.left = 0, None, None

        def part(self, offset, x_from=0, x_count=2):
            row, col = place_at(offset)
            return lax.dynamic_slice(
                self.parts,
                (row, x_from, col, 0, 0),
                (1, x_count, 1, 2 * own_rows, self.parts.shape[4]),
            ).reshape(x_count, 2 * own_rows, self.parts.shape[4])

        def advance(self, times):
            for _ in range(min(times, half_ring - self.step)):
                self.step += 1
                offset = half_ring - self.step + 1
                if self.step == 1:
                    to_right, to_left = self.part(offset, 0, 1), self.part(-offset, 1, 1)
                else:
                    to_right, to_left = self.joined(offset, -offset)
                self.right = send(to_right, right_perm)
                self.left = send(to_left, left_perm)

        def joined(self, at_right, at_left):
            to_right, to_left = self.part(at_right), self.part(at_left)
            if self.step == 2:
                to_right = jnp.concatenate([add_low(to_right[:1], self.right), to_right[1:]])
                to_left = jnp.concatenate([to_left[:1], add_low(to_left[1:], self.left)])
                return to_right, to_left
            return add_low(to_right, self.right), add_low(to_left, self.left)

        def wait_for(self, value):
            self.right, self.left = after((self.right, self.left), value)

        def result(self):
            self.advance(half_ring)
            own = self.part(0).astype(F32)
            if half_ring > 1:
                return own + self.right.astype(F32) + self.left.astype(F32)
            return own + jnp.concatenate([self.right, self.left]).astype(F32)

    def stage(moving, values):
        ends = [(member.right, member.left) for member in moving]
        ends, values = lax.optimization_barrier((ends, values))
        for member, (right, left) in zip(moving, ends):
            member.right, member.left = right, left
        return values

    def add_low(one, other):
        return (one.astype(F32) + other.astype(F32)).astype(BF)

    per_window = -(-half_ring // 4)

    def columns_of(quarters):
        return quarters.transpose(1, 0, 2).reshape(own_rows, -1)

    def reduce_core(partial):
        return partial[:rows].astype(F32) + send(partial[rows:], core_perm).astype(F32)

    def send_far(partial):
        return send(reduce_core(partial).astype(BF), x_perm).astype(F32)

    index = f_at * seq_count + s_at
    count = fsdp_count * seq_count
    doublings = [
        (bit, [(i, i ^ (1 << bit)) for i in range(count)]) for bit in range(count.bit_length() - 1)
    ]

    def sum_small(value):
        for bit, perm in doublings:
            value = value + send(value, perm)
        return value

    def after(value, other):
        return lax.optimization_barrier((value, other))[0]

    q_cols = HEADS // GROUP * HD
    qkv_cols = q_cols + 2 * HD
    hidden_cols = w_gate.shape[1] // GROUP
    start_rows = [starts[0], send(starts, x_perm)[0]]
    block_at = [rows * (2 * z_at + (c_at ^ dc)) for dc in range(2)]
    within = jnp.arange(rows, dtype=jnp.int32)
    base_block = 2 * (z_at - deep + 1)
    places = jnp.concatenate([block_at[dc] + within for dc in range(2)])[None]
    both_starts = jnp.stack(start_rows)
    both_firsts = jnp.zeros((2, 2 * rows), jnp.int32)
    for slot in range(both_starts.shape[1]):
        start = both_starts[:, slot : slot + 1]
        both_firsts = jnp.maximum(both_firsts, jnp.where(start <= places, start, 0))
    tables, first_rows, metas = [], [], []
    for dx in range(2):
        tables.append(rotary_tables((places - both_firsts)[dx]))
        firsts = [both_firsts[dx, dc * rows : (dc + 1) * rows] for dc in range(2)]
        first_rows.append(jnp.stack(firsts)[:, None, :])
        cells = [
            [
                firsts[dc][0] // rows - base_block,
                block_at[dc] // rows - base_block,
                base_block * rows,
                firsts[dc][rows - 1],
                block_at[dc],
            ]
            for dc in range(2)
        ]
        metas.append(jnp.stack([jnp.stack(cell) for cell in cells]).astype(jnp.int32))

    gain_columns = jnp.pad(jnp.stack([norm_attn, norm_mlp], axis=1), ((0, 0), (0, 126)))
    own_tokens, tables, first_rows, metas = after((tokens[0], tables, first_rows, metas), start_rows[1])
    own_tokens = after(own_tokens, (tables, first_rows, metas))
    group_blocks, whole_attn, whole_down, whole_gate_up = opening(
        own_tokens,
        to_quarters([w_query, w_key, w_value, w_out.T, jnp.tile(gain_columns, (1, GROUP))]),
        to_quarters([w_down.T]),
        to_quarters([w_gate, w_up]),
        wide,
        deep,
    )
    group_tokens = [group_blocks[2 * dx : 2 * dx + 2].reshape(2 * rows, width) for dx in range(2)]
    whole_attn = whole_attn.reshape(width, -1)
    w_down_t = whole_down.reshape(width, -1)
    w_qkv = whole_attn[:, :qkv_cols]
    w_out_t = whole_attn[:, qkv_cols : qkv_cols + q_cols]
    gains = whole_attn[:, qkv_cols + q_cols :].T.astype(F32)
    gain_attn, gain_mlp = gains[0], gains[1]
    ring_gate_up = Gather(whole_gate_up)
    rings = [ring_gate_up]

    def advance(members, times=per_window):
        for member in members:
            member.advance(times)

    advance(rings)
    own_cotangent = after(cotangent[0], group_blocks)
    far_cotangent = send(own_cotangent, x_perm)
    both_cotangent = jnp.concatenate(
        [own_cotangent, send(own_cotangent, core_perm), far_cotangent, send(far_cotangent, core_perm)]
    )

    heads = HEADS // GROUP
    normed, scales, queries, keyvals, attended, lses = ([None, None] for _ in range(6))
    for dx in (1, 0):
        group_inputs = group_tokens[dx].astype(F32)
        scales[dx] = lax.rsqrt(jnp.mean(group_inputs * group_inputs, axis=1, keepdims=True) + EPSILON)
        normed[dx] = (group_inputs * scales[dx] * gain_attn).astype(BF)
        pre = contract(w_qkv, normed[dx], 0, 1)
        turned = rotate(pre[:q_cols].reshape(heads, HD, -1), *tables[dx])
        queries[dx] = (turned * HD ** (-0.5)).astype(BF)
        key = rotate(pre[q_cols : q_cols + HD][None], *tables[dx])[0].astype(BF)
        keyval = jnp.concatenate([key, pre[q_cols + HD :].astype(BF)], axis=0).T
        keyval = jnp.concatenate(swap_pair(c_at, [keyval[:rows], keyval[rows:]]))
        earlier = [send(keyval, perm_of(along(step))) for step in range(deep - 1, 0, -1)]
        keyvals[dx] = jnp.concatenate(earlier + [keyval], axis=0)
    keyvals[1] = stage(rings, keyvals[1])
    advance(rings)
    attended[1], lses[1] = attend_forward(metas[1], queries[1], keyvals[1], first_rows[1])
    attended[1] = stage(rings, attended[1])
    advance(rings)
    far_sum = reduce_core(contract(attended[1].reshape(q_cols, -1), w_out_t, 0, 1).astype(BF)).astype(BF)
    far = send(far_sum, x_perm).astype(F32)
    query_near = after(queries[0], far_sum)
    attended[0], lses[0] = attend_forward(metas[0], query_near, keyvals[0], first_rows[0])
    attended[0] = stage(rings, attended[0])
    advance(rings, half_ring)
    attended[0], far = stage([], (attended[0], far))
    near = reduce_core(contract(attended[0].reshape(q_cols, -1), w_out_t, 0, 1).astype(BF))
    middle = own_tokens.astype(F32) + near + far
    attended_t = [a.reshape(q_cols, -1) for a in attended]

    scale_mlp = lax.rsqrt(jnp.mean(middle * middle, axis=1, keepdims=True) + EPSILON)
    normed_own = (middle * scale_mlp * gain_mlp).astype(BF)
    normed_far = send(normed_own, x_perm)
    normed_near = [normed_own, send(normed_own, core_perm)]
    w_gate_up = ring_gate_up.whole()
    normed_near, both_cotangent = stage([], (normed_near, both_cotangent))
    both = feed_forward(
        jnp.concatenate(normed_near), both_cotangent, w_gate_up, w_down_t, (0, 0, 0)
    )
    normed_far, both = stage([], (normed_far, both))
    both_normed = jnp.concatenate([*normed_near, normed_far, send(normed_far, core_perm)])
    both = feed_forward(both_normed, both_cotangent, w_gate_up, w_down_t, (1, 1, 1), both)
    both_hidden, both_d_gate_up = both
    hidden = [both_hidden[: 2 * rows], both_hidden[2 * rows :]]
    d_gate_up = [both_d_gate_up[: 2 * rows], both_d_gate_up[2 * rows :]]
    far_part = contract(d_gate_up[1], w_gate_up, 1, 1).astype(BF)
    far_sum = reduce_core(far_part).astype(BF)
    far = send(far_sum, x_perm)
    near_part = contract(after(d_gate_up[0], far_part), w_gate_up, 1, 1).astype(BF)
    near = reduce_core(near_part)
    both_hidden = after(both_hidden, (near_part, far_sum))
    ring_down = Scatter(contract(both_cotangent, both_hidden, 0, 0).astype(BF))
    ring_down.advance(per_window)
    both_d_gate_up = after(both_d_gate_up, ring_down.parts)
    ring_gate_up = Scatter(contract(both_normed, both_d_gate_up, 0, 0).astype(BF))
    far, ring_gate_up.parts = stage([ring_down], (far, ring_gate_up.parts))
    far = far.astype(F32)
    ring_gate_up.advance(per_window)
    d_normed_mlp = near + far

    def norm_backward(values, scale_rows, gain, grads_in):
        weighted = grads_in * gain
        inner_mean = jnp.mean(weighted * values, axis=1, keepdims=True)
        cube = scale_rows * scale_rows * scale_rows
        return scale_rows * weighted - values * cube * inner_mean

    gain_grad_mlp = jnp.sum(d_normed_mlp * middle * scale_mlp, axis=0)
    d_middle = norm_backward(middle, scale_mlp, gain_mlp, d_normed_mlp) + cotangent[0].astype(F32)
    rings = [ring_gate_up, ring_down]

    branch_own = d_middle.astype(BF)
    branch_far = send(branch_own, x_perm)
    d_branch = [with_core(branch_own), None]
    d_keyval, d_query = [None, None], [None, None]

    def d_attended(dx):
        return contract(w_out_t, d_branch[dx], 0, 1).astype(BF).reshape(queries[dx].shape)

    def keyval_home(d_keyvals):
        chunks = [d_keyvals[2 * rows * i : 2 * rows * (i + 1)] for i in range(deep)]
        total = chunks[deep - 1].astype(F32)
        came = [send(chunks[deep - 1 - step], perm_of(along(-step))) for step in range(1, deep)]
        for part in came:
            total = total + part.astype(F32)
        return jnp.concatenate(swap_pair(c_at, [total[:rows], total[rows:]])).T

    d_near = stage([ring_gate_up], d_attended(0))
    advance(rings)
    d_query[0], d_keyvals = attend_backward(
        metas[0], queries[0], keyvals[0], first_rows[0], attended[0], lses[0], d_near
    )
    d_query[0], d_keyvals, branch_far = stage(rings, (d_query[0], d_keyvals, branch_far))
    advance(rings)
    d_keyval[0] = keyval_home(d_keyvals)
    d_branch[1] = with_core(branch_far)
    result_part = contract(after(hidden[1], d_query[0]), w_down_t, 1, 1).astype(BF)
    result_sum = reduce_core(result_part).astype(BF)
    result_far = send(result_sum, x_perm).astype(F32)
    d_far = after(d_attended(1), (d_query[0], result_sum))
    d_query[1], d_keyvals = attend_backward(
        metas[1], queries[1], keyvals[1], first_rows[1], attended[1], lses[1], d_far
    )
    d_query[1], d_keyvals, d_keyval[0], result_far = stage(
        rings, (d_query[1], d_keyvals, d_keyval[0], result_far)
    )
    for member in rings:
        member.advance(half_ring)
    d_keyval[1] = keyval_home(d_keyvals)
    grad_out_part = contract(d_branch[0], attended_t[0], 0, 1) + contract(
        after(d_branch[1], d_query[1]), attended_t[1], 0, 1
    )
    result_near = reduce_core(contract(after(hidden[0], d_query[1]), w_down_t, 1, 1).astype(BF))
    result = middle + result_near + result_far

    d_pre = [None, None]
    for dx in range(2):
        d_query_pre = unrotate(d_query[dx].astype(F32), *tables[dx]).astype(BF)
        d_key_pre = unrotate(d_keyval[dx][None, :HD], *tables[dx])[0].astype(BF)
        d_value_pre = d_keyval[dx][HD:].astype(BF)
        d_pre[dx] = jnp.concatenate([d_query_pre.reshape(q_cols, -1), d_key_pre, d_value_pre])
    near_part = contract(d_pre[0], w_qkv, 0, 1).astype(BF)
    far_part = contract(d_pre[1], w_qkv, 0, 1).astype(BF)
    grad_qkv_part = contract(normed[0], d_pre[0], 0, 1) + contract(normed[1], d_pre[1], 0, 1)
    gain_grad_attn = sum(
        jnp.sum(part.astype(F32) * group_tokens[dx].astype(F32) * scales[dx], axis=0)
        for dx, part in enumerate((near_part, far_part))
    )
    gain_partial = jnp.pad(jnp.stack([gain_grad_attn, gain_grad_mlp], axis=1), ((0, 0), (0, 126)))
    partial = jnp.concatenate([grad_qkv_part, gain_partial, grad_out_part], axis=1).astype(BF)
    d_normed, grad_attn, grad_gate_up, grad_down = closing(
        partial.reshape(wide, 2, deep, 2 * own_rows, -1),
        near_part,
        far_part,
        ring_gate_up.result().astype(BF),
        ring_down.result().astype(BF),
        wide,
        deep,
    )
    grad_attn, grad_gate_up, grad_down = (
        grads.astype(F32) for grads in (grad_attn, grad_gate_up, grad_down)
    )
    gain_grads = jnp.sum(grad_attn[:, :, qkv_cols : qkv_cols + 2], axis=0).T
    d_inputs = norm_backward(own_tokens.astype(F32), scales[0][:rows], gain_attn, d_normed) + d_middle
    return (
        result.astype(BF)[None],
        d_inputs.astype(BF)[None],
        columns_of(grad_attn[:, :, :q_cols]),
        columns_of(grad_attn[:, :, q_cols : q_cols + HD]),
        columns_of(grad_attn[:, :, q_cols + HD : qkv_cols]),
        columns_of(grad_attn[:, :, qkv_cols + 128 :]).T,
        columns_of(grad_gate_up[:, :, :hidden_cols]),
        columns_of(grad_gate_up[:, :, hidden_cols:]),
        columns_of(grad_down).T,
        gain_grads[0],
        gain_grads[1],
    )


def solution(mesh):
    token_spec = P("fsdp", "seq", None)
    row_spec = P(AXES, None)
    column_spec = P(None, AXES)
    gain_spec = P(AXES)
    return jax.shard_map(
        shards,
        mesh=mesh,
        in_specs=(
            token_spec,
            P("fsdp", None),
            row_spec,
            row_spec,
            row_spec,
            column_spec,
            row_spec,
            row_spec,
            column_spec,
            gain_spec,
            gain_spec,
            token_spec,
        ),
        out_specs=(
            token_spec,
            token_spec,
            row_spec,
            row_spec,
            row_spec,
            column_spec,
            row_spec,
            row_spec,
            column_spec,
            gain_spec,
            gain_spec,
        ),
        check_vma=False,
    )
```
